32 devices in a mesh: gx: 8 (over z, core), gy: 4 (over y, x).
Axes of the slice: x: 2, y: 2, z: 4, core: 2. Of those that a mesh axis runs over, the one named last changes fastest.
Arguments:
- density: float32 [128, 32, 128], P('gx', 'gy'), may hold values from 0.05 to 0.95
- displacement: float32 [3, 128, 32, 128], P(None, 'gx', 'gy'), may hold values from -2 to 2
- passive: int32 [128, 32, 128], P('gx', 'gy'), may hold values from 0 to 2
Outputs:
- new_density: float32 [128, 32, 128], P('gx', 'gy')
- sensitivity: float32 [128, 32, 128], P('gx', 'gy')
The draws below stay inside these ranges and needn't reach their ends.
All inputs are finite; a program needn't handle non-finite values.
Results may differ from the reference program's by a relative error of at most 0.0003.
Values sent between devices are 32-bit elements; how exact they have to be, the bound alone decides.
A program may use at most 64 MiB of HBM per device.

```python
import math
import jax
import jax.numpy as jnp
import numpy as np
from jax import lax

CZ = 128
BISECT = 8
NX = 128
NY = 32


def draw_density(key, part):
    across = jnp.arange(NX, dtype=jnp.float32) / max(NX - 1, 1)
    along = jnp.arange(NY, dtype=jnp.float32) / max(NY - 1, 1)
    profile = (0.3 + 0.7 * across)[:, None, None] * (0.3 + 0.7 * along)[None, :, None]
    jitter = jax.random.uniform(key, (NX, NY, CZ), jnp.float32, 0.6, 1.0)
    return 0.05 + 0.9 * profile * jitter


def draw_passive(key, part):
    rolled = jax.random.randint(key, (NX, NY, CZ), 0, 16)
    return jnp.where(rolled == 0, 1, jnp.where(rolled == 1, 2, 0)).astype(jnp.int32)


def steps_of(stream_key, dims, cuts, smallest, high):
    gain = 1.0
    for axis_at, blocks in cuts:
        steps = jax.random.uniform(jax.random.fold_in(jax.random.fold_in(stream_key, 6), axis_at), (blocks,), jnp.float32, smallest / len(cuts), high / len(cuts))
        gain = gain * jnp.repeat(jnp.exp(steps), dims[axis_at] // blocks).reshape((-1,) + (1,) * (len(dims) - 1 - axis_at))
    return gain


def normal_values(rng, dims, scale, reach, shards=(), kind=jnp.bfloat16):
    entries = scale * jax.random.normal(rng, dims, jnp.float32)
    if shards:
        entries = entries * steps_of(rng, dims, shards, -0.22, 0.18)
    return jnp.clip(entries, -reach, reach).astype(kind)


def setup_inputs(seed: int = 0) -> dict:
    streams_of = jax.random.split(jax.random.key(seed), 4)
    return {
        "density": draw_density(jax.random.fold_in(streams_of[3], 71), 0),
        "displacement": normal_values(streams_of[1], (3, NX, NY, CZ), 0.3, 2.0, ((1, 8), (2, 4)), jnp.float32),
        "passive": draw_passive(jax.random.fold_in(streams_of[3], 71), 0),
    }


BRACKET = 8.0
MOVE_LIMIT = 0.2
VOLUME_SHARE = 0.35
DERIVATIVE = 3.0 * (1.0 - 1e-09)
EDGE_WEIGHT = 1.5 - math.sqrt(2.0)

def element_stiffness():
    poisson = 0.3
    lame_first = poisson / ((1.0 + poisson) * (1.0 - 2.0 * poisson))
    shear_modulus = 0.5 / (1.0 + poisson)
    elastic = np.zeros((6, 6))
    elastic[:3, :3] = lame_first
    for entry in range(3):
        elastic[entry, entry] = lame_first + 2.0 * shear_modulus
        elastic[entry + 3, entry + 3] = shear_modulus
    points = [0.5 - 0.5 / math.sqrt(3.0), 0.5 + 0.5 / math.sqrt(3.0)]
    stiffness = np.zeros((24, 24))
    for point_x in points:
        for point_y in points:
            for point_z in points:
                strain = np.zeros((6, 24))
                for a in (0, 1):
                    for b in (0, 1):
                        for c in (0, 1):
                            corner = 4 * a + 2 * b + c
                            value_x = point_x if a else 1.0 - point_x
                            value_y = point_y if b else 1.0 - point_y
                            value_z = point_z if c else 1.0 - point_z
                            slope_x = (1.0 if a else -1.0) * value_y * value_z
                            slope_y = value_x * (1.0 if b else -1.0) * value_z
                            slope_z = value_x * value_y * (1.0 if c else -1.0)
                            strain[0, 3 * corner] = slope_x
                            strain[1, 3 * corner + 1] = slope_y
                            strain[2, 3 * corner + 2] = slope_z
                            strain[3, 3 * corner] = slope_y
                            strain[3, 3 * corner + 1] = slope_x
                            strain[4, 3 * corner + 1] = slope_z
                            strain[4, 3 * corner + 2] = slope_y
                            strain[5, 3 * corner] = slope_z
                            strain[5, 3 * corner + 2] = slope_x
                stiffness = stiffness + 0.125 * strain.T @ elastic @ strain
    return stiffness.astype(np.float32)

def weight_sums(index_x, index_y, index_z, count_x, count_y, count_z):
    along_x = (index_x > 0).astype(jnp.float32) + (index_x < count_x - 1).astype(jnp.float32)
    along_y = (index_y > 0).astype(jnp.float32) + (index_y < count_y - 1).astype(jnp.float32)
    along_z = (index_z > 0).astype(jnp.float32) + (index_z < count_z - 1).astype(jnp.float32)
    return 1.5 + 0.5 * (along_x + along_y + along_z) + EDGE_WEIGHT * (along_x * along_y + along_x * along_z + along_y * along_z)

def apply_filter(field):
    extent_x, extent_y, extent_z = field.shape
    padded = jnp.pad(field, 1)
    summed = jnp.zeros_like(field)
    for shift_x in (-1, 0, 1):
        for shift_y in (-1, 0, 1):
            for shift_z in (-1, 0, 1):
                squared = shift_x * shift_x + shift_y * shift_y + shift_z * shift_z
                if squared <= 2:
                    factor = 1.5 - math.sqrt(squared)
                    summed = summed + factor * padded[1 + shift_x:1 + shift_x + extent_x, 1 + shift_y:1 + shift_y + extent_y, 1 + shift_z:1 + shift_z + extent_z]
    return summed

def element_energy(displacement):
    stiffness = jnp.asarray(element_stiffness())
    extent_x, extent_y, extent_z = displacement.shape[1:]
    node_field = jnp.pad(displacement, ((0, 0), (0, 1), (0, 1), (0, 1)))

    def slab_energy(first):
        section = lax.dynamic_slice_in_dim(node_field, first, 9, 1)
        corners = [section[:, a:a + 8, b:b + extent_y, c:c + extent_z] for a in (0, 1) for b in (0, 1) for c in (0, 1)]
        stacked = jnp.stack(corners, 0).reshape(24, 8 * extent_y * extent_z)
        mapped = jnp.dot(stiffness, stacked, precision=lax.Precision.HIGHEST)
        return lax.optimization_barrier(jnp.sum(stacked * mapped, axis=0)).reshape(8, extent_y, extent_z)
    starts = jnp.arange(extent_x // 8, dtype=jnp.int32) * 8
    return lax.map(slab_energy, starts).reshape(extent_x, extent_y, extent_z)

def reference(density, displacement, passive):
    extent_x, extent_y, extent_z = density.shape
    index_x = jnp.arange(extent_x, dtype=jnp.int32)[:, None, None]
    index_y = jnp.arange(extent_y, dtype=jnp.int32)[None, :, None]
    index_z = jnp.arange(extent_z, dtype=jnp.int32)[None, None, :]
    sums = weight_sums(index_x, index_y, index_z, extent_x, extent_y, extent_z)
    physical = apply_filter(density) / sums
    physical = jnp.where(passive == 1, 1.0, jnp.where(passive == 2, 0.0, physical))
    energy = element_energy(displacement)
    raw_field = -DERIVATIVE * physical * physical * energy
    sensitivity = apply_filter(raw_field / sums)
    volume_weight = apply_filter(1.0 / sums)
    scaled = density * jnp.sqrt(-sensitivity / volume_weight)
    lower = jnp.where(passive == 0, jnp.maximum(density - MOVE_LIMIT, 0.0), jnp.where(passive == 1, 1.0, 0.0))
    upper = jnp.where(passive == 0, jnp.minimum(density + MOVE_LIMIT, 1.0), jnp.where(passive == 1, 1.0, 0.0))
    target = VOLUME_SHARE * extent_x * extent_y * extent_z
    lower_end = jnp.asarray(-BRACKET, jnp.float32)
    upper_end = jnp.asarray(BRACKET, jnp.float32)
    for bisection_step in range(BISECT):
        middle = 0.5 * (lower_end + upper_end)
        volume = jnp.sum(jnp.minimum(jnp.maximum(scaled * jnp.exp(-0.5 * middle), lower), upper))
        exceeds = volume > target
        lower_end = jnp.where(exceeds, middle, lower_end)
        upper_end = jnp.where(exceeds, upper_end, middle)
    middle = 0.5 * (lower_end + upper_end)
    new_density = jnp.minimum(jnp.maximum(scaled * jnp.exp(-0.5 * middle), lower), upper)
    return (new_density, sensitivity)
```

```python
import functools
import math

import jax
import jax.numpy as jnp
from jax import lax
from jax.experimental import pallas as pl
from jax.experimental.pallas import tpu as pltpu
from jax.sharding import PartitionSpec as P

BISECT = 8
BRACKET = 8.0
MOVE_LIMIT = 0.2
VOLUME_SHARE = 0.35
DERIVATIVE = 3.0 * (1.0 - 1e-09)
EDGE_WEIGHT = 1.5 - math.sqrt(2.0)
POISSON = 0.3
LAME_FIRST = POISSON / ((1.0 + POISSON) * (1.0 - 2.0 * POISSON))
SHEAR = 0.5 / (1.0 + POISSON)
ROWS = 8
MESH = pl.DeviceIdType.MESH
WAYS = [(1, 0), (-1, 0), (0, 1), (0, -1), (1, 1), (-1, 1), (1, -1), (-1, -1)]


def z_neighbours(value, lane):
    planes = value.shape[-1]
    axis = value.ndim - 1
    above = jnp.where(lane == planes - 1, 0.0, pltpu.roll(value, planes - 1, axis))
    below = jnp.where(lane == 0, 0.0, pltpu.roll(value, 1, axis))
    return above + below


def parts_of_filter(value, lane):
    beside = z_neighbours(value, lane)
    return (
        1.5 * value + 0.5 * beside,
        0.5 * value + EDGE_WEIGHT * beside,
        EDGE_WEIGHT * value,
    )


def filter_rows(packed, lane, cols_x):
    _, near, far = parts_of_filter(packed, lane)
    count = packed.shape[0]
    return (near + pltpu.roll(far, 1, 0) + pltpu.roll(far, count - 1, 0))[:cols_x]


def filter_chunk(field, first, size, row_low, row_high, row, lane):
    planes = field.shape[-1]
    value = field[pl.ds(first * ROWS, (size + 2) * ROWS), :].reshape(size + 2, ROWS, planes)
    own, near, far = parts_of_filter(value, lane)
    side = near[1:-1] + far[:-2] + far[2:]
    above = row_high[pl.ds(first * ROWS, size * ROWS), :].reshape(size, ROWS, planes)
    below = row_low[pl.ds(first * ROWS, size * ROWS), :].reshape(size, ROWS, planes)
    above = jnp.where(row == ROWS - 1, above, pltpu.roll(side, ROWS - 1, 1))
    below = jnp.where(row == 0, below, pltpu.roll(side, 1, 1))
    return own[1:-1] + near[:-2] + near[2:] + (above + below)


def corner_modes(value, row_high, row, lane):
    planes = value.shape[-1]
    above = jnp.where(row == ROWS - 1, row_high, pltpu.roll(value, ROWS - 1, 1))
    total, step = value + above, above - value

    def next_z(field):
        return jnp.where(lane == planes - 1, 0.0, pltpu.roll(field, planes - 1, 2))

    total_next, step_next = next_z(total), next_z(step)
    both = total + total_next
    along_z = total_next - total
    along_y = step + step_next
    along_yz = step_next - step
    return (
        both[1:] - both[:-1],
        along_y[1:] + along_y[:-1],
        along_z[1:] + along_z[:-1],
        along_y[1:] - along_y[:-1],
        along_z[1:] - along_z[:-1],
        along_yz[1:] + along_yz[:-1],
        along_yz[1:] - along_yz[:-1],
    )


def element_energy(modes):
    (ax, ay, az, axy, axz, ayz, axyz), (bx, by, bz, bxy, bxz, byz, bxyz), (
        cx,
        cy,
        cz,
        cxy,
        cxz,
        cyz,
        cxyz,
    ) = modes

    def sq(value):
        return value * value

    first = (
        (LAME_FIRST / 16.0) * sq(ax + by + cz)
        + (2.0 * SHEAR / 16.0) * (sq(ax) + sq(by) + sq(cz))
        + (SHEAR / 16.0) * (sq(ay + bx) + sq(az + cx) + sq(bz + cy))
    )
    second = (
        (LAME_FIRST / 48.0) * (sq(axy + cyz) + sq(bxy + cxz) + sq(axz + byz))
        + (3.0 * SHEAR / 48.0) * (sq(axy) + sq(axz) + sq(bxy) + sq(byz) + sq(cxz) + sq(cyz))
        + (SHEAR / 48.0) * (sq(ayz + bxz) + sq(ayz + cxy) + sq(bxz + cxy))
    )
    third = ((LAME_FIRST + 4.0 * SHEAR) / 144.0) * (sq(axyz) + sq(bxyz) + sq(cxyz))
    return first + second + third


def peers(count, body):
    if count <= 64:
        for step in range(1, count):
            body(step)
    else:
        lax.fori_loop(1, count, lambda step, carry: (body(step), carry)[1], 0)


def kernel(
    count_x,
    count_y,
    dens_hbm,
    disp_hbm,
    pas_hbm,
    new_hbm,
    sens_hbm,
    big,
    passive,
    pack_low,
    pack_high,
    row_high,
    row_low,
    spread,
    spread_pack_low,
    spread_pack_high,
    spread_row_high,
    spread_row_low,
    corner_pp,
    corner_mp,
    corner_pm,
    corner_mm,
    s_corner_pp,
    s_corner_mp,
    s_corner_pm,
    s_corner_mm,
    node_row,
    tail_high,
    tail_low,
    inverse,
    inverse_volume,
    scaled,
    lower,
    upper,
    partial,
    totals,
    new_out,
    sens_out,
    local_sems,
    send_a,
    recv_a,
    send_b,
    recv_b,
    send_c,
    recv_c,
):
    planes = dens_hbm.shape[-1]
    cols_x = dens_hbm.shape[0] // ROWS
    block = cols_x * ROWS
    last = cols_x * ROWS
    ix, iy = lax.axis_index("gx"), lax.axis_index("gy")
    devices = count_x * count_y
    total_x, total_y = cols_x * count_x, ROWS * count_y

    def peer(step):
        step_x, step_y = step // count_y, step % count_y
        return (lax.rem(ix + step_x, count_x), lax.rem(iy + step_y, count_y))

    barrier = pltpu.get_barrier_semaphore()
    peers(
        devices,
        lambda step: pl.semaphore_signal(
            barrier, inc=1, device_id=peer(step), device_id_type=MESH
        ),
    )
    loads = [
        pltpu.make_async_copy(dens_hbm, big.at[0, pl.ds(ROWS, block)], local_sems.at[0]),
        pltpu.make_async_copy(disp_hbm, big.at[pl.ds(1, 3), pl.ds(ROWS, block)], local_sems.at[1]),
        pltpu.make_async_copy(pas_hbm, passive, local_sems.at[2]),
    ]
    for load in loads:
        load.start()

    def inside(x, y):
        return (x >= 0) & (x < count_x) & (y >= 0) & (y < count_y)

    def fill(way, refs):
        @pl.when(jnp.logical_not(inside(ix - way[0], iy - way[1])))
        def _():
            for ref in refs:
                ref[...] = jnp.zeros(ref.shape, ref.dtype)

    def exchange(pairs, send, recv):
        def copy(at):
            source, target = pairs[at]
            dx, dy = WAYS[at]
            return pltpu.make_async_remote_copy(
                src_ref=source,
                dst_ref=target,
                send_sem=send.at[at],
                recv_sem=recv.at[at],
                device_id=(ix + dx, iy + dy),
                device_id_type=MESH,
            )

        def start(at):
            dx, dy = WAYS[at]

            @pl.when(inside(ix + dx, iy + dy))
            def _():
                copy(at).start()

        def arrive(at):
            dx, dy = WAYS[at]

            @pl.when(inside(ix - dx, iy - dy))
            def _():
                copy(at).wait_recv()

        def sent(at):
            dx, dy = WAYS[at]

            @pl.when(inside(ix + dx, iy + dy))
            def _():
                copy(at).wait_send()

        return start, arrive, sent

    first_tile, last_tile = pl.ds(ROWS, ROWS), pl.ds(last, ROWS)
    low_tile, high_tile = pl.ds(0, ROWS), pl.ds(last + ROWS, ROWS)
    start_a, arrive_a, sent_a = exchange(
        [
            (big.at[0, last_tile], big.at[0, low_tile]),
            (big.at[:, first_tile], big.at[:, high_tile]),
            (pack_high, row_low.at[pl.ds(0, cols_x)]),
            (pack_low, row_high.at[:, pl.ds(0, cols_x)]),
            (big.at[0, last_tile], corner_pp),
            (big.at[0, first_tile], corner_mp),
            (big.at[0, last_tile], corner_pm),
            (big.at[:, first_tile], corner_mm),
        ],
        send_a,
        recv_a,
    )
    start_b, arrive_b, sent_b = exchange(
        [
            (spread.at[last_tile], spread.at[low_tile]),
            (spread.at[first_tile], spread.at[high_tile]),
            (spread_pack_high, spread_row_low.at[pl.ds(0, cols_x)]),
            (spread_pack_low, spread_row_high.at[pl.ds(0, cols_x)]),
            (spread.at[last_tile], s_corner_pp),
            (spread.at[first_tile], s_corner_mp),
            (spread.at[last_tile], s_corner_pm),
            (spread.at[first_tile], s_corner_mm),
        ],
        send_b,
        recv_b,
    )
    fill(WAYS[0], [big.at[0, low_tile], spread.at[low_tile]])
    fill(WAYS[1], [big.at[:, high_tile], spread.at[high_tile]])
    fill(WAYS[2], [row_low.at[pl.ds(0, cols_x)], spread_row_low.at[pl.ds(0, cols_x)]])
    fill(WAYS[3], [row_high.at[:, pl.ds(0, cols_x)], spread_row_high.at[pl.ds(0, cols_x)]])
    fill(WAYS[4], [corner_pp, s_corner_pp])
    fill(WAYS[5], [corner_mp, s_corner_mp])
    fill(WAYS[6], [corner_pm, s_corner_pm])
    fill(WAYS[7], [corner_mm, s_corner_mm])

    def strided(start):
        return pl.ds(start, cols_x, stride=ROWS)

    loads[0].wait()
    pack_high[...] = big[0, strided(ROWS + ROWS - 1), :]
    pack_low[0] = big[0, strided(ROWS), :]
    loads[1].wait()
    for c in (1, 2, 3):
        pack_low[c] = big[c, strided(ROWS), :]
    pl.semaphore_wait(barrier, devices - 1)
    for at in (3, 1, 2, 7, 0, 4, 5, 6):
        start_a(at)

    lane = lax.broadcasted_iota(jnp.int32, (ROWS, planes), 1)
    row = lax.broadcasted_iota(jnp.int32, (ROWS, planes), 0)

    def counted(at, total):
        one, none = jnp.float32(1.0), jnp.float32(0.0)
        return jnp.where(at > 0, one, none) + jnp.where(at < total - 1, one, none)

    along_z = counted(lane, planes)
    known = {}

    def representative(x):
        return x if x in (-1, 0, cols_x - 1, cols_x) else 1

    def inverse_sums(x, offset):
        x = representative(x)
        if (x, offset) not in known:
            y = iy * ROWS + row + offset
            along_y = counted(y, total_y)
            global_x = ix * cols_x + x
            along_x = counted(global_x, total_x)
            sums = (
                1.5
                + 0.5 * (along_x + along_y + along_z)
                + EDGE_WEIGHT * (along_x * along_y + along_x * along_z + along_y * along_z)
            )
            result = 1.0 / sums
            result = jnp.where((y >= 0) & (y < total_y), result, 0.0)
            if x in (-1, cols_x):
                held = (global_x >= 0) & (global_x < total_x)
                result = result * jnp.where(held, jnp.float32(1.0), jnp.float32(0.0))
            known[x, offset] = (result, parts_of_filter(result, lane))
        return known[x, offset]

    weights = {}
    for x in range(cols_x):
        tile = pl.ds(x * ROWS, ROWS)
        inverse[tile, :] = inverse_sums(x, 0)[0]
        key = tuple(representative(x + d) for d in (-1, 0, 1))
        if key not in weights:
            volume = inverse_sums(x, 0)[1][0]
            volume = volume + inverse_sums(x - 1, 0)[1][1] + inverse_sums(x + 1, 0)[1][1]
            for offset in (-1, 1):
                volume = volume + inverse_sums(x, offset)[1][1]
                volume = volume + inverse_sums(x - 1, offset)[1][2]
                volume = volume + inverse_sums(x + 1, offset)[1][2]
            weights[key] = 1.0 / volume
        inverse_volume[tile, :] = weights[key]

    loads[2].wait()
    for at in range(8):
        arrive_a(at)

    def join(rows, first, final):
        rows[pl.ds(cols_x, ROWS), :] = jnp.where(row == 0, first, jnp.where(row == 7, final, 0.0))

    def tails(rows_high, rows_low, pp, mp, pm, mm):
        join(rows_high, mm[0:1, :], pm[0:1, :])
        join(rows_low, mp[7:8, :], pp[7:8, :])
        lane_rows = lax.broadcasted_iota(jnp.int32, (cols_x + ROWS, planes), 1)
        tail_high[strided(ROWS - 1), :] = filter_rows(rows_high[...], lane_rows, cols_x)
        tail_low[strided(0), :] = filter_rows(rows_low[...], lane_rows, cols_x)

    tails(row_high.at[0], row_low, corner_pp, corner_mp, corner_pm, corner_mm.at[0])
    for c in range(3):
        node_row[c, strided(ROWS - 1), :] = row_high[1 + c, pl.ds(0, cols_x), :]
        node_row[c, pl.ds(block + ROWS - 1, 1), :] = corner_mm[1 + c, 0:1, :]

    density = big.at[0]

    def masks(size):
        shape = (size, ROWS, planes)
        return (
            lax.broadcasted_iota(jnp.int32, shape, 1),
            lax.broadcasted_iota(jnp.int32, shape, 2),
        )

    size = 4 if cols_x % 4 == 0 else 1
    rows_here = size * ROWS
    row_s, lane_s = masks(size)
    row_1, lane_1 = masks(size + 1)
    _, lane_2 = masks(size + 2)

    def tiles(ref, first):
        return ref[pl.ds(first * ROWS, rows_here), :].reshape(size, ROWS, planes)

    for first in range(0, cols_x, size):
        near = pl.ds((first + 1) * ROWS, (size + 1) * ROWS)
        high = pl.ds(first * ROWS, (size + 1) * ROWS)
        shape = (size + 1, ROWS, planes)
        modes = [
            corner_modes(
                big[1 + c, near, :].reshape(shape),
                node_row[c, high, :].reshape(shape),
                row_1,
                lane_1,
            )
            for c in range(3)
        ]
        energy = element_energy(modes)
        inv = tiles(inverse, first)
        kind = tiles(passive, first)
        physical = filter_chunk(density, first, size, tail_low, tail_high, row_s, lane_2) * inv
        physical = jnp.where(kind == 1, 1.0, jnp.where(kind == 2, 0.0, physical))
        raw = (-DERIVATIVE) * physical * physical * energy
        spread[pl.ds((first + 1) * ROWS, rows_here), :] = (raw * inv).reshape(rows_here, planes)

    spread_pack_high[...] = spread[strided(ROWS + ROWS - 1), :]
    spread_pack_low[...] = spread[strided(ROWS), :]
    for at in (3, 2, 1, 0, 7, 4, 5, 6):
        start_b(at)

    for first in range(0, cols_x, size):
        at = pl.ds(first * ROWS, rows_here)
        kind = tiles(passive, first)
        held = big[0, pl.ds((first + 1) * ROWS, rows_here), :].reshape(size, ROWS, planes)
        fixed = jnp.where(kind == 1, 1.0, 0.0)
        low = jnp.where(kind == 0, jnp.maximum(held - MOVE_LIMIT, 0.0), fixed)
        high = jnp.where(kind == 0, jnp.minimum(held + MOVE_LIMIT, 1.0), fixed)
        lower[at, :] = low.reshape(rows_here, planes)
        upper[at, :] = high.reshape(rows_here, planes)

    for at in range(8):
        arrive_b(at)
    tails(spread_row_high, spread_row_low, s_corner_pp, s_corner_mp, s_corner_pm, s_corner_mm)
    for first in range(0, cols_x, size):
        at = pl.ds(first * ROWS, rows_here)
        sens = filter_chunk(spread, first, size, tail_low, tail_high, row_s, lane_2)
        held = big[0, pl.ds((first + 1) * ROWS, rows_here), :].reshape(size, ROWS, planes)
        rate = held * jnp.sqrt(-sens * tiles(inverse_volume, first))
        sens_out[at, :] = sens.reshape(rows_here, planes)
        scaled[at, :] = rate.reshape(rows_here, planes)
    write_sens = pltpu.make_async_copy(sens_out, sens_hbm, local_sems.at[3])
    write_sens.start()

    slots = 2**BISECT
    group = 16
    spacing = 2.0 * BRACKET / slots
    scales = jnp.concatenate(
        [jnp.full((1, ROWS, planes), math.exp(-0.5 * spacing * j), jnp.float32) for j in range(group)]
    )

    def volumes(i, carry):
        begin = (-BRACKET) + (spacing * group) * i.astype(jnp.float32)
        factors = scales * jnp.exp(jnp.full((ROWS, planes), -0.5 * begin, jnp.float32))[None]
        total = jnp.zeros((group, ROWS, planes), jnp.float32)
        for x in range(cols_x):
            tile = pl.ds(x * ROWS, ROWS)
            moved = jnp.maximum(scaled[tile, :][None] * factors, lower[tile, :][None])
            total = total + jnp.minimum(moved, upper[tile, :][None])
        at = pl.multiple_of(i * (group * ROWS), group * ROWS)
        partial[pl.ds(at, group * ROWS), :] = total.reshape(group * ROWS, planes)
        return carry

    lax.fori_loop(0, slots // group, volumes, 0)
    me = ix * count_y + iy
    halves = slots // planes
    for half in range(halves):
        start = half * planes * ROWS
        lines = partial[pl.ds(start, planes, stride=ROWS), :]
        for s in range(1, ROWS):
            lines = lines + partial[pl.ds(start + s, planes, stride=ROWS), :]
        totals[me, half : half + 1, :] = jnp.sum(lines.T, axis=0, keepdims=True)

    def share(step):
        return pltpu.make_async_remote_copy(
            src_ref=totals.at[me],
            dst_ref=totals.at[me],
            send_sem=send_c,
            recv_sem=recv_c,
            device_id=peer(step),
            device_id_type=MESH,
        )

    peers(devices, lambda step: share(step).start())
    others = totals.at[pl.ds(0, devices - 1)]
    pltpu.make_async_copy(others, others, recv_c).wait()

    volume = jnp.sum(totals[...], axis=0)
    label = lax.broadcasted_iota(jnp.int32, volume.shape, 0) * planes + lax.broadcasted_iota(
        jnp.int32, volume.shape, 1
    )
    target = VOLUME_SHARE * total_x * total_y * planes
    over = jnp.where((label > 0) & (volume > target), 1.0, 0.0)
    reached = jnp.sum(jnp.sum(over, axis=0, keepdims=True), axis=1, keepdims=True)
    middle = (-BRACKET) + spacing * (jnp.broadcast_to(reached, (ROWS, planes)) + 0.5)
    factor = jnp.exp(-0.5 * middle)[None]
    for first in range(0, cols_x, size):
        at = pl.ds(first * ROWS, rows_here)
        moved = jnp.maximum(tiles(scaled, first) * factor, tiles(lower, first))
        new_out[at, :] = jnp.minimum(moved, tiles(upper, first)).reshape(rows_here, planes)
    write_new = pltpu.make_async_copy(new_out, new_hbm, local_sems.at[4])
    write_new.start()
    for at in range(8):
        sent_a(at)
        sent_b(at)
    pltpu.make_async_copy(others, others, send_c).wait()
    write_sens.wait()
    write_new.wait()


def per_device(count_x, count_y, density, displacement, passive):
    cols_x, cols_y, planes = density.shape
    assert cols_y == ROWS and cols_x % ROWS == 0 and planes == 128
    block = cols_x * ROWS
    devices = count_x * count_y
    slots = 2**BISECT

    def buffer(*shape):
        return pltpu.VMEM(shape, jnp.float32)

    field = buffer(block, planes)
    tile = buffer(ROWS, planes)
    wide = buffer(block + 2 * ROWS, planes)
    rows = buffer(cols_x, planes)
    ring = buffer(cols_x + ROWS, planes)
    out = jax.ShapeDtypeStruct((block, planes), jnp.float32)
    new_density, sensitivity = pl.pallas_call(
        functools.partial(kernel, count_x, count_y),
        out_shape=(out, out),
        in_specs=[pl.BlockSpec(memory_space=pl.ANY)] * 3,
        out_specs=[pl.BlockSpec(memory_space=pl.ANY)] * 2,
        scratch_shapes=[
            buffer(4, block + 2 * ROWS, planes),
            pltpu.VMEM((block, planes), jnp.int32),
            buffer(4, cols_x, planes),
            rows,
            buffer(4, cols_x + ROWS, planes),
            ring,
            wide,
            rows,
            rows,
            ring,
            ring,
            tile,
            tile,
            tile,
            buffer(4, ROWS, planes),
            tile,
            tile,
            tile,
            tile,
            buffer(3, block + ROWS, planes),
            field,
            field,
            field,
            field,
            field,
            field,
            field,
            buffer(slots * ROWS, planes),
            buffer(devices, slots // planes, planes),
            field,
            field,
            pltpu.SemaphoreType.DMA((5,)),
            pltpu.SemaphoreType.DMA((8,)),
            pltpu.SemaphoreType.DMA((8,)),
            pltpu.SemaphoreType.DMA((8,)),
            pltpu.SemaphoreType.DMA((8,)),
            pltpu.SemaphoreType.DMA,
            pltpu.SemaphoreType.DMA,
        ],
        compiler_params=pltpu.CompilerParams(
            collective_id=0, has_side_effects=True, vmem_limit_bytes=16 * 1024 * 1024
        ),
    )(
        density.reshape(block, planes),
        displacement.reshape(3, block, planes),
        passive.reshape(block, planes),
    )
    return (new_density.reshape(density.shape), sensitivity.reshape(density.shape))


def solution(mesh):
    return jax.shard_map(
        functools.partial(per_device, mesh.shape["gx"], mesh.shape["gy"]),
        mesh=mesh,
        in_specs=(P("gx", "gy", None), P(None, "gx", "gy", None), P("gx", "gy", None)),
        out_specs=(P("gx", "gy", None), P("gx", "gy", None)),
        check_vma=False,
    )
```

```python
import functools
import math

import jax
import jax.numpy as jnp
from jax import lax
from jax.experimental import pallas as pl
from jax.experimental.pallas import tpu as pltpu
from jax.sharding import PartitionSpec as P

BISECT = 8
BRACKET = 8.0
MOVE_LIMIT = 0.2
VOLUME_SHARE = 0.35
DERIVATIVE = 3.0 * (1.0 - 1e-09)
EDGE_WEIGHT = 1.5 - math.sqrt(2.0)
POISSON = 0.3
LAME_FIRST = POISSON / ((1.0 + POISSON) * (1.0 - 2.0 * POISSON))
SHEAR = 0.5 / (1.0 + POISSON)
ROWS = 8
MESH = pl.DeviceIdType.MESH
WAYS = [(1, 0), (-1, 0), (0, 1), (0, -1), (1, 1), (-1, 1), (1, -1), (-1, -1)]


def z_neighbours(value, lane):
    planes = value.shape[-1]
    axis = value.ndim - 1
    above = jnp.where(lane == planes - 1, 0.0, pltpu.roll(value, planes - 1, axis))
    below = jnp.where(lane == 0, 0.0, pltpu.roll(value, 1, axis))
    return above + below


def parts_of_filter(value, lane):
    beside = z_neighbours(value, lane)
    return (
        1.5 * value + 0.5 * beside,
        0.5 * value + EDGE_WEIGHT * beside,
        EDGE_WEIGHT * value,
    )


def filter_rows(packed, lane, cols_x):
    _, near, far = parts_of_filter(packed, lane)
    count = packed.shape[0]
    return (near + pltpu.roll(far, 1, 0) + pltpu.roll(far, count - 1, 0))[:cols_x]


def filter_chunk(field, first, size, row_low, row_high, row, lane):
    planes = field.shape[-1]
    value = field[pl.ds(first * ROWS, (size + 2) * ROWS), :].reshape(size + 2, ROWS, planes)
    own, near, far = parts_of_filter(value, lane)
    side = near[1:-1] + far[:-2] + far[2:]
    above = row_high[pl.ds(first * ROWS, size * ROWS), :].reshape(size, ROWS, planes)
    below = row_low[pl.ds(first * ROWS, size * ROWS), :].reshape(size, ROWS, planes)
    above = jnp.where(row == ROWS - 1, above, pltpu.roll(side, ROWS - 1, 1))
    below = jnp.where(row == 0, below, pltpu.roll(side, 1, 1))
    return own[1:-1] + near[:-2] + near[2:] + (above + below)


def corner_modes(value, row_high, row, lane):
    planes = value.shape[-1]
    above = jnp.where(row == ROWS - 1, row_high, pltpu.roll(value, ROWS - 1, 1))
    total, step = value + above, above - value

    def next_z(field):
        return jnp.where(lane == planes - 1, 0.0, pltpu.roll(field, planes - 1, 2))

    total_next, step_next = next_z(total), next_z(step)
    both = total + total_next
    along_z = total_next - total
    along_y = step + step_next
    along_yz = step_next - step
    return (
        both[1:] - both[:-1],
        along_y[1:] + along_y[:-1],
        along_z[1:] + along_z[:-1],
        along_y[1:] - along_y[:-1],
        along_z[1:] - along_z[:-1],
        along_yz[1:] + along_yz[:-1],
        along_yz[1:] - along_yz[:-1],
    )


def element_energy(modes):
    (ax, ay, az, axy, axz, ayz, axyz), (bx, by, bz, bxy, bxz, byz, bxyz), (
        cx,
        cy,
        cz,
        cxy,
        cxz,
        cyz,
        cxyz,
    ) = modes

    def sq(value):
        return value * value

    first = (
        (LAME_FIRST / 16.0) * sq(ax + by + cz)
        + (2.0 * SHEAR / 16.0) * (sq(ax) + sq(by) + sq(cz))
        + (SHEAR / 16.0) * (sq(ay + bx) + sq(az + cx) + sq(bz + cy))
    )
    second = (
        (LAME_FIRST / 48.0) * (sq(axy + cyz) + sq(bxy + cxz) + sq(axz + byz))
        + (3.0 * SHEAR / 48.0) * (sq(axy) + sq(axz) + sq(bxy) + sq(byz) + sq(cxz) + sq(cyz))
        + (SHEAR / 48.0) * (sq(ayz + bxz) + sq(ayz + cxy) + sq(bxz + cxy))
    )
    third = ((LAME_FIRST + 4.0 * SHEAR) / 144.0) * (sq(axyz) + sq(bxyz) + sq(cxyz))
    return first + second + third


def kernel(
    count_x,
    count_y,
    dens_hbm,
    disp_hbm,
    pas_hbm,
    new_hbm,
    sens_hbm,
    big,
    passive,
    pack_low,
    pack_high,
    row_high,
    row_low,
    spread,
    spread_pack_low,
    spread_pack_high,
    spread_row_high,
    spread_row_low,
    corner_pp,
    corner_mp,
    corner_pm,
    corner_mm,
    s_corner_pp,
    s_corner_mp,
    s_corner_pm,
    s_corner_mm,
    node_row,
    tail_high,
    tail_low,
    inverse,
    inverse_volume,
    scaled,
    lower,
    upper,
    partial,
    totals_x,
    totals_y,
    new_out,
    sens_out,
    local_sems,
    send_a,
    recv_a,
    send_b,
    recv_b,
    send_c,
    recv_c,
    send_d,
    recv_d,
):
    planes = dens_hbm.shape[-1]
    cols_x = dens_hbm.shape[0] // ROWS
    block = cols_x * ROWS
    last = cols_x * ROWS
    ix, iy = lax.axis_index("gx"), lax.axis_index("gy")
    total_x, total_y = cols_x * count_x, ROWS * count_y

    def inside(x, y):
        return (x >= 0) & (x < count_x) & (y >= 0) & (y < count_y)

    def along_x(step):
        return (lax.rem(ix + step, count_x), iy)

    def along_y(step):
        return (ix, lax.rem(iy + step, count_y))

    barrier = pltpu.get_barrier_semaphore()

    def greet(device):
        pl.semaphore_signal(barrier, inc=1, device_id=device, device_id_type=MESH)

    for step in range(1, count_x):
        greet(along_x(step))
    for step in range(1, count_y):
        greet(along_y(step))
    greetings = count_x - 1 + count_y - 1
    for dx, dy in WAYS[4:]:
        present = inside(ix + dx, iy + dy)
        greetings = greetings + jnp.where(present, 1, 0)

        @pl.when(present)
        def _(dx=dx, dy=dy):
            greet((ix + dx, iy + dy))

    loads = [
        pltpu.make_async_copy(dens_hbm, big.at[0, pl.ds(ROWS, block)], local_sems.at[0]),
        pltpu.make_async_copy(disp_hbm, big.at[pl.ds(1, 3), pl.ds(ROWS, block)], local_sems.at[1]),
        pltpu.make_async_copy(pas_hbm, passive, local_sems.at[2]),
    ]
    for load in loads:
        load.start()

    def fill(way, refs):
        @pl.when(jnp.logical_not(inside(ix - way[0], iy - way[1])))
        def _():
            for ref in refs:
                ref[...] = jnp.zeros(ref.shape, ref.dtype)

    def exchange(pairs, send, recv):
        def copy(at):
            source, target = pairs[at]
            dx, dy = WAYS[at]
            return pltpu.make_async_remote_copy(
                src_ref=source,
                dst_ref=target,
                send_sem=send.at[at],
                recv_sem=recv.at[at],
                device_id=(ix + dx, iy + dy),
                device_id_type=MESH,
            )

        def start(at):
            dx, dy = WAYS[at]

            @pl.when(inside(ix + dx, iy + dy))
            def _():
                copy(at).start()

        def arrive(at):
            dx, dy = WAYS[at]

            @pl.when(inside(ix - dx, iy - dy))
            def _():
                copy(at).wait_recv()

        def sent(at):
            dx, dy = WAYS[at]

            @pl.when(inside(ix + dx, iy + dy))
            def _():
                copy(at).wait_send()

        return start, arrive, sent

    first_tile, last_tile = pl.ds(ROWS, ROWS), pl.ds(last, ROWS)
    low_tile, high_tile = pl.ds(0, ROWS), pl.ds(last + ROWS, ROWS)
    start_a, arrive_a, sent_a = exchange(
        [
            (big.at[0, last_tile], big.at[0, low_tile]),
            (big.at[:, first_tile], big.at[:, high_tile]),
            (pack_high, row_low.at[pl.ds(0, cols_x)]),
            (pack_low, row_high.at[:, pl.ds(0, cols_x)]),
            (big.at[0, last_tile], corner_pp),
            (big.at[0, first_tile], corner_mp),
            (big.at[0, last_tile], corner_pm),
            (big.at[:, first_tile], corner_mm),
        ],
        send_a,
        recv_a,
    )
    start_b, arrive_b, sent_b = exchange(
        [
            (spread.at[last_tile], spread.at[low_tile]),
            (spread.at[first_tile], spread.at[high_tile]),
            (spread_pack_high, spread_row_low.at[pl.ds(0, cols_x)]),
            (spread_pack_low, spread_row_high.at[pl.ds(0, cols_x)]),
            (spread.at[last_tile], s_corner_pp),
            (spread.at[first_tile], s_corner_mp),
            (spread.at[last_tile], s_corner_pm),
            (spread.at[first_tile], s_corner_mm),
        ],
        send_b,
        recv_b,
    )
    fill(WAYS[0], [big.at[0, low_tile], spread.at[low_tile]])
    fill(WAYS[1], [big.at[:, high_tile], spread.at[high_tile]])
    fill(WAYS[2], [row_low.at[pl.ds(0, cols_x)], spread_row_low.at[pl.ds(0, cols_x)]])
    fill(WAYS[3], [row_high.at[:, pl.ds(0, cols_x)], spread_row_high.at[pl.ds(0, cols_x)]])
    fill(WAYS[4], [corner_pp, s_corner_pp])
    fill(WAYS[5], [corner_mp, s_corner_mp])
    fill(WAYS[6], [corner_pm, s_corner_pm])
    fill(WAYS[7], [corner_mm, s_corner_mm])

    def strided(start):
        return pl.ds(start, cols_x, stride=ROWS)

    loads[0].wait()
    pack_high[...] = big[0, strided(ROWS + ROWS - 1), :]
    pack_low[0] = big[0, strided(ROWS), :]
    loads[1].wait()
    for c in (1, 2, 3):
        pack_low[c] = big[c, strided(ROWS), :]
    pl.semaphore_wait(barrier, greetings)
    for at in (3, 1, 2, 7, 0, 4, 5, 6):
        start_a(at)

    lane = lax.broadcasted_iota(jnp.int32, (ROWS, planes), 1)
    row = lax.broadcasted_iota(jnp.int32, (ROWS, planes), 0)

    def counted(at, total):
        one, none = jnp.float32(1.0), jnp.float32(0.0)
        return jnp.where(at > 0, one, none) + jnp.where(at < total - 1, one, none)

    count_z = counted(lane, planes)
    known = {}

    def representative(x):
        return x if x in (-1, 0, cols_x - 1, cols_x) else 1

    def inverse_sums(x, offset):
        x = representative(x)
        if (x, offset) not in known:
            y = iy * ROWS + row + offset
            beside_y = counted(y, total_y)
            global_x = ix * cols_x + x
            beside_x = counted(global_x, total_x)
            sums = (
                1.5
                + 0.5 * (beside_x + beside_y + count_z)
                + EDGE_WEIGHT * (beside_x * beside_y + beside_x * count_z + beside_y * count_z)
            )
            result = 1.0 / sums
            result = jnp.where((y >= 0) & (y < total_y), result, 0.0)
            if x in (-1, cols_x):
                held = (global_x >= 0) & (global_x < total_x)
                result = result * jnp.where(held, jnp.float32(1.0), jnp.float32(0.0))
            known[x, offset] = (result, parts_of_filter(result, lane))
        return known[x, offset]

    weights = {}
    for x in range(cols_x):
        tile = pl.ds(x * ROWS, ROWS)
        inverse[tile, :] = inverse_sums(x, 0)[0]
        key = tuple(representative(x + d) for d in (-1, 0, 1))
        if key not in weights:
            volume = inverse_sums(x, 0)[1][0]
            volume = volume + inverse_sums(x - 1, 0)[1][1] + inverse_sums(x + 1, 0)[1][1]
            for offset in (-1, 1):
                volume = volume + inverse_sums(x, offset)[1][1]
                volume = volume + inverse_sums(x - 1, offset)[1][2]
                volume = volume + inverse_sums(x + 1, offset)[1][2]
            weights[key] = 1.0 / volume
        inverse_volume[tile, :] = weights[key]

    loads[2].wait()
    for at in range(8):
        arrive_a(at)

    def join(rows, first, final):
        rows[pl.ds(cols_x, ROWS), :] = jnp.where(row == 0, first, jnp.where(row == 7, final, 0.0))

    def tails(rows_high, rows_low, pp, mp, pm, mm):
        join(rows_high, mm[0:1, :], pm[0:1, :])
        join(rows_low, mp[7:8, :], pp[7:8, :])
        lane_rows = lax.broadcasted_iota(jnp.int32, (cols_x + ROWS, planes), 1)
        tail_high[strided(ROWS - 1), :] = filter_rows(rows_high[...], lane_rows, cols_x)
        tail_low[strided(0), :] = filter_rows(rows_low[...], lane_rows, cols_x)

    tails(row_high.at[0], row_low, corner_pp, corner_mp, corner_pm, corner_mm.at[0])
    for c in range(3):
        node_row[c, strided(ROWS - 1), :] = row_high[1 + c, pl.ds(0, cols_x), :]
        node_row[c, pl.ds(block + ROWS - 1, 1), :] = corner_mm[1 + c, 0:1, :]

    density = big.at[0]

    def masks(size):
        shape = (size, ROWS, planes)
        return (
            lax.broadcasted_iota(jnp.int32, shape, 1),
            lax.broadcasted_iota(jnp.int32, shape, 2),
        )

    size = 4 if cols_x % 4 == 0 else 1
    rows_here = size * ROWS
    row_s, lane_s = masks(size)
    row_1, lane_1 = masks(size + 1)
    _, lane_2 = masks(size + 2)

    def tiles(ref, first):
        return ref[pl.ds(first * ROWS, rows_here), :].reshape(size, ROWS, planes)

    for first in range(0, cols_x, size):
        near = pl.ds((first + 1) * ROWS, (size + 1) * ROWS)
        high = pl.ds(first * ROWS, (size + 1) * ROWS)
        shape = (size + 1, ROWS, planes)
        modes = [
            corner_modes(
                big[1 + c, near, :].reshape(shape),
                node_row[c, high, :].reshape(shape),
                row_1,
                lane_1,
            )
            for c in range(3)
        ]
        energy = element_energy(modes)
        inv = tiles(inverse, first)
        kind = tiles(passive, first)
        physical = filter_chunk(density, first, size, tail_low, tail_high, row_s, lane_2) * inv
        physical = jnp.where(kind == 1, 1.0, jnp.where(kind == 2, 0.0, physical))
        raw = (-DERIVATIVE) * physical * physical * energy
        spread[pl.ds((first + 1) * ROWS, rows_here), :] = (raw * inv).reshape(rows_here, planes)

    spread_pack_high[...] = spread[strided(ROWS + ROWS - 1), :]
    spread_pack_low[...] = spread[strided(ROWS), :]
    for at in (3, 2, 1, 0, 7, 4, 5, 6):
        start_b(at)

    for first in range(0, cols_x, size):
        at = pl.ds(first * ROWS, rows_here)
        kind = tiles(passive, first)
        held = big[0, pl.ds((first + 1) * ROWS, rows_here), :].reshape(size, ROWS, planes)
        fixed = jnp.where(kind == 1, 1.0, 0.0)
        low = jnp.where(kind == 0, jnp.maximum(held - MOVE_LIMIT, 0.0), fixed)
        high = jnp.where(kind == 0, jnp.minimum(held + MOVE_LIMIT, 1.0), fixed)
        lower[at, :] = low.reshape(rows_here, planes)
        upper[at, :] = high.reshape(rows_here, planes)

    for at in range(8):
        arrive_b(at)
    tails(spread_row_high, spread_row_low, s_corner_pp, s_corner_mp, s_corner_pm, s_corner_mm)
    for first in range(0, cols_x, size):
        at = pl.ds(first * ROWS, rows_here)
        sens = filter_chunk(spread, first, size, tail_low, tail_high, row_s, lane_2)
        held = big[0, pl.ds((first + 1) * ROWS, rows_here), :].reshape(size, ROWS, planes)
        rate = held * jnp.sqrt(-sens * tiles(inverse_volume, first))
        sens_out[at, :] = sens.reshape(rows_here, planes)
        scaled[at, :] = rate.reshape(rows_here, planes)
    write_sens = pltpu.make_async_copy(sens_out, sens_hbm, local_sems.at[3])
    write_sens.start()

    slots = 2**BISECT
    group = 16
    spacing = 2.0 * BRACKET / slots
    scales = jnp.concatenate(
        [jnp.full((1, ROWS, planes), math.exp(-0.5 * spacing * j), jnp.float32) for j in range(group)]
    )

    def volumes(i, carry):
        begin = (-BRACKET) + (spacing * group) * i.astype(jnp.float32)
        factors = scales * jnp.exp(jnp.full((ROWS, planes), -0.5 * begin, jnp.float32))[None]
        total = jnp.zeros((group, ROWS, planes), jnp.float32)
        for x in range(cols_x):
            tile = pl.ds(x * ROWS, ROWS)
            moved = jnp.maximum(scaled[tile, :][None] * factors, lower[tile, :][None])
            total = total + jnp.minimum(moved, upper[tile, :][None])
        at = pl.multiple_of(i * (group * ROWS), group * ROWS)
        partial[pl.ds(at, group * ROWS), :] = total.reshape(group * ROWS, planes)
        return carry

    lax.fori_loop(0, slots // group, volumes, 0)
    halves = slots // planes
    for half in range(halves):
        start = half * planes * ROWS
        lines = partial[pl.ds(start, planes, stride=ROWS), :]
        for s in range(1, ROWS):
            lines = lines + partial[pl.ds(start + s, planes, stride=ROWS), :]
        totals_x[ix, half : half + 1, :] = jnp.sum(lines.T, axis=0, keepdims=True)

    def shared(totals, me, target, count, send, recv):
        for step in range(1, count):
            pltpu.make_async_remote_copy(
                src_ref=totals.at[me],
                dst_ref=totals.at[me],
                send_sem=send,
                recv_sem=recv,
                device_id=target(step),
                device_id_type=MESH,
            ).start()
        others = totals.at[pl.ds(0, count - 1)]
        pltpu.make_async_copy(others, others, recv).wait()
        return jnp.sum(totals[...], axis=0), others

    column, sent_x = shared(totals_x, ix, along_x, count_x, send_c, recv_c)
    totals_y[iy] = column
    volume, sent_y = shared(totals_y, iy, along_y, count_y, send_d, recv_d)
    label = lax.broadcasted_iota(jnp.int32, volume.shape, 0) * planes + lax.broadcasted_iota(
        jnp.int32, volume.shape, 1
    )
    target = VOLUME_SHARE * total_x * total_y * planes
    over = jnp.where((label > 0) & (volume > target), 1.0, 0.0)
    reached = jnp.sum(jnp.sum(over, axis=0, keepdims=True), axis=1, keepdims=True)
    middle = (-BRACKET) + spacing * (jnp.broadcast_to(reached, (ROWS, planes)) + 0.5)
    factor = jnp.exp(-0.5 * middle)[None]
    for first in range(0, cols_x, size):
        at = pl.ds(first * ROWS, rows_here)
        moved = jnp.maximum(tiles(scaled, first) * factor, tiles(lower, first))
        new_out[at, :] = jnp.minimum(moved, tiles(upper, first)).reshape(rows_here, planes)
    write_new = pltpu.make_async_copy(new_out, new_hbm, local_sems.at[4])
    write_new.start()
    for at in range(8):
        sent_a(at)
        sent_b(at)
    pltpu.make_async_copy(sent_x, sent_x, send_c).wait()
    pltpu.make_async_copy(sent_y, sent_y, send_d).wait()
    write_sens.wait()
    write_new.wait()


def hand_over(new_held, sens_held, new_hbm, sens_hbm, sems):
    copies = [
        pltpu.make_async_copy(new_held, new_hbm, sems.at[0]),
        pltpu.make_async_copy(sens_held, sens_hbm, sems.at[1]),
    ]
    for copy in copies:
        copy.start()
    for copy in copies:
        copy.wait()


def per_device(count_x, count_y, density, displacement, passive):
    cols_x, cols_y, planes = density.shape
    assert cols_y == ROWS and cols_x % ROWS == 0 and planes == 128
    block = cols_x * ROWS
    slots = 2**BISECT

    def buffer(*shape):
        return pltpu.VMEM(shape, jnp.float32)

    field = buffer(block, planes)
    tile = buffer(ROWS, planes)
    wide = buffer(block + 2 * ROWS, planes)
    rows = buffer(cols_x, planes)
    ring = buffer(cols_x + ROWS, planes)
    anywhere = pl.BlockSpec(memory_space=pl.ANY)
    out = jax.ShapeDtypeStruct((block, planes), jnp.float32)
    new_density, sensitivity = pl.pallas_call(
        functools.partial(kernel, count_x, count_y),
        out_shape=(out, out),
        in_specs=[anywhere] * 3,
        out_specs=[anywhere] * 2,
        scratch_shapes=[
            buffer(4, block + 2 * ROWS, planes),
            pltpu.VMEM((block, planes), jnp.int32),
            buffer(4, cols_x, planes),
            rows,
            buffer(4, cols_x + ROWS, planes),
            ring,
            wide,
            rows,
            rows,
            ring,
            ring,
            tile,
            tile,
            tile,
            buffer(4, ROWS, planes),
            tile,
            tile,
            tile,
            tile,
            buffer(3, block + ROWS, planes),
            field,
            field,
            field,
            field,
            field,
            field,
            field,
            buffer(slots * ROWS, planes),
            buffer(count_x, slots // planes, planes),
            buffer(count_y, slots // planes, planes),
            field,
            field,
            pltpu.SemaphoreType.DMA((5,)),
            pltpu.SemaphoreType.DMA((8,)),
            pltpu.SemaphoreType.DMA((8,)),
            pltpu.SemaphoreType.DMA((8,)),
            pltpu.SemaphoreType.DMA((8,)),
            pltpu.SemaphoreType.DMA,
            pltpu.SemaphoreType.DMA,
            pltpu.SemaphoreType.DMA,
            pltpu.SemaphoreType.DMA,
        ],
        compiler_params=pltpu.CompilerParams(
            collective_id=0, has_side_effects=True, vmem_limit_bytes=60 * 1024 * 1024
        ),
    )(
        density.reshape(block, planes),
        displacement.reshape(3, block, planes),
        passive.reshape(block, planes),
    )
    new_density, sensitivity = pl.pallas_call(
        hand_over,
        out_shape=(out, out),
        in_specs=[anywhere] * 2,
        out_specs=[anywhere] * 2,
        scratch_shapes=[pltpu.SemaphoreType.DMA((2,))],
        compiler_params=pltpu.CompilerParams(vmem_limit_bytes=60 * 1024 * 1024),
    )(new_density, sensitivity)
    return (new_density.reshape(density.shape), sensitivity.reshape(density.shape))


def solution(mesh):
    return jax.shard_map(
        functools.partial(per_device, mesh.shape["gx"], mesh.shape["gy"]),
        mesh=mesh,
        in_specs=(P("gx", "gy", None), P(None, "gx", "gy", None), P("gx", "gy", None)),
        out_specs=(P("gx", "gy", None), P("gx", "gy", None)),
        check_vma=False,
    )
```

```python
import functools
import math

import jax
import jax.numpy as jnp
from jax import lax
from jax.experimental import pallas as pl
from jax.experimental.pallas import tpu as pltpu
from jax.sharding import PartitionSpec as P

BISECT = 8
BRACKET = 8.0
MOVE_LIMIT = 0.2
VOLUME_SHARE = 0.35
DERIVATIVE = 3.0 * (1.0 - 1e-09)
EDGE_WEIGHT = 1.5 - math.sqrt(2.0)
POISSON = 0.3
LAME_FIRST = POISSON / ((1.0 + POISSON) * (1.0 - 2.0 * POISSON))
SHEAR = 0.5 / (1.0 + POISSON)
ROWS = 8
MESH = pl.DeviceIdType.MESH
WAYS = [(1, 0), (-1, 0), (0, 1), (0, -1), (1, 1), (-1, 1), (1, -1), (-1, -1)]


def z_neighbours(value, lane):
    planes = value.shape[-1]
    axis = value.ndim - 1
    above = jnp.where(lane == planes - 1, 0.0, pltpu.roll(value, planes - 1, axis))
    below = jnp.where(lane == 0, 0.0, pltpu.roll(value, 1, axis))
    return above + below


def parts_of_filter(value, lane):
    beside = z_neighbours(value, lane)
    return (
        1.5 * value + 0.5 * beside,
        0.5 * value + EDGE_WEIGHT * beside,
        EDGE_WEIGHT * value,
    )


def filter_rows(packed, lane, cols_x):
    _, near, far = parts_of_filter(packed, lane)
    count = packed.shape[0]
    return (near + pltpu.roll(far, 1, 0) + pltpu.roll(far, count - 1, 0))[:cols_x]


def filter_chunk(field, first, size, row_low, row_high, row, lane):
    planes = field.shape[-1]
    value = field[pl.ds(first * ROWS, (size + 2) * ROWS), :].reshape(size + 2, ROWS, planes)
    own, near, far = parts_of_filter(value, lane)
    side = near[1:-1] + far[:-2] + far[2:]
    above = row_high[pl.ds(first * ROWS, size * ROWS), :].reshape(size, ROWS, planes)
    below = row_low[pl.ds(first * ROWS, size * ROWS), :].reshape(size, ROWS, planes)
    above = jnp.where(row == ROWS - 1, above, pltpu.roll(side, ROWS - 1, 1))
    below = jnp.where(row == 0, below, pltpu.roll(side, 1, 1))
    return own[1:-1] + near[:-2] + near[2:] + (above + below)


def corner_modes(value, row_high, row, lane):
    planes = value.shape[-1]
    above = jnp.where(row == ROWS - 1, row_high, pltpu.roll(value, ROWS - 1, 1))
    total, step = value + above, above - value

    def next_z(field):
        return jnp.where(lane == planes - 1, 0.0, pltpu.roll(field, planes - 1, 2))

    total_next, step_next = next_z(total), next_z(step)
    both = total + total_next
    along_z = total_next - total
    along_y = step + step_next
    along_yz = step_next - step
    return (
        both[1:] - both[:-1],
        along_y[1:] + along_y[:-1],
        along_z[1:] + along_z[:-1],
        along_y[1:] - along_y[:-1],
        along_z[1:] - along_z[:-1],
        along_yz[1:] + along_yz[:-1],
        along_yz[1:] - along_yz[:-1],
    )


def element_energy(modes):
    (ax, ay, az, axy, axz, ayz, axyz), (bx, by, bz, bxy, bxz, byz, bxyz), (
        cx,
        cy,
        cz,
        cxy,
        cxz,
        cyz,
        cxyz,
    ) = modes

    def sq(value):
        return value * value

    first = (
        (LAME_FIRST / 16.0) * sq(ax + by + cz)
        + (2.0 * SHEAR / 16.0) * (sq(ax) + sq(by) + sq(cz))
        + (SHEAR / 16.0) * (sq(ay + bx) + sq(az + cx) + sq(bz + cy))
    )
    second = (
        (LAME_FIRST / 48.0) * (sq(axy + cyz) + sq(bxy + cxz) + sq(axz + byz))
        + (3.0 * SHEAR / 48.0) * (sq(axy) + sq(axz) + sq(bxy) + sq(byz) + sq(cxz) + sq(cyz))
        + (SHEAR / 48.0) * (sq(ayz + bxz) + sq(ayz + cxy) + sq(bxz + cxy))
    )
    third = ((LAME_FIRST + 4.0 * SHEAR) / 144.0) * (sq(axyz) + sq(bxyz) + sq(cxyz))
    return first + second + third


def kernel(
    count_x,
    count_y,
    dens_hbm,
    disp_hbm,
    pas_hbm,
    new_out,
    sens_out,
    big,
    passive,
    pack_low,
    pack_high,
    row_high,
    row_low,
    spread,
    spread_pack_low,
    spread_pack_high,
    spread_row_high,
    spread_row_low,
    corner_pp,
    corner_mp,
    corner_pm,
    corner_mm,
    s_corner_pp,
    s_corner_mp,
    s_corner_pm,
    s_corner_mm,
    node_row,
    tail_high,
    tail_low,
    inverse,
    inverse_volume,
    scaled,
    lower,
    upper,
    partial,
    totals_x,
    totals_y,
    local_sems,
    send_a,
    recv_a,
    send_b,
    recv_b,
    send_c,
    recv_c,
    send_d,
    recv_d,
):
    planes = dens_hbm.shape[-1]
    cols_x = dens_hbm.shape[0] // ROWS
    block = cols_x * ROWS
    last = cols_x * ROWS
    ix, iy = lax.axis_index("gx"), lax.axis_index("gy")
    total_x, total_y = cols_x * count_x, ROWS * count_y

    def inside(x, y):
        return (x >= 0) & (x < count_x) & (y >= 0) & (y < count_y)

    def along_x(step):
        return (lax.rem(ix + step, count_x), iy)

    def along_y(step):
        return (ix, lax.rem(iy + step, count_y))

    barrier = pltpu.get_barrier_semaphore()

    def greet(device):
        pl.semaphore_signal(barrier, inc=1, device_id=device, device_id_type=MESH)

    for step in range(1, count_x):
        greet(along_x(step))
    for step in range(1, count_y):
        greet(along_y(step))
    greetings = count_x - 1 + count_y - 1
    for dx, dy in WAYS[4:]:
        present = inside(ix + dx, iy + dy)
        greetings = greetings + jnp.where(present, 1, 0)

        @pl.when(present)
        def _(dx=dx, dy=dy):
            greet((ix + dx, iy + dy))

    loads = [
        pltpu.make_async_copy(dens_hbm, big.at[0, pl.ds(ROWS, block)], local_sems.at[0]),
        pltpu.make_async_copy(disp_hbm, big.at[pl.ds(1, 3), pl.ds(ROWS, block)], local_sems.at[1]),
        pltpu.make_async_copy(pas_hbm, passive, local_sems.at[2]),
    ]
    for load in loads:
        load.start()

    def fill(way, refs):
        @pl.when(jnp.logical_not(inside(ix - way[0], iy - way[1])))
        def _():
            for ref in refs:
                ref[...] = jnp.zeros(ref.shape, ref.dtype)

    def exchange(pairs, send, recv):
        def copy(at):
            source, target = pairs[at]
            dx, dy = WAYS[at]
            return pltpu.make_async_remote_copy(
                src_ref=source,
                dst_ref=target,
                send_sem=send.at[at],
                recv_sem=recv.at[at],
                device_id=(ix + dx, iy + dy),
                device_id_type=MESH,
            )

        def start(at):
            dx, dy = WAYS[at]

            @pl.when(inside(ix + dx, iy + dy))
            def _():
                copy(at).start()

        def arrive(at):
            dx, dy = WAYS[at]

            @pl.when(inside(ix - dx, iy - dy))
            def _():
                copy(at).wait_recv()

        def sent(at):
            dx, dy = WAYS[at]

            @pl.when(inside(ix + dx, iy + dy))
            def _():
                copy(at).wait_send()

        return start, arrive, sent

    first_tile, last_tile = pl.ds(ROWS, ROWS), pl.ds(last, ROWS)
    low_tile, high_tile = pl.ds(0, ROWS), pl.ds(last + ROWS, ROWS)
    start_a, arrive_a, sent_a = exchange(
        [
            (big.at[0, last_tile], big.at[0, low_tile]),
            (big.at[:, first_tile], big.at[:, high_tile]),
            (pack_high, row_low.at[pl.ds(0, cols_x)]),
            (pack_low, row_high.at[:, pl.ds(0, cols_x)]),
            (big.at[0, last_tile], corner_pp),
            (big.at[0, first_tile], corner_mp),
            (big.at[0, last_tile], corner_pm),
            (big.at[:, first_tile], corner_mm),
        ],
        send_a,
        recv_a,
    )
    start_b, arrive_b, sent_b = exchange(
        [
            (spread.at[last_tile], spread.at[low_tile]),
            (spread.at[first_tile], spread.at[high_tile]),
            (spread_pack_high, spread_row_low.at[pl.ds(0, cols_x)]),
            (spread_pack_low, spread_row_high.at[pl.ds(0, cols_x)]),
            (spread.at[last_tile], s_corner_pp),
            (spread.at[first_tile], s_corner_mp),
            (spread.at[last_tile], s_corner_pm),
            (spread.at[first_tile], s_corner_mm),
        ],
        send_b,
        recv_b,
    )
    fill(WAYS[0], [big.at[0, low_tile], spread.at[low_tile]])
    fill(WAYS[1], [big.at[:, high_tile], spread.at[high_tile]])
    fill(WAYS[2], [row_low.at[pl.ds(0, cols_x)], spread_row_low.at[pl.ds(0, cols_x)]])
    fill(WAYS[3], [row_high.at[:, pl.ds(0, cols_x)], spread_row_high.at[pl.ds(0, cols_x)]])
    fill(WAYS[4], [corner_pp, s_corner_pp])
    fill(WAYS[5], [corner_mp, s_corner_mp])
    fill(WAYS[6], [corner_pm, s_corner_pm])
    fill(WAYS[7], [corner_mm, s_corner_mm])

    def strided(start):
        return pl.ds(start, cols_x, stride=ROWS)

    loads[0].wait()
    pack_high[...] = big[0, strided(ROWS + ROWS - 1), :]
    pack_low[0] = big[0, strided(ROWS), :]
    loads[1].wait()
    for c in (1, 2, 3):
        pack_low[c] = big[c, strided(ROWS), :]
    pl.semaphore_wait(barrier, greetings)
    for at in (3, 1, 2, 7, 0, 4, 5, 6):
        start_a(at)

    lane = lax.broadcasted_iota(jnp.int32, (ROWS, planes), 1)
    row = lax.broadcasted_iota(jnp.int32, (ROWS, planes), 0)

    def counted(at, total):
        one, none = jnp.float32(1.0), jnp.float32(0.0)
        return jnp.where(at > 0, one, none) + jnp.where(at < total - 1, one, none)

    count_z = counted(lane, planes)
    known = {}

    def representative(x):
        return x if x in (-1, 0, cols_x - 1, cols_x) else 1

    def inverse_sums(x, offset):
        x = representative(x)
        if (x, offset) not in known:
            y = iy * ROWS + row + offset
            beside_y = counted(y, total_y)
            global_x = ix * cols_x + x
            beside_x = counted(global_x, total_x)
            sums = (
                1.5
                + 0.5 * (beside_x + beside_y + count_z)
                + EDGE_WEIGHT * (beside_x * beside_y + beside_x * count_z + beside_y * count_z)
            )
            result = 1.0 / sums
            result = jnp.where((y >= 0) & (y < total_y), result, 0.0)
            if x in (-1, cols_x):
                held = (global_x >= 0) & (global_x < total_x)
                result = result * jnp.where(held, jnp.float32(1.0), jnp.float32(0.0))
            known[x, offset] = (result, parts_of_filter(result, lane))
        return known[x, offset]

    weights = {}
    for x in range(cols_x):
        tile = pl.ds(x * ROWS, ROWS)
        inverse[tile, :] = inverse_sums(x, 0)[0]
        key = tuple(representative(x + d) for d in (-1, 0, 1))
        if key not in weights:
            volume = inverse_sums(x, 0)[1][0]
            volume = volume + inverse_sums(x - 1, 0)[1][1] + inverse_sums(x + 1, 0)[1][1]
            for offset in (-1, 1):
                volume = volume + inverse_sums(x, offset)[1][1]
                volume = volume + inverse_sums(x - 1, offset)[1][2]
                volume = volume + inverse_sums(x + 1, offset)[1][2]
            weights[key] = 1.0 / volume
        inverse_volume[tile, :] = weights[key]

    loads[2].wait()
    for at in range(8):
        arrive_a(at)

    def join(rows, first, final):
        rows[pl.ds(cols_x, ROWS), :] = jnp.where(row == 0, first, jnp.where(row == 7, final, 0.0))

    def tails(rows_high, rows_low, pp, mp, pm, mm):
        join(rows_high, mm[0:1, :], pm[0:1, :])
        join(rows_low, mp[7:8, :], pp[7:8, :])
        lane_rows = lax.broadcasted_iota(jnp.int32, (cols_x + ROWS, planes), 1)
        tail_high[strided(ROWS - 1), :] = filter_rows(rows_high[...], lane_rows, cols_x)
        tail_low[strided(0), :] = filter_rows(rows_low[...], lane_rows, cols_x)

    tails(row_high.at[0], row_low, corner_pp, corner_mp, corner_pm, corner_mm.at[0])
    for c in range(3):
        node_row[c, strided(ROWS - 1), :] = row_high[1 + c, pl.ds(0, cols_x), :]
        node_row[c, pl.ds(block + ROWS - 1, 1), :] = corner_mm[1 + c, 0:1, :]

    density = big.at[0]

    def masks(size):
        shape = (size, ROWS, planes)
        return (
            lax.broadcasted_iota(jnp.int32, shape, 1),
            lax.broadcasted_iota(jnp.int32, shape, 2),
        )

    size = 4 if cols_x % 4 == 0 else 1
    rows_here = size * ROWS
    row_s, lane_s = masks(size)
    row_1, lane_1 = masks(size + 1)
    _, lane_2 = masks(size + 2)

    def tiles(ref, first):
        return ref[pl.ds(first * ROWS, rows_here), :].reshape(size, ROWS, planes)

    for first in range(0, cols_x, size):
        near = pl.ds((first + 1) * ROWS, (size + 1) * ROWS)
        high = pl.ds(first * ROWS, (size + 1) * ROWS)
        shape = (size + 1, ROWS, planes)
        modes = [
            corner_modes(
                big[1 + c, near, :].reshape(shape),
                node_row[c, high, :].reshape(shape),
                row_1,
                lane_1,
            )
            for c in range(3)
        ]
        energy = element_energy(modes)
        inv = tiles(inverse, first)
        kind = tiles(passive, first)
        physical = filter_chunk(density, first, size, tail_low, tail_high, row_s, lane_2) * inv
        physical = jnp.where(kind == 1, 1.0, jnp.where(kind == 2, 0.0, physical))
        raw = (-DERIVATIVE) * physical * physical * energy
        spread[pl.ds((first + 1) * ROWS, rows_here), :] = (raw * inv).reshape(rows_here, planes)

    spread_pack_high[...] = spread[strided(ROWS + ROWS - 1), :]
    spread_pack_low[...] = spread[strided(ROWS), :]
    for at in (3, 2, 1, 0, 7, 4, 5, 6):
        start_b(at)

    for first in range(0, cols_x, size):
        at = pl.ds(first * ROWS, rows_here)
        kind = tiles(passive, first)
        held = big[0, pl.ds((first + 1) * ROWS, rows_here), :].reshape(size, ROWS, planes)
        fixed = jnp.where(kind == 1, 1.0, 0.0)
        low = jnp.where(kind == 0, jnp.maximum(held - MOVE_LIMIT, 0.0), fixed)
        high = jnp.where(kind == 0, jnp.minimum(held + MOVE_LIMIT, 1.0), fixed)
        lower[at, :] = low.reshape(rows_here, planes)
        upper[at, :] = high.reshape(rows_here, planes)

    for at in range(8):
        arrive_b(at)
    tails(spread_row_high, spread_row_low, s_corner_pp, s_corner_mp, s_corner_pm, s_corner_mm)
    for first in range(0, cols_x, size):
        at = pl.ds(first * ROWS, rows_here)
        sens = filter_chunk(spread, first, size, tail_low, tail_high, row_s, lane_2)
        held = big[0, pl.ds((first + 1) * ROWS, rows_here), :].reshape(size, ROWS, planes)
        rate = held * jnp.sqrt(-sens * tiles(inverse_volume, first))
        sens_out[at, :] = sens.reshape(rows_here, planes)
        scaled[at, :] = rate.reshape(rows_here, planes)

    slots = 2**BISECT
    group = 16
    spacing = 2.0 * BRACKET / slots
    scales = jnp.concatenate(
        [jnp.full((1, ROWS, planes), math.exp(-0.5 * spacing * j), jnp.float32) for j in range(group)]
    )

    def volumes(i, carry):
        begin = (-BRACKET) + (spacing * group) * i.astype(jnp.float32)
        factors = scales * jnp.exp(jnp.full((ROWS, planes), -0.5 * begin, jnp.float32))[None]
        total = jnp.zeros((group, ROWS, planes), jnp.float32)
        for x in range(cols_x):
            tile = pl.ds(x * ROWS, ROWS)
            moved = jnp.maximum(scaled[tile, :][None] * factors, lower[tile, :][None])
            total = total + jnp.minimum(moved, upper[tile, :][None])
        at = pl.multiple_of(i * (group * ROWS), group * ROWS)
        partial[pl.ds(at, group * ROWS), :] = total.reshape(group * ROWS, planes)
        return carry

    lax.fori_loop(0, slots // group, volumes, 0)
    halves = slots // planes
    for half in range(halves):
        start = half * planes * ROWS
        lines = partial[pl.ds(start, planes, stride=ROWS), :]
        for s in range(1, ROWS):
            lines = lines + partial[pl.ds(start + s, planes, stride=ROWS), :]
        totals_x[ix, half : half + 1, :] = jnp.sum(lines.T, axis=0, keepdims=True)

    def shared(totals, me, target, count, send, recv):
        for step in range(1, count):
            pltpu.make_async_remote_copy(
                src_ref=totals.at[me],
                dst_ref=totals.at[me],
                send_sem=send,
                recv_sem=recv,
                device_id=target(step),
                device_id_type=MESH,
            ).start()
        others = totals.at[pl.ds(0, count - 1)]
        pltpu.make_async_copy(others, others, recv).wait()
        return jnp.sum(totals[...], axis=0), others

    column, sent_x = shared(totals_x, ix, along_x, count_x, send_c, recv_c)
    totals_y[iy] = column
    volume, sent_y = shared(totals_y, iy, along_y, count_y, send_d, recv_d)
    label = lax.broadcasted_iota(jnp.int32, volume.shape, 0) * planes + lax.broadcasted_iota(
        jnp.int32, volume.shape, 1
    )
    target = VOLUME_SHARE * total_x * total_y * planes
    over = jnp.where((label > 0) & (volume > target), 1.0, 0.0)
    reached = jnp.sum(jnp.sum(over, axis=0, keepdims=True), axis=1, keepdims=True)
    middle = (-BRACKET) + spacing * (jnp.broadcast_to(reached, (ROWS, planes)) + 0.5)
    factor = jnp.exp(-0.5 * middle)[None]
    for first in range(0, cols_x, size):
        at = pl.ds(first * ROWS, rows_here)
        moved = jnp.maximum(tiles(scaled, first) * factor, tiles(lower, first))
        new_out[at, :] = jnp.minimum(moved, tiles(upper, first)).reshape(rows_here, planes)
    for at in range(8):
        sent_a(at)
        sent_b(at)
    pltpu.make_async_copy(sent_x, sent_x, send_c).wait()
    pltpu.make_async_copy(sent_y, sent_y, send_d).wait()


def per_device(count_x, count_y, density, displacement, passive):
    cols_x, cols_y, planes = density.shape
    assert cols_y == ROWS and cols_x % ROWS == 0 and planes == 128
    block = cols_x * ROWS
    slots = 2**BISECT

    def buffer(*shape):
        return pltpu.VMEM(shape, jnp.float32)

    field = buffer(block, planes)
    tile = buffer(ROWS, planes)
    wide = buffer(block + 2 * ROWS, planes)
    rows = buffer(cols_x, planes)
    ring = buffer(cols_x + ROWS, planes)
    held = functools.partial(pltpu.with_memory_space_constraint, memory_space=pltpu.HBM)
    anywhere = pl.BlockSpec(memory_space=pl.ANY)
    out = jax.ShapeDtypeStruct((block, planes), jnp.float32)
    new_density, sensitivity = pl.pallas_call(
        functools.partial(kernel, count_x, count_y),
        out_shape=(out, out),
        in_specs=[anywhere] * 3,
        out_specs=[pl.BlockSpec(memory_space=pltpu.VMEM)] * 2,
        scratch_shapes=[
            buffer(4, block + 2 * ROWS, planes),
            pltpu.VMEM((block, planes), jnp.int32),
            buffer(4, cols_x, planes),
            rows,
            buffer(4, cols_x + ROWS, planes),
            ring,
            wide,
            rows,
            rows,
            ring,
            ring,
            tile,
            tile,
            tile,
            buffer(4, ROWS, planes),
            tile,
            tile,
            tile,
            tile,
            buffer(3, block + ROWS, planes),
            field,
            field,
            field,
            field,
            field,
            field,
            field,
            buffer(slots * ROWS, planes),
            buffer(count_x, slots // planes, planes),
            buffer(count_y, slots // planes, planes),
            pltpu.SemaphoreType.DMA((3,)),
            pltpu.SemaphoreType.DMA((8,)),
            pltpu.SemaphoreType.DMA((8,)),
            pltpu.SemaphoreType.DMA((8,)),
            pltpu.SemaphoreType.DMA((8,)),
            pltpu.SemaphoreType.DMA,
            pltpu.SemaphoreType.DMA,
            pltpu.SemaphoreType.DMA,
            pltpu.SemaphoreType.DMA,
        ],
        compiler_params=pltpu.CompilerParams(
            collective_id=0, has_side_effects=True, vmem_limit_bytes=16 * 1024 * 1024
        ),
    )(
        held(density.reshape(block, planes)),
        held(displacement.reshape(3, block, planes)),
        held(passive.reshape(block, planes)),
    )
    return (new_density.reshape(density.shape), sensitivity.reshape(density.shape))


def solution(mesh):
    return jax.shard_map(
        functools.partial(per_device, mesh.shape["gx"], mesh.shape["gy"]),
        mesh=mesh,
        in_specs=(P("gx", "gy", None), P(None, "gx", "gy", None), P("gx", "gy", None)),
        out_specs=(P("gx", "gy", None), P("gx", "gy", None)),
        check_vma=False,
    )
```

```python
import functools
import math

import jax
import jax.numpy as jnp
from jax import lax
from jax.experimental import pallas as pl
from jax.experimental.pallas import tpu as pltpu
from jax.sharding import PartitionSpec as P

BISECT = 8
BRACKET = 8.0
MOVE_LIMIT = 0.2
VOLUME_SHARE = 0.35
DERIVATIVE = 3.0 * (1.0 - 1e-09)
EDGE_WEIGHT = 1.5 - math.sqrt(2.0)
POISSON = 0.3
LAME_FIRST = POISSON / ((1.0 + POISSON) * (1.0 - 2.0 * POISSON))
SHEAR = 0.5 / (1.0 + POISSON)
ROWS = 8
MESH = pl.DeviceIdType.MESH
WAYS = [(1, 0), (-1, 0), (0, 1), (0, -1), (1, 1), (-1, 1), (1, -1), (-1, -1)]


def z_neighbours(value, lane):
    planes = value.shape[-1]
    axis = value.ndim - 1
    above = jnp.where(lane == planes - 1, 0.0, pltpu.roll(value, planes - 1, axis))
    below = jnp.where(lane == 0, 0.0, pltpu.roll(value, 1, axis))
    return above + below


def parts_of_filter(value, lane):
    beside = z_neighbours(value, lane)
    return (
        1.5 * value + 0.5 * beside,
        0.5 * value + EDGE_WEIGHT * beside,
        EDGE_WEIGHT * value,
    )


def filter_rows(packed, lane, cols_x):
    _, near, far = parts_of_filter(packed, lane)
    count = packed.shape[0]
    return (near + pltpu.roll(far, 1, 0) + pltpu.roll(far, count - 1, 0))[:cols_x]


def filter_chunk(field, first, size, row_low, row_high, row, lane):
    planes = field.shape[-1]
    value = field[pl.ds(first * ROWS, (size + 2) * ROWS), :].reshape(size + 2, ROWS, planes)
    own, near, far = parts_of_filter(value, lane)
    side = near[1:-1] + far[:-2] + far[2:]
    above = row_high[pl.ds(first * ROWS, size * ROWS), :].reshape(size, ROWS, planes)
    below = row_low[pl.ds(first * ROWS, size * ROWS), :].reshape(size, ROWS, planes)
    above = jnp.where(row == ROWS - 1, above, pltpu.roll(side, ROWS - 1, 1))
    below = jnp.where(row == 0, below, pltpu.roll(side, 1, 1))
    return own[1:-1] + near[:-2] + near[2:] + (above + below)


def corner_modes(value, row_high, row, lane):
    planes = value.shape[-1]
    above = jnp.where(row == ROWS - 1, row_high, pltpu.roll(value, ROWS - 1, 1))
    total, step = value + above, above - value

    def next_z(field):
        return jnp.where(lane == planes - 1, 0.0, pltpu.roll(field, planes - 1, 2))

    total_next, step_next = next_z(total), next_z(step)
    both = total + total_next
    along_z = total_next - total
    along_y = step + step_next
    along_yz = step_next - step
    return (
        both[1:] - both[:-1],
        along_y[1:] + along_y[:-1],
        along_z[1:] + along_z[:-1],
        along_y[1:] - along_y[:-1],
        along_z[1:] - along_z[:-1],
        along_yz[1:] + along_yz[:-1],
        along_yz[1:] - along_yz[:-1],
    )


def element_energy(modes):
    (ax, ay, az, axy, axz, ayz, axyz), (bx, by, bz, bxy, bxz, byz, bxyz), (
        cx,
        cy,
        cz,
        cxy,
        cxz,
        cyz,
        cxyz,
    ) = modes

    def sq(value):
        return value * value

    first = (
        (LAME_FIRST / 16.0) * sq(ax + by + cz)
        + (2.0 * SHEAR / 16.0) * (sq(ax) + sq(by) + sq(cz))
        + (SHEAR / 16.0) * (sq(ay + bx) + sq(az + cx) + sq(bz + cy))
    )
    second = (
        (LAME_FIRST / 48.0) * (sq(axy + cyz) + sq(bxy + cxz) + sq(axz + byz))
        + (3.0 * SHEAR / 48.0) * (sq(axy) + sq(axz) + sq(bxy) + sq(byz) + sq(cxz) + sq(cyz))
        + (SHEAR / 48.0) * (sq(ayz + bxz) + sq(ayz + cxy) + sq(bxz + cxy))
    )
    third = ((LAME_FIRST + 4.0 * SHEAR) / 144.0) * (sq(axyz) + sq(bxyz) + sq(cxyz))
    return first + second + third


def kernel(
    count_x,
    count_y,
    dens_hbm,
    disp_hbm,
    pas_hbm,
    new_out,
    sens_out,
    big,
    passive,
    pack_low,
    pack_high,
    row_high,
    row_low,
    spread,
    spread_pack_low,
    spread_pack_high,
    spread_row_high,
    spread_row_low,
    corner_pp,
    corner_mp,
    corner_pm,
    corner_mm,
    s_corner_pp,
    s_corner_mp,
    s_corner_pm,
    s_corner_mm,
    node_row,
    tail_high,
    tail_low,
    inverse,
    inverse_volume,
    scaled,
    lower,
    upper,
    sum_scaled,
    sum_lower,
    sum_upper,
    partial,
    totals_x,
    totals_y,
    local_sems,
    send_a,
    recv_a,
    send_b,
    recv_b,
    send_c,
    recv_c,
    send_d,
    recv_d,
):
    planes = dens_hbm.shape[-1]
    cols_x = dens_hbm.shape[0] // ROWS
    block = cols_x * ROWS
    last = cols_x * ROWS
    ix, iy = lax.axis_index("gx"), lax.axis_index("gy")
    total_x, total_y = cols_x * count_x, ROWS * count_y

    def inside(x, y):
        return (x >= 0) & (x < count_x) & (y >= 0) & (y < count_y)

    def along_x(step):
        return (lax.rem(ix + step, count_x), iy)

    def along_y(step):
        return (ix, lax.rem(iy + step, count_y))

    barrier = pltpu.get_barrier_semaphore()

    def greet(device):
        pl.semaphore_signal(barrier, inc=1, device_id=device, device_id_type=MESH)

    for step in range(1, count_x):
        greet(along_x(step))
    for step in range(1, count_y):
        greet(along_y(step))
    greetings = count_x - 1 + count_y - 1
    for dx, dy in WAYS[4:]:
        present = inside(ix + dx, iy + dy)
        greetings = greetings + jnp.where(present, 1, 0)

        @pl.when(present)
        def _(dx=dx, dy=dy):
            greet((ix + dx, iy + dy))

    loads = [
        pltpu.make_async_copy(dens_hbm, big.at[0, pl.ds(ROWS, block)], local_sems.at[0]),
        pltpu.make_async_copy(disp_hbm, big.at[pl.ds(1, 3), pl.ds(ROWS, block)], local_sems.at[1]),
        pltpu.make_async_copy(pas_hbm, passive, local_sems.at[2]),
    ]
    for load in loads:
        load.start()

    def fill(way, refs):
        @pl.when(jnp.logical_not(inside(ix - way[0], iy - way[1])))
        def _():
            for ref in refs:
                ref[...] = jnp.zeros(ref.shape, ref.dtype)

    def exchange(pairs, send, recv):
        def copy(at):
            source, target = pairs[at]
            dx, dy = WAYS[at]
            return pltpu.make_async_remote_copy(
                src_ref=source,
                dst_ref=target,
                send_sem=send.at[at],
                recv_sem=recv.at[at],
                device_id=(ix + dx, iy + dy),
                device_id_type=MESH,
            )

        def start(at):
            dx, dy = WAYS[at]

            @pl.when(inside(ix + dx, iy + dy))
            def _():
                copy(at).start()

        def arrive(at):
            dx, dy = WAYS[at]

            @pl.when(inside(ix - dx, iy - dy))
            def _():
                copy(at).wait_recv()

        def sent(at):
            dx, dy = WAYS[at]

            @pl.when(inside(ix + dx, iy + dy))
            def _():
                copy(at).wait_send()

        return start, arrive, sent

    first_tile, last_tile = pl.ds(ROWS, ROWS), pl.ds(last, ROWS)
    low_tile, high_tile = pl.ds(0, ROWS), pl.ds(last + ROWS, ROWS)
    start_a, arrive_a, sent_a = exchange(
        [
            (big.at[0, last_tile], big.at[0, low_tile]),
            (big.at[:, first_tile], big.at[:, high_tile]),
            (pack_high, row_low.at[pl.ds(0, cols_x)]),
            (pack_low, row_high.at[:, pl.ds(0, cols_x)]),
            (big.at[0, last_tile], corner_pp),
            (big.at[0, first_tile], corner_mp),
            (big.at[0, last_tile], corner_pm),
            (big.at[:, first_tile], corner_mm),
        ],
        send_a,
        recv_a,
    )
    start_b, arrive_b, sent_b = exchange(
        [
            (spread.at[last_tile], spread.at[low_tile]),
            (spread.at[first_tile], spread.at[high_tile]),
            (spread_pack_high, spread_row_low.at[pl.ds(0, cols_x)]),
            (spread_pack_low, spread_row_high.at[pl.ds(0, cols_x)]),
            (spread.at[last_tile], s_corner_pp),
            (spread.at[first_tile], s_corner_mp),
            (spread.at[last_tile], s_corner_pm),
            (spread.at[first_tile], s_corner_mm),
        ],
        send_b,
        recv_b,
    )
    fill(WAYS[0], [big.at[0, low_tile], spread.at[low_tile]])
    fill(WAYS[1], [big.at[:, high_tile], spread.at[high_tile]])
    fill(WAYS[2], [row_low.at[pl.ds(0, cols_x)], spread_row_low.at[pl.ds(0, cols_x)]])
    fill(WAYS[3], [row_high.at[:, pl.ds(0, cols_x)], spread_row_high.at[pl.ds(0, cols_x)]])
    fill(WAYS[4], [corner_pp, s_corner_pp])
    fill(WAYS[5], [corner_mp, s_corner_mp])
    fill(WAYS[6], [corner_pm, s_corner_pm])
    fill(WAYS[7], [corner_mm, s_corner_mm])

    def strided(start):
        return pl.ds(start, cols_x, stride=ROWS)

    loads[0].wait()
    pack_high[...] = big[0, strided(ROWS + ROWS - 1), :]
    pack_low[0] = big[0, strided(ROWS), :]
    loads[1].wait()
    for c in (1, 2, 3):
        pack_low[c] = big[c, strided(ROWS), :]
    pl.semaphore_wait(barrier, greetings)
    for at in (3, 1, 2, 7, 0, 4, 5, 6):
        start_a(at)

    lane = lax.broadcasted_iota(jnp.int32, (ROWS, planes), 1)
    row = lax.broadcasted_iota(jnp.int32, (ROWS, planes), 0)

    def counted(at, total):
        one, none = jnp.float32(1.0), jnp.float32(0.0)
        return jnp.where(at > 0, one, none) + jnp.where(at < total - 1, one, none)

    count_z = counted(lane, planes)
    known = {}

    def representative(x):
        return x if x in (-1, 0, cols_x - 1, cols_x) else 1

    def inverse_sums(x, offset):
        x = representative(x)
        if (x, offset) not in known:
            y = iy * ROWS + row + offset
            beside_y = counted(y, total_y)
            global_x = ix * cols_x + x
            beside_x = counted(global_x, total_x)
            sums = (
                1.5
                + 0.5 * (beside_x + beside_y + count_z)
                + EDGE_WEIGHT * (beside_x * beside_y + beside_x * count_z + beside_y * count_z)
            )
            result = 1.0 / sums
            result = jnp.where((y >= 0) & (y < total_y), result, 0.0)
            if x in (-1, cols_x):
                held = (global_x >= 0) & (global_x < total_x)
                result = result * jnp.where(held, jnp.float32(1.0), jnp.float32(0.0))
            known[x, offset] = (result, parts_of_filter(result, lane))
        return known[x, offset]

    weights = {}
    for x in range(cols_x):
        tile = pl.ds(x * ROWS, ROWS)
        inverse[tile, :] = inverse_sums(x, 0)[0]
        key = tuple(representative(x + d) for d in (-1, 0, 1))
        if key not in weights:
            volume = inverse_sums(x, 0)[1][0]
            volume = volume + inverse_sums(x - 1, 0)[1][1] + inverse_sums(x + 1, 0)[1][1]
            for offset in (-1, 1):
                volume = volume + inverse_sums(x, offset)[1][1]
                volume = volume + inverse_sums(x - 1, offset)[1][2]
                volume = volume + inverse_sums(x + 1, offset)[1][2]
            weights[key] = 1.0 / volume
        inverse_volume[tile, :] = weights[key]

    loads[2].wait()
    for at in range(8):
        arrive_a(at)

    def join(rows, first, final):
        rows[pl.ds(cols_x, ROWS), :] = jnp.where(row == 0, first, jnp.where(row == 7, final, 0.0))

    def tails(rows_high, rows_low, pp, mp, pm, mm):
        join(rows_high, mm[0:1, :], pm[0:1, :])
        join(rows_low, mp[7:8, :], pp[7:8, :])
        lane_rows = lax.broadcasted_iota(jnp.int32, (cols_x + ROWS, planes), 1)
        tail_high[strided(ROWS - 1), :] = filter_rows(rows_high[...], lane_rows, cols_x)
        tail_low[strided(0), :] = filter_rows(rows_low[...], lane_rows, cols_x)

    tails(row_high.at[0], row_low, corner_pp, corner_mp, corner_pm, corner_mm.at[0])
    for c in range(3):
        node_row[c, strided(ROWS - 1), :] = row_high[1 + c, pl.ds(0, cols_x), :]
        node_row[c, pl.ds(block + ROWS - 1, 1), :] = corner_mm[1 + c, 0:1, :]

    density = big.at[0]

    def masks(size):
        shape = (size, ROWS, planes)
        return (
            lax.broadcasted_iota(jnp.int32, shape, 1),
            lax.broadcasted_iota(jnp.int32, shape, 2),
        )

    size = 4 if cols_x % 4 == 0 else 1
    rows_here = size * ROWS
    row_s, lane_s = masks(size)
    row_1, lane_1 = masks(size + 1)
    _, lane_2 = masks(size + 2)

    def tiles(ref, first):
        return ref[pl.ds(first * ROWS, rows_here), :].reshape(size, ROWS, planes)

    for first in range(0, cols_x, size):
        near = pl.ds((first + 1) * ROWS, (size + 1) * ROWS)
        high = pl.ds(first * ROWS, (size + 1) * ROWS)
        shape = (size + 1, ROWS, planes)
        modes = [
            corner_modes(
                big[1 + c, near, :].reshape(shape),
                node_row[c, high, :].reshape(shape),
                row_1,
                lane_1,
            )
            for c in range(3)
        ]
        energy = element_energy(modes)
        inv = tiles(inverse, first)
        kind = tiles(passive, first)
        physical = filter_chunk(density, first, size, tail_low, tail_high, row_s, lane_2) * inv
        physical = jnp.where(kind == 1, 1.0, jnp.where(kind == 2, 0.0, physical))
        raw = (-DERIVATIVE) * physical * physical * energy
        spread[pl.ds((first + 1) * ROWS, rows_here), :] = (raw * inv).reshape(rows_here, planes)

    spread_pack_high[...] = spread[strided(ROWS + ROWS - 1), :]
    spread_pack_low[...] = spread[strided(ROWS), :]
    for at in (3, 2, 1, 0, 7, 4, 5, 6):
        start_b(at)

    for first in range(0, cols_x, size):
        at = pl.ds(first * ROWS, rows_here)
        kind = tiles(passive, first)
        held = big[0, pl.ds((first + 1) * ROWS, rows_here), :].reshape(size, ROWS, planes)
        fixed = jnp.where(kind == 1, 1.0, 0.0)
        low = jnp.where(kind == 0, jnp.maximum(held - MOVE_LIMIT, 0.0), fixed)
        high = jnp.where(kind == 0, jnp.minimum(held + MOVE_LIMIT, 1.0), fixed)
        lower[at, :] = low.reshape(rows_here, planes)
        upper[at, :] = high.reshape(rows_here, planes)

    def rate_of(sens, held, weight):
        return held * jnp.sqrt(-sens * weight)

    def middle_rows(value, index):
        return jnp.where((index > 0) & (index < ROWS - 1), value, 0.0)

    def plane_group(first, count, place):
        shape = (count, ROWS, planes)
        row_c = lax.broadcasted_iota(jnp.int32, shape, 1)
        lane_c = lax.broadcasted_iota(jnp.int32, (count + 2, ROWS, planes), 2)
        wide = spread[pl.ds(first * ROWS, (count + 2) * ROWS), :].reshape(count + 2, ROWS, planes)
        own, near, far = parts_of_filter(wide, lane_c)
        side = near[1:-1] + far[:-2] + far[2:]
        sens = own[1:-1] + near[:-2] + near[2:]
        sens = sens + (pltpu.roll(side, ROWS - 1, 1) + pltpu.roll(side, 1, 1))
        at = pl.ds(first * ROWS, count * ROWS)
        held = big[0, pl.ds((first + 1) * ROWS, count * ROWS), :].reshape(shape)
        sens = middle_rows(sens, row_c)
        rate = rate_of(sens, held, inverse_volume[at, :].reshape(shape))
        sens_out[at, :] = sens.reshape(count * ROWS, planes)
        scaled[at, :] = rate.reshape(count * ROWS, planes)
        to = pl.ds(place * ROWS, count * ROWS)
        sum_scaled[to, :] = rate.reshape(count * ROWS, planes)
        for source, target in ((lower, sum_lower), (upper, sum_upper)):
            kept = middle_rows(source[at, :].reshape(shape), row_c)
            target[to, :] = kept.reshape(count * ROWS, planes)

    slots = 2**BISECT
    group = 16
    spacing = 2.0 * BRACKET / slots
    scales = jnp.concatenate(
        [jnp.full((1, ROWS, planes), math.exp(-0.5 * spacing * j), jnp.float32) for j in range(group)]
    )

    def add_volumes(first_tile, end_tile, fresh):
        def volumes(i, carry):
            begin = (-BRACKET) + (spacing * group) * i.astype(jnp.float32)
            factors = scales * jnp.exp(jnp.full((ROWS, planes), -0.5 * begin, jnp.float32))[None]
            at = pl.ds(pl.multiple_of(i * (group * ROWS), group * ROWS), group * ROWS)
            if fresh:
                total = jnp.zeros((group, ROWS, planes), jnp.float32)
            else:
                total = partial[at, :].reshape(group, ROWS, planes)
            for x in range(first_tile, end_tile):
                tile = pl.ds(x * ROWS, ROWS)
                moved = jnp.maximum(sum_scaled[tile, :][None] * factors, sum_lower[tile, :][None])
                total = total + jnp.minimum(moved, sum_upper[tile, :][None])
            partial[at, :] = total.reshape(group * ROWS, planes)
            return carry

        lax.fori_loop(0, slots // group, volumes, 0)

    inner = cols_x - 2
    for first in range(1, 1 + inner, size):
        plane_group(first, min(size, 1 + inner - first), first - 1)
    add_volumes(0, inner, True)

    for at in range(8):
        arrive_b(at)
    plane_group(0, 1, inner)
    plane_group(cols_x - 1, 1, inner + 1)
    join(spread_row_high, s_corner_mm[0:1, :], s_corner_pm[0:1, :])
    join(spread_row_low, s_corner_mp[7:8, :], s_corner_pp[7:8, :])
    lane_p = lax.broadcasted_iota(jnp.int32, (cols_x + ROWS, planes), 1)

    def packed_row(r):
        above = spread[pl.ds(last + ROWS + r, 1), :]
        below = spread[pl.ds(r, 1), :]
        tail = jnp.where(row == 0, above, jnp.where(row == ROWS - 1, below, 0.0))
        return jnp.concatenate([spread[strided(ROWS + r), :], tail], axis=0)

    def edge_row(r, beyond, next_row, held, place):
        own, near, _ = parts_of_filter(packed_row(r), lane_p)
        count = own.shape[0]
        sens = (own + pltpu.roll(near, 1, 0) + pltpu.roll(near, count - 1, 0))[:cols_x]
        sens = sens + filter_rows(beyond, lane_p, cols_x)
        sens = sens + filter_rows(packed_row(next_row), lane_p, cols_x)
        rate = rate_of(sens, held, inverse_volume[strided(r), :])
        sens_out[strided(r), :] = sens
        scaled[strided(r), :] = rate
        to = pl.ds(place * ROWS, cols_x)
        sum_scaled[to, :] = rate
        sum_lower[to, :] = lower[strided(r), :]
        sum_upper[to, :] = upper[strided(r), :]

    edge_row(0, spread_row_low[...], 1, pack_low[0], inner + 2)
    edge_row(ROWS - 1, spread_row_high[...], ROWS - 2, pack_high[...], inner + 2 + cols_x // ROWS)
    add_volumes(inner, inner + 2 + 2 * (cols_x // ROWS), False)
    halves = slots // planes
    for half in range(halves):
        start = half * planes * ROWS
        lines = partial[pl.ds(start, planes, stride=ROWS), :]
        for s in range(1, ROWS):
            lines = lines + partial[pl.ds(start + s, planes, stride=ROWS), :]
        totals_x[ix, half : half + 1, :] = jnp.sum(lines.T, axis=0, keepdims=True)

    def shared(totals, me, target, count, send, recv):
        for step in range(1, count):
            pltpu.make_async_remote_copy(
                src_ref=totals.at[me],
                dst_ref=totals.at[me],
                send_sem=send,
                recv_sem=recv,
                device_id=target(step),
                device_id_type=MESH,
            ).start()
        others = totals.at[pl.ds(0, count - 1)]
        pltpu.make_async_copy(others, others, recv).wait()
        return jnp.sum(totals[...], axis=0), others

    column, sent_x = shared(totals_x, ix, along_x, count_x, send_c, recv_c)
    totals_y[iy] = column
    volume, sent_y = shared(totals_y, iy, along_y, count_y, send_d, recv_d)
    label = lax.broadcasted_iota(jnp.int32, volume.shape, 0) * planes + lax.broadcasted_iota(
        jnp.int32, volume.shape, 1
    )
    target = VOLUME_SHARE * total_x * total_y * planes
    over = jnp.where((label > 0) & (volume > target), 1.0, 0.0)
    reached = jnp.sum(jnp.sum(over, axis=0, keepdims=True), axis=1, keepdims=True)
    middle = (-BRACKET) + spacing * (jnp.broadcast_to(reached, (ROWS, planes)) + 0.5)
    factor = jnp.exp(-0.5 * middle)[None]
    for first in range(0, cols_x, size):
        at = pl.ds(first * ROWS, rows_here)
        moved = jnp.maximum(tiles(scaled, first) * factor, tiles(lower, first))
        new_out[at, :] = jnp.minimum(moved, tiles(upper, first)).reshape(rows_here, planes)
    for at in range(8):
        sent_a(at)
        sent_b(at)
    pltpu.make_async_copy(sent_x, sent_x, send_c).wait()
    pltpu.make_async_copy(sent_y, sent_y, send_d).wait()


def per_device(count_x, count_y, density, displacement, passive):
    cols_x, cols_y, planes = density.shape
    assert cols_y == ROWS and cols_x % ROWS == 0 and planes == 128
    block = cols_x * ROWS
    slots = 2**BISECT

    def buffer(*shape):
        return pltpu.VMEM(shape, jnp.float32)

    field = buffer(block, planes)
    tile = buffer(ROWS, planes)
    wide = buffer(block + 2 * ROWS, planes)
    rows = buffer(cols_x, planes)
    sums = buffer(block + 2 * cols_x, planes)
    ring = buffer(cols_x + ROWS, planes)
    held = functools.partial(pltpu.with_memory_space_constraint, memory_space=pltpu.HBM)
    anywhere = pl.BlockSpec(memory_space=pl.ANY)
    out = jax.ShapeDtypeStruct((block, planes), jnp.float32)
    new_density, sensitivity = pl.pallas_call(
        functools.partial(kernel, count_x, count_y),
        out_shape=(out, out),
        in_specs=[anywhere] * 3,
        out_specs=[pl.BlockSpec(memory_space=pltpu.VMEM)] * 2,
        scratch_shapes=[
            buffer(4, block + 2 * ROWS, planes),
            pltpu.VMEM((block, planes), jnp.int32),
            buffer(4, cols_x, planes),
            rows,
            buffer(4, cols_x + ROWS, planes),
            ring,
            wide,
            rows,
            rows,
            ring,
            ring,
            tile,
            tile,
            tile,
            buffer(4, ROWS, planes),
            tile,
            tile,
            tile,
            tile,
            buffer(3, block + ROWS, planes),
            field,
            field,
            field,
            field,
            field,
            field,
            field,
            sums,
            sums,
            sums,
            buffer(slots * ROWS, planes),
            buffer(count_x, slots // planes, planes),
            buffer(count_y, slots // planes, planes),
            pltpu.SemaphoreType.DMA((3,)),
            pltpu.SemaphoreType.DMA((8,)),
            pltpu.SemaphoreType.DMA((8,)),
            pltpu.SemaphoreType.DMA((8,)),
            pltpu.SemaphoreType.DMA((8,)),
            pltpu.SemaphoreType.DMA,
            pltpu.SemaphoreType.DMA,
            pltpu.SemaphoreType.DMA,
            pltpu.SemaphoreType.DMA,
        ],
        compiler_params=pltpu.CompilerParams(
            collective_id=0, has_side_effects=True, vmem_limit_bytes=16 * 1024 * 1024
        ),
    )(
        held(density.reshape(block, planes)),
        held(displacement.reshape(3, block, planes)),
        held(passive.reshape(block, planes)),
    )
    return (new_density.reshape(density.shape), sensitivity.reshape(density.shape))


def solution(mesh):
    return jax.shard_map(
        functools.partial(per_device, mesh.shape["gx"], mesh.shape["gy"]),
        mesh=mesh,
        in_specs=(P("gx", "gy", None), P(None, "gx", "gy", None), P("gx", "gy", None)),
        out_specs=(P("gx", "gy", None), P("gx", "gy", None)),
        check_vma=False,
    )
```

```python
import functools
import math

import jax
import jax.numpy as jnp
from jax import lax
from jax.experimental import pallas as pl
from jax.experimental.pallas import tpu as pltpu
from jax.sharding import PartitionSpec as P

BISECT = 8
BRACKET = 8.0
MOVE_LIMIT = 0.2
VOLUME_SHARE = 0.35
DERIVATIVE = 3.0 * (1.0 - 1e-09)
EDGE_WEIGHT = 1.5 - math.sqrt(2.0)
POISSON = 0.3
LAME_FIRST = POISSON / ((1.0 + POISSON) * (1.0 - 2.0 * POISSON))
SHEAR = 0.5 / (1.0 + POISSON)
ROWS = 8
MESH = pl.DeviceIdType.MESH
WAYS = [(1, 0), (-1, 0), (0, 1), (0, -1), (1, 1), (-1, 1), (1, -1), (-1, -1)]


def z_neighbours(value, lane):
    planes = value.shape[-1]
    axis = value.ndim - 1
    above = jnp.where(lane == planes - 1, 0.0, pltpu.roll(value, planes - 1, axis))
    below = jnp.where(lane == 0, 0.0, pltpu.roll(value, 1, axis))
    return above + below


def parts_of_filter(value, lane):
    beside = z_neighbours(value, lane)
    return (
        1.5 * value + 0.5 * beside,
        0.5 * value + EDGE_WEIGHT * beside,
        EDGE_WEIGHT * value,
    )


def filter_rows(packed, lane, cols_x):
    _, near, far = parts_of_filter(packed, lane)
    count = packed.shape[0]
    return (near + pltpu.roll(far, 1, 0) + pltpu.roll(far, count - 1, 0))[:cols_x]


def filter_chunk(field, first, size, row_low, row_high, row, lane):
    planes = field.shape[-1]
    start = pl.multiple_of(first * ROWS, ROWS)
    value = field[pl.ds(start, (size + 2) * ROWS), :].reshape(size + 2, ROWS, planes)
    own, near, far = parts_of_filter(value, lane)
    side = near[1:-1] + far[:-2] + far[2:]
    above = row_high[pl.ds(start, size * ROWS), :].reshape(size, ROWS, planes)
    below = row_low[pl.ds(start, size * ROWS), :].reshape(size, ROWS, planes)
    above = jnp.where(row == ROWS - 1, above, pltpu.roll(side, ROWS - 1, 1))
    below = jnp.where(row == 0, below, pltpu.roll(side, 1, 1))
    return own[1:-1] + near[:-2] + near[2:] + (above + below)


def corner_modes(value, row_high, row, lane):
    planes = value.shape[-1]
    above = jnp.where(row == ROWS - 1, row_high, pltpu.roll(value, ROWS - 1, 1))
    total, step = value + above, above - value

    def next_z(field):
        return jnp.where(lane == planes - 1, 0.0, pltpu.roll(field, planes - 1, 2))

    total_next, step_next = next_z(total), next_z(step)
    both = total + total_next
    along_z = total_next - total
    along_y = step + step_next
    along_yz = step_next - step
    return (
        both[1:] - both[:-1],
        along_y[1:] + along_y[:-1],
        along_z[1:] + along_z[:-1],
        along_y[1:] - along_y[:-1],
        along_z[1:] - along_z[:-1],
        along_yz[1:] + along_yz[:-1],
        along_yz[1:] - along_yz[:-1],
    )


def element_energy(modes):
    (ax, ay, az, axy, axz, ayz, axyz), (bx, by, bz, bxy, bxz, byz, bxyz), (
        cx,
        cy,
        cz,
        cxy,
        cxz,
        cyz,
        cxyz,
    ) = modes

    def sq(value):
        return value * value

    first = (
        (LAME_FIRST / 16.0) * sq(ax + by + cz)
        + (2.0 * SHEAR / 16.0) * (sq(ax) + sq(by) + sq(cz))
        + (SHEAR / 16.0) * (sq(ay + bx) + sq(az + cx) + sq(bz + cy))
    )
    second = (
        (LAME_FIRST / 48.0) * (sq(axy + cyz) + sq(bxy + cxz) + sq(axz + byz))
        + (3.0 * SHEAR / 48.0) * (sq(axy) + sq(axz) + sq(bxy) + sq(byz) + sq(cxz) + sq(cyz))
        + (SHEAR / 48.0) * (sq(ayz + bxz) + sq(ayz + cxy) + sq(bxz + cxy))
    )
    third = ((LAME_FIRST + 4.0 * SHEAR) / 144.0) * (sq(axyz) + sq(bxyz) + sq(cxyz))
    return first + second + third


def kernel(
    count_x,
    count_y,
    dens_hbm,
    disp_hbm,
    pas_hbm,
    new_out,
    sens_out,
    big,
    passive,
    pack_low,
    pack_high,
    row_high,
    row_low,
    spread,
    spread_pack_low,
    spread_pack_high,
    spread_row_high,
    spread_row_low,
    corner_pp,
    corner_mp,
    corner_pm,
    corner_mm,
    s_corner_pp,
    s_corner_mp,
    s_corner_pm,
    s_corner_mm,
    node_row,
    tail_high,
    tail_low,
    inverse,
    inverse_volume,
    scaled,
    lower,
    upper,
    sum_scaled,
    sum_lower,
    sum_upper,
    partial,
    totals_x,
    totals_y,
    local_sems,
    send_a,
    recv_a,
    send_b,
    recv_b,
    send_c,
    recv_c,
    send_d,
    recv_d,
):
    planes = dens_hbm.shape[-1]
    cols_x = dens_hbm.shape[0] // ROWS
    block = cols_x * ROWS
    last = cols_x * ROWS
    ix, iy = lax.axis_index("gx"), lax.axis_index("gy")
    total_x, total_y = cols_x * count_x, ROWS * count_y

    def inside(x, y):
        return (x >= 0) & (x < count_x) & (y >= 0) & (y < count_y)

    def along_x(step):
        return (lax.rem(ix + step, count_x), iy)

    def along_y(step):
        return (ix, lax.rem(iy + step, count_y))

    barrier = pltpu.get_barrier_semaphore()

    def greet(device):
        pl.semaphore_signal(barrier, inc=1, device_id=device, device_id_type=MESH)

    for step in range(1, count_x):
        greet(along_x(step))
    for step in range(1, count_y):
        greet(along_y(step))
    greetings = count_x - 1 + count_y - 1
    for dx, dy in WAYS[4:]:
        present = inside(ix + dx, iy + dy)
        greetings = greetings + jnp.where(present, 1, 0)

        @pl.when(present)
        def _(dx=dx, dy=dy):
            greet((ix + dx, iy + dy))

    loads = [
        pltpu.make_async_copy(dens_hbm, big.at[0, pl.ds(ROWS, block)], local_sems.at[0]),
        pltpu.make_async_copy(disp_hbm, big.at[pl.ds(1, 3), pl.ds(ROWS, block)], local_sems.at[1]),
        pltpu.make_async_copy(pas_hbm, passive, local_sems.at[2]),
    ]
    for load in loads:
        load.start()

    def fill(way, refs):
        @pl.when(jnp.logical_not(inside(ix - way[0], iy - way[1])))
        def _():
            for ref in refs:
                ref[...] = jnp.zeros(ref.shape, ref.dtype)

    def exchange(pairs, send, recv):
        def copy(at):
            source, target = pairs[at]
            dx, dy = WAYS[at]
            return pltpu.make_async_remote_copy(
                src_ref=source,
                dst_ref=target,
                send_sem=send.at[at],
                recv_sem=recv.at[at],
                device_id=(ix + dx, iy + dy),
                device_id_type=MESH,
            )

        def start(at):
            dx, dy = WAYS[at]

            @pl.when(inside(ix + dx, iy + dy))
            def _():
                copy(at).start()

        def arrive(at):
            dx, dy = WAYS[at]

            @pl.when(inside(ix - dx, iy - dy))
            def _():
                copy(at).wait_recv()

        def sent(at):
            dx, dy = WAYS[at]

            @pl.when(inside(ix + dx, iy + dy))
            def _():
                copy(at).wait_send()

        return start, arrive, sent

    first_tile, last_tile = pl.ds(ROWS, ROWS), pl.ds(last, ROWS)
    low_tile, high_tile = pl.ds(0, ROWS), pl.ds(last + ROWS, ROWS)
    start_a, arrive_a, sent_a = exchange(
        [
            (big.at[0, last_tile], big.at[0, low_tile]),
            (big.at[:, first_tile], big.at[:, high_tile]),
            (pack_high, row_low.at[pl.ds(0, cols_x)]),
            (pack_low, row_high.at[:, pl.ds(0, cols_x)]),
            (big.at[0, last_tile], corner_pp),
            (big.at[0, first_tile], corner_mp),
            (big.at[0, last_tile], corner_pm),
            (big.at[:, first_tile], corner_mm),
        ],
        send_a,
        recv_a,
    )
    start_b, arrive_b, sent_b = exchange(
        [
            (spread.at[last_tile], spread.at[low_tile]),
            (spread.at[first_tile], spread.at[high_tile]),
            (spread_pack_high, spread_row_low.at[pl.ds(0, cols_x)]),
            (spread_pack_low, spread_row_high.at[pl.ds(0, cols_x)]),
            (spread.at[last_tile], s_corner_pp),
            (spread.at[first_tile], s_corner_mp),
            (spread.at[last_tile], s_corner_pm),
            (spread.at[first_tile], s_corner_mm),
        ],
        send_b,
        recv_b,
    )
    fill(WAYS[0], [big.at[0, low_tile], spread.at[low_tile]])
    fill(WAYS[1], [big.at[:, high_tile], spread.at[high_tile]])
    fill(WAYS[2], [row_low.at[pl.ds(0, cols_x)], spread_row_low.at[pl.ds(0, cols_x)]])
    fill(WAYS[3], [row_high.at[:, pl.ds(0, cols_x)], spread_row_high.at[pl.ds(0, cols_x)]])
    fill(WAYS[4], [corner_pp, s_corner_pp])
    fill(WAYS[5], [corner_mp, s_corner_mp])
    fill(WAYS[6], [corner_pm, s_corner_pm])
    fill(WAYS[7], [corner_mm, s_corner_mm])

    def strided(start):
        return pl.ds(start, cols_x, stride=ROWS)

    loads[0].wait()
    pack_high[...] = big[0, strided(ROWS + ROWS - 1), :]
    pack_low[0] = big[0, strided(ROWS), :]
    loads[1].wait()
    for c in (1, 2, 3):
        pack_low[c] = big[c, strided(ROWS), :]
    pl.semaphore_wait(barrier, greetings)
    for at in (3, 1, 2, 7, 0, 4, 5, 6):
        start_a(at)

    lane = lax.broadcasted_iota(jnp.int32, (ROWS, planes), 1)
    row = lax.broadcasted_iota(jnp.int32, (ROWS, planes), 0)

    def counted(at, total):
        one, none = jnp.float32(1.0), jnp.float32(0.0)
        return jnp.where(at > 0, one, none) + jnp.where(at < total - 1, one, none)

    count_z = counted(lane, planes)
    known = {}

    def representative(x):
        return x if x in (-1, 0, cols_x - 1, cols_x) else 1

    def inverse_sums(x, offset):
        x = representative(x)
        if (x, offset) not in known:
            y = iy * ROWS + row + offset
            beside_y = counted(y, total_y)
            global_x = ix * cols_x + x
            beside_x = counted(global_x, total_x)
            sums = (
                1.5
                + 0.5 * (beside_x + beside_y + count_z)
                + EDGE_WEIGHT * (beside_x * beside_y + beside_x * count_z + beside_y * count_z)
            )
            result = 1.0 / sums
            result = jnp.where((y >= 0) & (y < total_y), result, 0.0)
            if x in (-1, cols_x):
                held = (global_x >= 0) & (global_x < total_x)
                result = result * jnp.where(held, jnp.float32(1.0), jnp.float32(0.0))
            known[x, offset] = (result, parts_of_filter(result, lane))
        return known[x, offset]

    weights = {}
    for x in range(cols_x):
        tile = pl.ds(x * ROWS, ROWS)
        inverse[tile, :] = inverse_sums(x, 0)[0]
        key = tuple(representative(x + d) for d in (-1, 0, 1))
        if key not in weights:
            volume = inverse_sums(x, 0)[1][0]
            volume = volume + inverse_sums(x - 1, 0)[1][1] + inverse_sums(x + 1, 0)[1][1]
            for offset in (-1, 1):
                volume = volume + inverse_sums(x, offset)[1][1]
                volume = volume + inverse_sums(x - 1, offset)[1][2]
                volume = volume + inverse_sums(x + 1, offset)[1][2]
            weights[key] = 1.0 / volume
        inverse_volume[tile, :] = weights[key]

    loads[2].wait()
    for at in range(8):
        arrive_a(at)

    def join(rows, first, final):
        rows[pl.ds(cols_x, ROWS), :] = jnp.where(row == 0, first, jnp.where(row == 7, final, 0.0))

    def tails(rows_high, rows_low, pp, mp, pm, mm):
        join(rows_high, mm[0:1, :], pm[0:1, :])
        join(rows_low, mp[7:8, :], pp[7:8, :])
        lane_rows = lax.broadcasted_iota(jnp.int32, (cols_x + ROWS, planes), 1)
        tail_high[strided(ROWS - 1), :] = filter_rows(rows_high[...], lane_rows, cols_x)
        tail_low[strided(0), :] = filter_rows(rows_low[...], lane_rows, cols_x)

    tails(row_high.at[0], row_low, corner_pp, corner_mp, corner_pm, corner_mm.at[0])
    for c in range(3):
        node_row[c, strided(ROWS - 1), :] = row_high[1 + c, pl.ds(0, cols_x), :]
        node_row[c, pl.ds(block + ROWS - 1, 1), :] = corner_mm[1 + c, 0:1, :]

    density = big.at[0]

    def masks(size):
        shape = (size, ROWS, planes)
        return (
            lax.broadcasted_iota(jnp.int32, shape, 1),
            lax.broadcasted_iota(jnp.int32, shape, 2),
        )

    size = 4 if cols_x % 4 == 0 else 1
    rows_here = size * ROWS
    row_s, lane_s = masks(size)
    row_1, lane_1 = masks(size + 1)
    _, lane_2 = masks(size + 2)

    def rows_of(first, count):
        start = first * ROWS
        return pl.ds(start if isinstance(start, int) else pl.multiple_of(start, ROWS), count * ROWS)

    def tiles(ref, first):
        return ref[rows_of(first, size), :].reshape(size, ROWS, planes)

    def each_group(begin, end, step, body):
        lax.fori_loop(0, (end - begin) // step, lambda i, c: (body(begin + i * step), c)[1], 0)

    def spread_group(first):
        near = rows_of(first + 1, size + 1)
        high = rows_of(first, size + 1)
        shape = (size + 1, ROWS, planes)
        modes = [
            corner_modes(
                big[1 + c, near, :].reshape(shape),
                node_row[c, high, :].reshape(shape),
                row_1,
                lane_1,
            )
            for c in range(3)
        ]
        energy = element_energy(modes)
        inv = tiles(inverse, first)
        kind = tiles(passive, first)
        physical = filter_chunk(density, first, size, tail_low, tail_high, row_s, lane_2) * inv
        physical = jnp.where(kind == 1, 1.0, jnp.where(kind == 2, 0.0, physical))
        raw = (-DERIVATIVE) * physical * physical * energy
        spread[rows_of(first + 1, size), :] = (raw * inv).reshape(rows_here, planes)

    each_group(0, cols_x, size, spread_group)

    spread_pack_high[...] = spread[strided(ROWS + ROWS - 1), :]
    spread_pack_low[...] = spread[strided(ROWS), :]
    for at in (3, 2, 1, 0, 7, 4, 5, 6):
        start_b(at)

    def limit_group(first):
        at = rows_of(first, size)
        kind = tiles(passive, first)
        held = big[0, rows_of(first + 1, size), :].reshape(size, ROWS, planes)
        fixed = jnp.where(kind == 1, 1.0, 0.0)
        low = jnp.where(kind == 0, jnp.maximum(held - MOVE_LIMIT, 0.0), fixed)
        high = jnp.where(kind == 0, jnp.minimum(held + MOVE_LIMIT, 1.0), fixed)
        lower[at, :] = low.reshape(rows_here, planes)
        upper[at, :] = high.reshape(rows_here, planes)

    each_group(0, cols_x, size, limit_group)

    def rate_of(sens, held, weight):
        return held * jnp.sqrt(-sens * weight)

    def middle_rows(value, index):
        return jnp.where((index > 0) & (index < ROWS - 1), value, 0.0)

    def plane_group(first, count, place):
        shape = (count, ROWS, planes)
        row_c = lax.broadcasted_iota(jnp.int32, shape, 1)
        lane_c = lax.broadcasted_iota(jnp.int32, (count + 2, ROWS, planes), 2)
        wide = spread[rows_of(first, count + 2), :].reshape(count + 2, ROWS, planes)
        own, near, far = parts_of_filter(wide, lane_c)
        side = near[1:-1] + far[:-2] + far[2:]
        sens = own[1:-1] + near[:-2] + near[2:]
        sens = sens + (pltpu.roll(side, ROWS - 1, 1) + pltpu.roll(side, 1, 1))
        at = rows_of(first, count)
        held = big[0, rows_of(first + 1, count), :].reshape(shape)
        sens = middle_rows(sens, row_c)
        rate = rate_of(sens, held, inverse_volume[at, :].reshape(shape))
        sens_out[at, :] = sens.reshape(count * ROWS, planes)
        scaled[at, :] = rate.reshape(count * ROWS, planes)
        to = rows_of(place, count)
        sum_scaled[to, :] = rate.reshape(count * ROWS, planes)
        for source, target in ((lower, sum_lower), (upper, sum_upper)):
            kept = middle_rows(source[at, :].reshape(shape), row_c)
            target[to, :] = kept.reshape(count * ROWS, planes)

    slots = 2**BISECT
    group = 16
    spacing = 2.0 * BRACKET / slots
    scales = jnp.concatenate(
        [jnp.full((1, ROWS, planes), math.exp(-0.5 * spacing * j), jnp.float32) for j in range(group)]
    )

    def add_volumes(first_tile, end_tile, fresh):
        def volumes(i, carry):
            begin = (-BRACKET) + (spacing * group) * i.astype(jnp.float32)
            factors = scales * jnp.exp(jnp.full((ROWS, planes), -0.5 * begin, jnp.float32))[None]
            at = pl.ds(pl.multiple_of(i * (group * ROWS), group * ROWS), group * ROWS)
            if fresh:
                total = jnp.zeros((group, ROWS, planes), jnp.float32)
            else:
                total = partial[at, :].reshape(group, ROWS, planes)
            for x in range(first_tile, end_tile):
                tile = pl.ds(x * ROWS, ROWS)
                moved = jnp.maximum(sum_scaled[tile, :][None] * factors, sum_lower[tile, :][None])
                total = total + jnp.minimum(moved, sum_upper[tile, :][None])
            partial[at, :] = total.reshape(group * ROWS, planes)
            return carry

        lax.fori_loop(0, slots // group, volumes, 0)

    inner = cols_x - 2
    per_pass = max(d for d in range(1, 8) if inner % d == 0)
    each_group(1, 1 + inner, per_pass, lambda first: plane_group(first, per_pass, first - 1))
    add_volumes(0, inner, True)

    for at in range(8):
        arrive_b(at)
    plane_group(0, 1, inner)
    plane_group(cols_x - 1, 1, inner + 1)
    join(spread_row_high, s_corner_mm[0:1, :], s_corner_pm[0:1, :])
    join(spread_row_low, s_corner_mp[7:8, :], s_corner_pp[7:8, :])
    lane_p = lax.broadcasted_iota(jnp.int32, (cols_x + ROWS, planes), 1)

    def packed_row(r):
        above = spread[pl.ds(last + ROWS + r, 1), :]
        below = spread[pl.ds(r, 1), :]
        tail = jnp.where(row == 0, above, jnp.where(row == ROWS - 1, below, 0.0))
        return jnp.concatenate([spread[strided(ROWS + r), :], tail], axis=0)

    def edge_row(r, beyond, next_row, held, place):
        own, near, _ = parts_of_filter(packed_row(r), lane_p)
        count = own.shape[0]
        sens = (own + pltpu.roll(near, 1, 0) + pltpu.roll(near, count - 1, 0))[:cols_x]
        sens = sens + filter_rows(beyond, lane_p, cols_x)
        sens = sens + filter_rows(packed_row(next_row), lane_p, cols_x)
        rate = rate_of(sens, held, inverse_volume[strided(r), :])
        sens_out[strided(r), :] = sens
        scaled[strided(r), :] = rate
        to = pl.ds(place * ROWS, cols_x)
        sum_scaled[to, :] = rate
        sum_lower[to, :] = lower[strided(r), :]
        sum_upper[to, :] = upper[strided(r), :]

    edge_row(0, spread_row_low[...], 1, pack_low[0], inner + 2)
    edge_row(ROWS - 1, spread_row_high[...], ROWS - 2, pack_high[...], inner + 2 + cols_x // ROWS)
    add_volumes(inner, inner + 2 + 2 * (cols_x // ROWS), False)
    halves = slots // planes
    for half in range(halves):
        start = half * planes * ROWS
        lines = partial[pl.ds(start, planes, stride=ROWS), :]
        for s in range(1, ROWS):
            lines = lines + partial[pl.ds(start + s, planes, stride=ROWS), :]
        totals_x[ix, half : half + 1, :] = jnp.sum(lines.T, axis=0, keepdims=True)

    def shared(totals, me, target, count, send, recv):
        for step in range(1, count):
            pltpu.make_async_remote_copy(
                src_ref=totals.at[me],
                dst_ref=totals.at[me],
                send_sem=send,
                recv_sem=recv,
                device_id=target(step),
                device_id_type=MESH,
            ).start()
        others = totals.at[pl.ds(0, count - 1)]
        pltpu.make_async_copy(others, others, recv).wait()
        return jnp.sum(totals[...], axis=0), others

    column, sent_x = shared(totals_x, ix, along_x, count_x, send_c, recv_c)
    totals_y[iy] = column
    volume, sent_y = shared(totals_y, iy, along_y, count_y, send_d, recv_d)
    label = lax.broadcasted_iota(jnp.int32, volume.shape, 0) * planes + lax.broadcasted_iota(
        jnp.int32, volume.shape, 1
    )
    target = VOLUME_SHARE * total_x * total_y * planes
    over = jnp.where((label > 0) & (volume > target), 1.0, 0.0)
    reached = jnp.sum(jnp.sum(over, axis=0, keepdims=True), axis=1, keepdims=True)
    middle = (-BRACKET) + spacing * (jnp.broadcast_to(reached, (ROWS, planes)) + 0.5)
    factor = jnp.exp(-0.5 * middle)[None]
    def final_group(first):
        at = rows_of(first, size)
        moved = jnp.maximum(tiles(scaled, first) * factor, tiles(lower, first))
        new_out[at, :] = jnp.minimum(moved, tiles(upper, first)).reshape(rows_here, planes)
    each_group(0, cols_x, size, final_group)
    for at in range(8):
        sent_a(at)
        sent_b(at)
    pltpu.make_async_copy(sent_x, sent_x, send_c).wait()
    pltpu.make_async_copy(sent_y, sent_y, send_d).wait()


def hand_over(new_held, sens_held, new_hbm, sens_hbm, sems):
    copies = [
        pltpu.make_async_copy(new_held, new_hbm, sems.at[0]),
        pltpu.make_async_copy(sens_held, sens_hbm, sems.at[1]),
    ]
    for copy in copies:
        copy.start()
    for copy in copies:
        copy.wait()


def per_device(count_x, count_y, density, displacement, passive):
    cols_x, cols_y, planes = density.shape
    assert cols_y == ROWS and cols_x % ROWS == 0 and planes == 128
    block = cols_x * ROWS
    slots = 2**BISECT

    def buffer(*shape):
        return pltpu.VMEM(shape, jnp.float32)

    field = buffer(block, planes)
    tile = buffer(ROWS, planes)
    wide = buffer(block + 2 * ROWS, planes)
    rows = buffer(cols_x, planes)
    sums = buffer(block + 2 * cols_x, planes)
    ring = buffer(cols_x + ROWS, planes)
    held = functools.partial(pltpu.with_memory_space_constraint, memory_space=pltpu.HBM)
    anywhere = pl.BlockSpec(memory_space=pl.ANY)
    out = jax.ShapeDtypeStruct((block, planes), jnp.float32)
    new_density, sensitivity = pl.pallas_call(
        functools.partial(kernel, count_x, count_y),
        out_shape=(out, out),
        in_specs=[anywhere] * 3,
        out_specs=[pl.BlockSpec(memory_space=pltpu.VMEM)] * 2,
        scratch_shapes=[
            buffer(4, block + 2 * ROWS, planes),
            pltpu.VMEM((block, planes), jnp.int32),
            buffer(4, cols_x, planes),
            rows,
            buffer(4, cols_x + ROWS, planes),
            ring,
            wide,
            rows,
            rows,
            ring,
            ring,
            tile,
            tile,
            tile,
            buffer(4, ROWS, planes),
            tile,
            tile,
            tile,
            tile,
            buffer(3, block + ROWS, planes),
            field,
            field,
            field,
            field,
            field,
            field,
            field,
            sums,
            sums,
            sums,
            buffer(slots * ROWS, planes),
            buffer(count_x, slots // planes, planes),
            buffer(count_y, slots // planes, planes),
            pltpu.SemaphoreType.DMA((3,)),
            pltpu.SemaphoreType.DMA((8,)),
            pltpu.SemaphoreType.DMA((8,)),
            pltpu.SemaphoreType.DMA((8,)),
            pltpu.SemaphoreType.DMA((8,)),
            pltpu.SemaphoreType.DMA,
            pltpu.SemaphoreType.DMA,
            pltpu.SemaphoreType.DMA,
            pltpu.SemaphoreType.DMA,
        ],
        compiler_params=pltpu.CompilerParams(
            collective_id=0, has_side_effects=True, vmem_limit_bytes=16 * 1024 * 1024
        ),
    )(
        held(density.reshape(block, planes)),
        held(displacement.reshape(3, block, planes)),
        held(passive.reshape(block, planes)),
    )
    new_density, sensitivity = pl.pallas_call(
        hand_over,
        out_shape=(out, out),
        in_specs=[anywhere] * 2,
        out_specs=[anywhere] * 2,
        scratch_shapes=[pltpu.SemaphoreType.DMA((2,))],
    )(new_density, sensitivity)
    return (new_density.reshape(density.shape), sensitivity.reshape(density.shape))


def solution(mesh):
    return jax.shard_map(
        functools.partial(per_device, mesh.shape["gx"], mesh.shape["gy"]),
        mesh=mesh,
        in_specs=(P("gx", "gy", None), P(None, "gx", "gy", None), P("gx", "gy", None)),
        out_specs=(P("gx", "gy", None), P("gx", "gy", None)),
        check_vma=False,
    )
```

```python
import functools
import math

import jax
import jax.numpy as jnp
from jax import lax
from jax.experimental import pallas as pl
from jax.experimental.pallas import tpu as pltpu
from jax.sharding import PartitionSpec as P

BISECT = 8
BRACKET = 8.0
MOVE_LIMIT = 0.2
VOLUME_SHARE = 0.35
DERIVATIVE = 3.0 * (1.0 - 1e-09)
EDGE_WEIGHT = 1.5 - math.sqrt(2.0)
POISSON = 0.3
LAME_FIRST = POISSON / ((1.0 + POISSON) * (1.0 - 2.0 * POISSON))
SHEAR = 0.5 / (1.0 + POISSON)
ROWS = 8
MESH = pl.DeviceIdType.MESH
WAYS = [(1, 0), (-1, 0), (0, 1), (0, -1), (1, 1), (-1, 1), (1, -1), (-1, -1)]


def z_neighbours(value, lane):
    planes = value.shape[-1]
    axis = value.ndim - 1
    above = jnp.where(lane == planes - 1, 0.0, pltpu.roll(value, planes - 1, axis))
    below = jnp.where(lane == 0, 0.0, pltpu.roll(value, 1, axis))
    return above + below


def parts_of_filter(value, lane):
    beside = z_neighbours(value, lane)
    return (
        1.5 * value + 0.5 * beside,
        0.5 * value + EDGE_WEIGHT * beside,
        EDGE_WEIGHT * value,
    )


def filter_rows(packed, lane, cols_x):
    _, near, far = parts_of_filter(packed, lane)
    count = packed.shape[0]
    return (near + pltpu.roll(far, 1, 0) + pltpu.roll(far, count - 1, 0))[:cols_x]


def filter_chunk(field, first, size, row_low, row_high, row, lane):
    planes = field.shape[-1]
    value = field[pl.ds(first * ROWS, (size + 2) * ROWS), :].reshape(size + 2, ROWS, planes)
    own, near, far = parts_of_filter(value, lane)
    side = near[1:-1] + far[:-2] + far[2:]
    above = row_high[pl.ds(first * ROWS, size * ROWS), :].reshape(size, ROWS, planes)
    below = row_low[pl.ds(first * ROWS, size * ROWS), :].reshape(size, ROWS, planes)
    above = jnp.where(row == ROWS - 1, above, pltpu.roll(side, ROWS - 1, 1))
    below = jnp.where(row == 0, below, pltpu.roll(side, 1, 1))
    return own[1:-1] + near[:-2] + near[2:] + (above + below)


def corner_modes(value, row_high, row, lane):
    planes = value.shape[-1]
    above = jnp.where(row == ROWS - 1, row_high, pltpu.roll(value, ROWS - 1, 1))
    total, step = value + above, above - value

    def next_z(field):
        return jnp.where(lane == planes - 1, 0.0, pltpu.roll(field, planes - 1, 2))

    total_next, step_next = next_z(total), next_z(step)
    both = total + total_next
    along_z = total_next - total
    along_y = step + step_next
    along_yz = step_next - step
    return (
        both[1:] - both[:-1],
        along_y[1:] + along_y[:-1],
        along_z[1:] + along_z[:-1],
        along_y[1:] - along_y[:-1],
        along_z[1:] - along_z[:-1],
        along_yz[1:] + along_yz[:-1],
        along_yz[1:] - along_yz[:-1],
    )


def element_energy(modes):
    (ax, ay, az, axy, axz, ayz, axyz), (bx, by, bz, bxy, bxz, byz, bxyz), (
        cx,
        cy,
        cz,
        cxy,
        cxz,
        cyz,
        cxyz,
    ) = modes

    def sq(value):
        return value * value

    first = (
        (LAME_FIRST / 16.0) * sq(ax + by + cz)
        + (2.0 * SHEAR / 16.0) * (sq(ax) + sq(by) + sq(cz))
        + (SHEAR / 16.0) * (sq(ay + bx) + sq(az + cx) + sq(bz + cy))
    )
    second = (
        (LAME_FIRST / 48.0) * (sq(axy + cyz) + sq(bxy + cxz) + sq(axz + byz))
        + (3.0 * SHEAR / 48.0) * (sq(axy) + sq(axz) + sq(bxy) + sq(byz) + sq(cxz) + sq(cyz))
        + (SHEAR / 48.0) * (sq(ayz + bxz) + sq(ayz + cxy) + sq(bxz + cxy))
    )
    third = ((LAME_FIRST + 4.0 * SHEAR) / 144.0) * (sq(axyz) + sq(bxyz) + sq(cxyz))
    return first + second + third


def peers(count, body):
    if count <= 64:
        for step in range(1, count):
            body(step)
    else:
        lax.fori_loop(1, count, lambda step, carry: (body(step), carry)[1], 0)


def kernel(
    count_x,
    count_y,
    dens_hbm,
    disp_hbm,
    pas_hbm,
    new_out,
    sens_out,
    big,
    passive,
    pack_low,
    pack_high,
    row_high,
    row_low,
    spread,
    spread_pack_low,
    spread_pack_high,
    spread_row_high,
    spread_row_low,
    corner_pp,
    corner_mp,
    corner_pm,
    corner_mm,
    s_corner_pp,
    s_corner_mp,
    s_corner_pm,
    s_corner_mm,
    node_row,
    tail_high,
    tail_low,
    inverse,
    inverse_volume,
    scaled,
    lower,
    upper,
    sum_scaled,
    sum_lower,
    sum_upper,
    partial,
    totals,
    local_sems,
    send_a,
    recv_a,
    send_b,
    recv_b,
    send_c,
    recv_c,
):
    planes = dens_hbm.shape[-1]
    cols_x = dens_hbm.shape[0] // ROWS
    block = cols_x * ROWS
    last = cols_x * ROWS
    ix, iy = lax.axis_index("gx"), lax.axis_index("gy")
    total_x, total_y = cols_x * count_x, ROWS * count_y

    def inside(x, y):
        return (x >= 0) & (x < count_x) & (y >= 0) & (y < count_y)

    loads = [
        pltpu.make_async_copy(dens_hbm, big.at[0, pl.ds(ROWS, block)], local_sems.at[0]),
        pltpu.make_async_copy(disp_hbm, big.at[pl.ds(1, 3), pl.ds(ROWS, block)], local_sems.at[1]),
        pltpu.make_async_copy(pas_hbm, passive, local_sems.at[2]),
    ]
    for load in loads:
        load.start()

    devices = count_x * count_y

    def peer(step):
        return (lax.rem(ix + step // count_y, count_x), lax.rem(iy + step % count_y, count_y))

    barrier = pltpu.get_barrier_semaphore()
    peers(
        devices,
        lambda step: pl.semaphore_signal(
            barrier, inc=1, device_id=peer(step), device_id_type=MESH
        ),
    )

    def fill(way, refs):
        @pl.when(jnp.logical_not(inside(ix - way[0], iy - way[1])))
        def _():
            for ref in refs:
                ref[...] = jnp.zeros(ref.shape, ref.dtype)

    def exchange(pairs, send, recv):
        def copy(at):
            source, target = pairs[at]
            dx, dy = WAYS[at]
            return pltpu.make_async_remote_copy(
                src_ref=source,
                dst_ref=target,
                send_sem=send.at[at],
                recv_sem=recv.at[at],
                device_id=(ix + dx, iy + dy),
                device_id_type=MESH,
            )

        def start(at):
            dx, dy = WAYS[at]

            @pl.when(inside(ix + dx, iy + dy))
            def _():
                copy(at).start()

        def arrive(at):
            dx, dy = WAYS[at]

            @pl.when(inside(ix - dx, iy - dy))
            def _():
                copy(at).wait_recv()

        def sent(at):
            dx, dy = WAYS[at]

            @pl.when(inside(ix + dx, iy + dy))
            def _():
                copy(at).wait_send()

        return start, arrive, sent

    first_tile, last_tile = pl.ds(ROWS, ROWS), pl.ds(last, ROWS)
    low_tile, high_tile = pl.ds(0, ROWS), pl.ds(last + ROWS, ROWS)
    start_a, arrive_a, sent_a = exchange(
        [
            (big.at[0, last_tile], big.at[0, low_tile]),
            (big.at[:, first_tile], big.at[:, high_tile]),
            (pack_high, row_low.at[pl.ds(0, cols_x)]),
            (pack_low, row_high.at[:, pl.ds(0, cols_x)]),
            (big.at[0, last_tile], corner_pp),
            (big.at[0, first_tile], corner_mp),
            (big.at[0, last_tile], corner_pm),
            (big.at[:, first_tile], corner_mm),
        ],
        send_a,
        recv_a,
    )
    start_b, arrive_b, sent_b = exchange(
        [
            (spread.at[last_tile], spread.at[low_tile]),
            (spread.at[first_tile], spread.at[high_tile]),
            (spread_pack_high, spread_row_low.at[pl.ds(0, cols_x)]),
            (spread_pack_low, spread_row_high.at[pl.ds(0, cols_x)]),
            (spread.at[last_tile], s_corner_pp),
            (spread.at[first_tile], s_corner_mp),
            (spread.at[last_tile], s_corner_pm),
            (spread.at[first_tile], s_corner_mm),
        ],
        send_b,
        recv_b,
    )
    fill(WAYS[0], [big.at[0, low_tile], spread.at[low_tile]])
    fill(WAYS[1], [big.at[:, high_tile], spread.at[high_tile]])
    fill(WAYS[2], [row_low.at[pl.ds(0, cols_x)], spread_row_low.at[pl.ds(0, cols_x)]])
    fill(WAYS[3], [row_high.at[:, pl.ds(0, cols_x)], spread_row_high.at[pl.ds(0, cols_x)]])
    fill(WAYS[4], [corner_pp, s_corner_pp])
    fill(WAYS[5], [corner_mp, s_corner_mp])
    fill(WAYS[6], [corner_pm, s_corner_pm])
    fill(WAYS[7], [corner_mm, s_corner_mm])

    def strided(start):
        return pl.ds(start, cols_x, stride=ROWS)

    loads[0].wait()
    pack_high[...] = big[0, strided(ROWS + ROWS - 1), :]
    pack_low[0] = big[0, strided(ROWS), :]
    loads[1].wait()
    for c in (1, 2, 3):
        pack_low[c] = big[c, strided(ROWS), :]
    pl.semaphore_wait(barrier, devices - 1)
    for at in (3, 1, 2, 7, 0, 4, 5, 6):
        start_a(at)

    lane = lax.broadcasted_iota(jnp.int32, (ROWS, planes), 1)
    row = lax.broadcasted_iota(jnp.int32, (ROWS, planes), 0)

    def counted(at, total):
        one, none = jnp.float32(1.0), jnp.float32(0.0)
        return jnp.where(at > 0, one, none) + jnp.where(at < total - 1, one, none)

    count_z = counted(lane, planes)
    known = {}

    def representative(x):
        return x if x in (-1, 0, cols_x - 1, cols_x) else 1

    def inverse_sums(x, offset):
        x = representative(x)
        if (x, offset) not in known:
            y = iy * ROWS + row + offset
            beside_y = counted(y, total_y)
            global_x = ix * cols_x + x
            beside_x = counted(global_x, total_x)
            sums = (
                1.5
                + 0.5 * (beside_x + beside_y + count_z)
                + EDGE_WEIGHT * (beside_x * beside_y + beside_x * count_z + beside_y * count_z)
            )
            result = 1.0 / sums
            result = jnp.where((y >= 0) & (y < total_y), result, 0.0)
            if x in (-1, cols_x):
                held = (global_x >= 0) & (global_x < total_x)
                result = result * jnp.where(held, jnp.float32(1.0), jnp.float32(0.0))
            known[x, offset] = (result, parts_of_filter(result, lane))
        return known[x, offset]

    weights = {}
    for x in range(cols_x):
        tile = pl.ds(x * ROWS, ROWS)
        inverse[tile, :] = inverse_sums(x, 0)[0]
        key = tuple(representative(x + d) for d in (-1, 0, 1))
        if key not in weights:
            volume = inverse_sums(x, 0)[1][0]
            volume = volume + inverse_sums(x - 1, 0)[1][1] + inverse_sums(x + 1, 0)[1][1]
            for offset in (-1, 1):
                volume = volume + inverse_sums(x, offset)[1][1]
                volume = volume + inverse_sums(x - 1, offset)[1][2]
                volume = volume + inverse_sums(x + 1, offset)[1][2]
            weights[key] = 1.0 / volume
        inverse_volume[tile, :] = weights[key]

    def masks(size):
        shape = (size, ROWS, planes)
        return (
            lax.broadcasted_iota(jnp.int32, shape, 1),
            lax.broadcasted_iota(jnp.int32, shape, 2),
        )

    size = 4 if cols_x % 4 == 0 else 1
    rows_here = size * ROWS
    row_s, lane_s = masks(size)
    row_1, lane_1 = masks(size + 1)
    _, lane_2 = masks(size + 2)

    def tiles(ref, first):
        return ref[pl.ds(first * ROWS, rows_here), :].reshape(size, ROWS, planes)

    loads[2].wait()
    for first in range(0, cols_x, size):
        at = pl.ds(first * ROWS, rows_here)
        kind = tiles(passive, first)
        held = big[0, pl.ds((first + 1) * ROWS, rows_here), :].reshape(size, ROWS, planes)
        fixed = jnp.where(kind == 1, 1.0, 0.0)
        low = jnp.where(kind == 0, jnp.maximum(held - MOVE_LIMIT, 0.0), fixed)
        high = jnp.where(kind == 0, jnp.minimum(held + MOVE_LIMIT, 1.0), fixed)
        lower[at, :] = low.reshape(rows_here, planes)
        upper[at, :] = high.reshape(rows_here, planes)

    for at in range(8):
        arrive_a(at)

    def join(rows, first, final):
        rows[pl.ds(cols_x, ROWS), :] = jnp.where(row == 0, first, jnp.where(row == 7, final, 0.0))

    def tails(rows_high, rows_low, pp, mp, pm, mm):
        join(rows_high, mm[0:1, :], pm[0:1, :])
        join(rows_low, mp[7:8, :], pp[7:8, :])
        lane_rows = lax.broadcasted_iota(jnp.int32, (cols_x + ROWS, planes), 1)
        tail_high[strided(ROWS - 1), :] = filter_rows(rows_high[...], lane_rows, cols_x)
        tail_low[strided(0), :] = filter_rows(rows_low[...], lane_rows, cols_x)

    tails(row_high.at[0], row_low, corner_pp, corner_mp, corner_pm, corner_mm.at[0])
    for c in range(3):
        node_row[c, strided(ROWS - 1), :] = row_high[1 + c, pl.ds(0, cols_x), :]
        node_row[c, pl.ds(block + ROWS - 1, 1), :] = corner_mm[1 + c, 0:1, :]

    density = big.at[0]

    for first in range(0, cols_x, size):
        near = pl.ds((first + 1) * ROWS, (size + 1) * ROWS)
        high = pl.ds(first * ROWS, (size + 1) * ROWS)
        shape = (size + 1, ROWS, planes)
        modes = [
            corner_modes(
                big[1 + c, near, :].reshape(shape),
                node_row[c, high, :].reshape(shape),
                row_1,
                lane_1,
            )
            for c in range(3)
        ]
        energy = element_energy(modes)
        inv = tiles(inverse, first)
        kind = tiles(passive, first)
        physical = filter_chunk(density, first, size, tail_low, tail_high, row_s, lane_2) * inv
        physical = jnp.where(kind == 1, 1.0, jnp.where(kind == 2, 0.0, physical))
        raw = (-DERIVATIVE) * physical * physical * energy
        spread[pl.ds((first + 1) * ROWS, rows_here), :] = (raw * inv).reshape(rows_here, planes)

    spread_pack_high[...] = spread[strided(ROWS + ROWS - 1), :]
    spread_pack_low[...] = spread[strided(ROWS), :]
    for at in (3, 2, 1, 0, 7, 4, 5, 6):
        start_b(at)

    def rate_of(sens, held, weight):
        return held * jnp.sqrt(-sens * weight)

    def middle_rows(value, index):
        return jnp.where((index > 0) & (index < ROWS - 1), value, 0.0)

    def plane_group(first, count, place):
        shape = (count, ROWS, planes)
        row_c = lax.broadcasted_iota(jnp.int32, shape, 1)
        lane_c = lax.broadcasted_iota(jnp.int32, (count + 2, ROWS, planes), 2)
        wide = spread[pl.ds(first * ROWS, (count + 2) * ROWS), :].reshape(count + 2, ROWS, planes)
        own, near, far = parts_of_filter(wide, lane_c)
        side = near[1:-1] + far[:-2] + far[2:]
        sens = own[1:-1] + near[:-2] + near[2:]
        sens = sens + (pltpu.roll(side, ROWS - 1, 1) + pltpu.roll(side, 1, 1))
        at = pl.ds(first * ROWS, count * ROWS)
        held = big[0, pl.ds((first + 1) * ROWS, count * ROWS), :].reshape(shape)
        sens = middle_rows(sens, row_c)
        rate = rate_of(sens, held, inverse_volume[at, :].reshape(shape))
        sens_out[at, :] = sens.reshape(count * ROWS, planes)
        scaled[at, :] = rate.reshape(count * ROWS, planes)
        to = pl.ds(place * ROWS, count * ROWS)
        sum_scaled[to, :] = rate.reshape(count * ROWS, planes)
        for source, target in ((lower, sum_lower), (upper, sum_upper)):
            kept = middle_rows(source[at, :].reshape(shape), row_c)
            target[to, :] = kept.reshape(count * ROWS, planes)

    slots = 2**BISECT
    group = 16
    spacing = 2.0 * BRACKET / slots
    scales = jnp.concatenate(
        [jnp.full((1, ROWS, planes), math.exp(-0.5 * spacing * j), jnp.float32) for j in range(group)]
    )

    def add_volumes(first_tile, end_tile, fresh):
        def volumes(i, carry):
            begin = (-BRACKET) + (spacing * group) * i.astype(jnp.float32)
            factors = scales * jnp.exp(jnp.full((ROWS, planes), -0.5 * begin, jnp.float32))[None]
            at = pl.ds(pl.multiple_of(i * (group * ROWS), group * ROWS), group * ROWS)
            if fresh:
                total = jnp.zeros((group, ROWS, planes), jnp.float32)
            else:
                total = partial[at, :].reshape(group, ROWS, planes)
            for x in range(first_tile, end_tile):
                tile = pl.ds(x * ROWS, ROWS)
                moved = jnp.maximum(sum_scaled[tile, :][None] * factors, sum_lower[tile, :][None])
                total = total + jnp.minimum(moved, sum_upper[tile, :][None])
            partial[at, :] = total.reshape(group * ROWS, planes)
            return carry

        lax.fori_loop(0, slots // group, volumes, 0)

    inner = cols_x - 2
    for first in range(1, 1 + inner, size):
        plane_group(first, min(size, 1 + inner - first), first - 1)
    add_volumes(0, inner, True)

    for at in range(8):
        arrive_b(at)
    plane_group(0, 1, inner)
    plane_group(cols_x - 1, 1, inner + 1)
    join(spread_row_high, s_corner_mm[0:1, :], s_corner_pm[0:1, :])
    join(spread_row_low, s_corner_mp[7:8, :], s_corner_pp[7:8, :])
    lane_p = lax.broadcasted_iota(jnp.int32, (cols_x + ROWS, planes), 1)

    def packed_row(r):
        above = spread[pl.ds(last + ROWS + r, 1), :]
        below = spread[pl.ds(r, 1), :]
        tail = jnp.where(row == 0, above, jnp.where(row == ROWS - 1, below, 0.0))
        return jnp.concatenate([spread[strided(ROWS + r), :], tail], axis=0)

    def edge_row(r, beyond, next_row, held, place):
        own, near, _ = parts_of_filter(packed_row(r), lane_p)
        count = own.shape[0]
        sens = (own + pltpu.roll(near, 1, 0) + pltpu.roll(near, count - 1, 0))[:cols_x]
        sens = sens + filter_rows(beyond, lane_p, cols_x)
        sens = sens + filter_rows(packed_row(next_row), lane_p, cols_x)
        rate = rate_of(sens, held, inverse_volume[strided(r), :])
        sens_out[strided(r), :] = sens
        scaled[strided(r), :] = rate
        to = pl.ds(place * ROWS, cols_x)
        sum_scaled[to, :] = rate
        sum_lower[to, :] = lower[strided(r), :]
        sum_upper[to, :] = upper[strided(r), :]

    edge_row(0, spread_row_low[...], 1, pack_low[0], inner + 2)
    edge_row(ROWS - 1, spread_row_high[...], ROWS - 2, pack_high[...], inner + 2 + cols_x // ROWS)
    add_volumes(inner, inner + 2 + 2 * (cols_x // ROWS), False)
    me = ix * count_y + iy
    halves = slots // planes
    for half in range(halves):
        start = half * planes * ROWS
        lines = partial[pl.ds(start, planes, stride=ROWS), :]
        for s in range(1, ROWS):
            lines = lines + partial[pl.ds(start + s, planes, stride=ROWS), :]
        totals[me, half : half + 1, :] = jnp.sum(lines.T, axis=0, keepdims=True)

    def share(step):
        pltpu.make_async_remote_copy(
            src_ref=totals.at[me],
            dst_ref=totals.at[me],
            send_sem=send_c,
            recv_sem=recv_c,
            device_id=peer(step),
            device_id_type=MESH,
        ).start()

    peers(devices, share)
    others = totals.at[pl.ds(0, devices - 1)]
    pltpu.make_async_copy(others, others, recv_c).wait()
    volume = jnp.sum(totals[...], axis=0)
    label = lax.broadcasted_iota(jnp.int32, volume.shape, 0) * planes + lax.broadcasted_iota(
        jnp.int32, volume.shape, 1
    )
    target = VOLUME_SHARE * total_x * total_y * planes
    over = jnp.where((label > 0) & (volume > target), 1.0, 0.0)
    reached = jnp.sum(jnp.sum(over, axis=0, keepdims=True), axis=1, keepdims=True)
    middle = (-BRACKET) + spacing * (jnp.broadcast_to(reached, (ROWS, planes)) + 0.5)
    factor = jnp.exp(-0.5 * middle)[None]
    for first in range(0, cols_x, size):
        at = pl.ds(first * ROWS, rows_here)
        moved = jnp.maximum(tiles(scaled, first) * factor, tiles(lower, first))
        new_out[at, :] = jnp.minimum(moved, tiles(upper, first)).reshape(rows_here, planes)
    for at in range(8):
        sent_a(at)
        sent_b(at)
    pltpu.make_async_copy(others, others, send_c).wait()


def per_device(count_x, count_y, density, displacement, passive):
    cols_x, cols_y, planes = density.shape
    assert cols_y == ROWS and cols_x % ROWS == 0 and planes == 128
    block = cols_x * ROWS
    slots = 2**BISECT

    def buffer(*shape):
        return pltpu.VMEM(shape, jnp.float32)

    field = buffer(block, planes)
    tile = buffer(ROWS, planes)
    wide = buffer(block + 2 * ROWS, planes)
    rows = buffer(cols_x, planes)
    sums = buffer(block + 2 * cols_x, planes)
    ring = buffer(cols_x + ROWS, planes)
    held = functools.partial(pltpu.with_memory_space_constraint, memory_space=pltpu.HBM)
    anywhere = pl.BlockSpec(memory_space=pl.ANY)
    out = jax.ShapeDtypeStruct((block, planes), jnp.float32)
    new_density, sensitivity = pl.pallas_call(
        functools.partial(kernel, count_x, count_y),
        out_shape=(out, out),
        in_specs=[anywhere] * 3,
        out_specs=[pl.BlockSpec(memory_space=pltpu.VMEM)] * 2,
        scratch_shapes=[
            buffer(4, block + 2 * ROWS, planes),
            pltpu.VMEM((block, planes), jnp.int32),
            buffer(4, cols_x, planes),
            rows,
            buffer(4, cols_x + ROWS, planes),
            ring,
            wide,
            rows,
            rows,
            ring,
            ring,
            tile,
            tile,
            tile,
            buffer(4, ROWS, planes),
            tile,
            tile,
            tile,
            tile,
            buffer(3, block + ROWS, planes),
            field,
            field,
            field,
            field,
            field,
            field,
            field,
            sums,
            sums,
            sums,
            buffer(slots * ROWS, planes),
            buffer(count_x * count_y, slots // planes, planes),
            pltpu.SemaphoreType.DMA((3,)),
            pltpu.SemaphoreType.DMA((8,)),
            pltpu.SemaphoreType.DMA((8,)),
            pltpu.SemaphoreType.DMA((8,)),
            pltpu.SemaphoreType.DMA((8,)),
            pltpu.SemaphoreType.DMA,
            pltpu.SemaphoreType.DMA,
        ],
        compiler_params=pltpu.CompilerParams(
            collective_id=0, has_side_effects=True, vmem_limit_bytes=16 * 1024 * 1024
        ),
    )(
        held(density.reshape(block, planes)),
        held(displacement.reshape(3, block, planes)),
        held(passive.reshape(block, planes)),
    )
    return (new_density.reshape(density.shape), sensitivity.reshape(density.shape))


def solution(mesh):
    return jax.shard_map(
        functools.partial(per_device, mesh.shape["gx"], mesh.shape["gy"]),
        mesh=mesh,
        in_specs=(P("gx", "gy", None), P(None, "gx", "gy", None), P("gx", "gy", None)),
        out_specs=(P("gx", "gy", None), P("gx", "gy", None)),
        check_vma=False,
    )
```

```python
import functools
import math

import jax
import jax.numpy as jnp
from jax import lax
from jax.experimental import pallas as pl
from jax.experimental.pallas import tpu as pltpu
from jax.sharding import PartitionSpec as P

BISECT = 8
BRACKET = 8.0
MOVE_LIMIT = 0.2
VOLUME_SHARE = 0.35
DERIVATIVE = 3.0 * (1.0 - 1e-09)
EDGE_WEIGHT = 1.5 - math.sqrt(2.0)
POISSON = 0.3
LAME_FIRST = POISSON / ((1.0 + POISSON) * (1.0 - 2.0 * POISSON))
SHEAR = 0.5 / (1.0 + POISSON)
ROWS = 8
MESH = pl.DeviceIdType.MESH
WAYS = [(1, 0), (-1, 0), (0, 1), (0, -1), (1, 1), (-1, 1), (1, -1), (-1, -1)]


def z_neighbours(value, lane):
    planes = value.shape[-1]
    axis = value.ndim - 1
    above = jnp.where(lane == planes - 1, 0.0, pltpu.roll(value, planes - 1, axis))
    below = jnp.where(lane == 0, 0.0, pltpu.roll(value, 1, axis))
    return above + below


def parts_of_filter(value, lane):
    beside = z_neighbours(value, lane)
    return (
        1.5 * value + 0.5 * beside,
        0.5 * value + EDGE_WEIGHT * beside,
        EDGE_WEIGHT * value,
    )


def filter_rows(packed, lane, cols_x):
    _, near, far = parts_of_filter(packed, lane)
    count = packed.shape[0]
    return (near + pltpu.roll(far, 1, 0) + pltpu.roll(far, count - 1, 0))[:cols_x]


def filter_chunk(field, first, size, row_low, row_high, row, lane):
    planes = field.shape[-1]
    value = field[pl.ds(first * ROWS, (size + 2) * ROWS), :].reshape(size + 2, ROWS, planes)
    own, near, far = parts_of_filter(value, lane)
    side = near[1:-1] + far[:-2] + far[2:]
    above = row_high[pl.ds(first * ROWS, size * ROWS), :].reshape(size, ROWS, planes)
    below = row_low[pl.ds(first * ROWS, size * ROWS), :].reshape(size, ROWS, planes)
    above = jnp.where(row == ROWS - 1, above, pltpu.roll(side, ROWS - 1, 1))
    below = jnp.where(row == 0, below, pltpu.roll(side, 1, 1))
    return own[1:-1] + near[:-2] + near[2:] + (above + below)


def corner_modes(value, row_high, row, lane):
    planes = value.shape[-1]
    above = jnp.where(row == ROWS - 1, row_high, pltpu.roll(value, ROWS - 1, 1))
    total, step = value + above, above - value

    def next_z(field):
        return jnp.where(lane == planes - 1, 0.0, pltpu.roll(field, planes - 1, 2))

    total_next, step_next = next_z(total), next_z(step)
    both = total + total_next
    along_z = total_next - total
    along_y = step + step_next
    along_yz = step_next - step
    return (
        both[1:] - both[:-1],
        along_y[1:] + along_y[:-1],
        along_z[1:] + along_z[:-1],
        along_y[1:] - along_y[:-1],
        along_z[1:] - along_z[:-1],
        along_yz[1:] + along_yz[:-1],
        along_yz[1:] - along_yz[:-1],
    )


def element_energy(modes):
    (ax, ay, az, axy, axz, ayz, axyz), (bx, by, bz, bxy, bxz, byz, bxyz), (
        cx,
        cy,
        cz,
        cxy,
        cxz,
        cyz,
        cxyz,
    ) = modes

    def sq(value):
        return value * value

    first = (
        (LAME_FIRST / 16.0) * sq(ax + by + cz)
        + (2.0 * SHEAR / 16.0) * (sq(ax) + sq(by) + sq(cz))
        + (SHEAR / 16.0) * (sq(ay + bx) + sq(az + cx) + sq(bz + cy))
    )
    second = (
        (LAME_FIRST / 48.0) * (sq(axy + cyz) + sq(bxy + cxz) + sq(axz + byz))
        + (3.0 * SHEAR / 48.0) * (sq(axy) + sq(axz) + sq(bxy) + sq(byz) + sq(cxz) + sq(cyz))
        + (SHEAR / 48.0) * (sq(ayz + bxz) + sq(ayz + cxy) + sq(bxz + cxy))
    )
    third = ((LAME_FIRST + 4.0 * SHEAR) / 144.0) * (sq(axyz) + sq(bxyz) + sq(cxyz))
    return first + second + third


def peers(count, body):
    if count <= 64:
        for step in range(1, count):
            body(step)
    else:
        lax.fori_loop(1, count, lambda step, carry: (body(step), carry)[1], 0)


def kernel(
    count_x,
    count_y,
    dens_hbm,
    disp_hbm,
    pas_hbm,
    results,
    big,
    passive,
    pack_low,
    pack_high,
    row_high,
    row_low,
    spread,
    spread_pack_low,
    spread_pack_high,
    spread_row_high,
    spread_row_low,
    corner_pp,
    corner_mp,
    corner_pm,
    corner_mm,
    s_corner_pp,
    s_corner_mp,
    s_corner_pm,
    s_corner_mm,
    node_row,
    tail_high,
    tail_low,
    inverse,
    inverse_volume,
    scaled,
    lower,
    upper,
    sum_scaled,
    sum_lower,
    sum_upper,
    partial,
    totals,
    local_sems,
    send_a,
    recv_a,
    send_b,
    recv_b,
    send_c,
    recv_c,
):
    new_out, sens_out = results.at[0], results.at[1]
    planes = dens_hbm.shape[-1]
    cols_x = dens_hbm.shape[0] // ROWS
    block = cols_x * ROWS
    last = cols_x * ROWS
    ix, iy = lax.axis_index("gx"), lax.axis_index("gy")
    total_x, total_y = cols_x * count_x, ROWS * count_y

    def inside(x, y):
        return (x >= 0) & (x < count_x) & (y >= 0) & (y < count_y)

    loads = [
        pltpu.make_async_copy(dens_hbm, big.at[0, pl.ds(ROWS, block)], local_sems.at[0]),
        pltpu.make_async_copy(disp_hbm, big.at[pl.ds(1, 3), pl.ds(ROWS, block)], local_sems.at[1]),
        pltpu.make_async_copy(pas_hbm, passive, local_sems.at[2]),
    ]
    for load in loads:
        load.start()

    devices = count_x * count_y

    def peer(step):
        return (lax.rem(ix + step // count_y, count_x), lax.rem(iy + step % count_y, count_y))

    barrier = pltpu.get_barrier_semaphore()
    peers(
        devices,
        lambda step: pl.semaphore_signal(
            barrier, inc=1, device_id=peer(step), device_id_type=MESH
        ),
    )

    def fill(way, refs):
        @pl.when(jnp.logical_not(inside(ix - way[0], iy - way[1])))
        def _():
            for ref in refs:
                ref[...] = jnp.zeros(ref.shape, ref.dtype)

    def exchange(pairs, send, recv):
        def copy(at):
            source, target = pairs[at]
            dx, dy = WAYS[at]
            return pltpu.make_async_remote_copy(
                src_ref=source,
                dst_ref=target,
                send_sem=send.at[at],
                recv_sem=recv.at[at],
                device_id=(ix + dx, iy + dy),
                device_id_type=MESH,
            )

        def start(at):
            dx, dy = WAYS[at]

            @pl.when(inside(ix + dx, iy + dy))
            def _():
                copy(at).start()

        def arrive(at):
            dx, dy = WAYS[at]

            @pl.when(inside(ix - dx, iy - dy))
            def _():
                copy(at).wait_recv()

        def sent(at):
            dx, dy = WAYS[at]

            @pl.when(inside(ix + dx, iy + dy))
            def _():
                copy(at).wait_send()

        return start, arrive, sent

    first_tile, last_tile = pl.ds(ROWS, ROWS), pl.ds(last, ROWS)
    low_tile, high_tile = pl.ds(0, ROWS), pl.ds(last + ROWS, ROWS)
    start_a, arrive_a, sent_a = exchange(
        [
            (big.at[0, last_tile], big.at[0, low_tile]),
            (big.at[:, first_tile], big.at[:, high_tile]),
            (pack_high, row_low.at[pl.ds(0, cols_x)]),
            (pack_low, row_high.at[:, pl.ds(0, cols_x)]),
            (big.at[0, last_tile], corner_pp),
            (big.at[0, first_tile], corner_mp),
            (big.at[0, last_tile], corner_pm),
            (big.at[:, first_tile], corner_mm),
        ],
        send_a,
        recv_a,
    )
    start_b, arrive_b, sent_b = exchange(
        [
            (spread.at[last_tile], spread.at[low_tile]),
            (spread.at[first_tile], spread.at[high_tile]),
            (spread_pack_high, spread_row_low.at[pl.ds(0, cols_x)]),
            (spread_pack_low, spread_row_high.at[pl.ds(0, cols_x)]),
            (spread.at[last_tile], s_corner_pp),
            (spread.at[first_tile], s_corner_mp),
            (spread.at[last_tile], s_corner_pm),
            (spread.at[first_tile], s_corner_mm),
        ],
        send_b,
        recv_b,
    )
    fill(WAYS[0], [big.at[0, low_tile], spread.at[low_tile]])
    fill(WAYS[1], [big.at[:, high_tile], spread.at[high_tile]])
    fill(WAYS[2], [row_low.at[pl.ds(0, cols_x)], spread_row_low.at[pl.ds(0, cols_x)]])
    fill(WAYS[3], [row_high.at[:, pl.ds(0, cols_x)], spread_row_high.at[pl.ds(0, cols_x)]])
    fill(WAYS[4], [corner_pp, s_corner_pp])
    fill(WAYS[5], [corner_mp, s_corner_mp])
    fill(WAYS[6], [corner_pm, s_corner_pm])
    fill(WAYS[7], [corner_mm, s_corner_mm])

    def strided(start):
        return pl.ds(start, cols_x, stride=ROWS)

    loads[0].wait()
    pack_high[...] = big[0, strided(ROWS + ROWS - 1), :]
    pack_low[0] = big[0, strided(ROWS), :]
    loads[1].wait()
    for c in (1, 2, 3):
        pack_low[c] = big[c, strided(ROWS), :]
    pl.semaphore_wait(barrier, devices - 1)
    for at in (3, 1, 2, 7, 0, 4, 5, 6):
        start_a(at)

    lane = lax.broadcasted_iota(jnp.int32, (ROWS, planes), 1)
    row = lax.broadcasted_iota(jnp.int32, (ROWS, planes), 0)

    def counted(at, total):
        one, none = jnp.float32(1.0), jnp.float32(0.0)
        return jnp.where(at > 0, one, none) + jnp.where(at < total - 1, one, none)

    count_z = counted(lane, planes)
    known = {}

    def representative(x):
        return x if x in (-1, 0, cols_x - 1, cols_x) else 1

    def inverse_sums(x, offset):
        x = representative(x)
        if (x, offset) not in known:
            y = iy * ROWS + row + offset
            beside_y = counted(y, total_y)
            global_x = ix * cols_x + x
            beside_x = counted(global_x, total_x)
            sums = (
                1.5
                + 0.5 * (beside_x + beside_y + count_z)
                + EDGE_WEIGHT * (beside_x * beside_y + beside_x * count_z + beside_y * count_z)
            )
            result = 1.0 / sums
            result = jnp.where((y >= 0) & (y < total_y), result, 0.0)
            if x in (-1, cols_x):
                held = (global_x >= 0) & (global_x < total_x)
                result = result * jnp.where(held, jnp.float32(1.0), jnp.float32(0.0))
            known[x, offset] = (result, parts_of_filter(result, lane))
        return known[x, offset]

    weights = {}
    for x in range(cols_x):
        tile = pl.ds(x * ROWS, ROWS)
        inverse[tile, :] = inverse_sums(x, 0)[0]
        key = tuple(representative(x + d) for d in (-1, 0, 1))
        if key not in weights:
            volume = inverse_sums(x, 0)[1][0]
            volume = volume + inverse_sums(x - 1, 0)[1][1] + inverse_sums(x + 1, 0)[1][1]
            for offset in (-1, 1):
                volume = volume + inverse_sums(x, offset)[1][1]
                volume = volume + inverse_sums(x - 1, offset)[1][2]
                volume = volume + inverse_sums(x + 1, offset)[1][2]
            weights[key] = 1.0 / volume
        inverse_volume[tile, :] = weights[key]

    def masks(size):
        shape = (size, ROWS, planes)
        return (
            lax.broadcasted_iota(jnp.int32, shape, 1),
            lax.broadcasted_iota(jnp.int32, shape, 2),
        )

    size = 4 if cols_x % 4 == 0 else 1
    rows_here = size * ROWS
    row_s, lane_s = masks(size)
    row_1, lane_1 = masks(size + 1)
    _, lane_2 = masks(size + 2)

    def tiles(ref, first):
        return ref[pl.ds(first * ROWS, rows_here), :].reshape(size, ROWS, planes)

    loads[2].wait()
    for first in range(0, cols_x, size):
        at = pl.ds(first * ROWS, rows_here)
        kind = tiles(passive, first)
        held = big[0, pl.ds((first + 1) * ROWS, rows_here), :].reshape(size, ROWS, planes)
        fixed = jnp.where(kind == 1, 1.0, 0.0)
        low = jnp.where(kind == 0, jnp.maximum(held - MOVE_LIMIT, 0.0), fixed)
        high = jnp.where(kind == 0, jnp.minimum(held + MOVE_LIMIT, 1.0), fixed)
        lower[at, :] = low.reshape(rows_here, planes)
        upper[at, :] = high.reshape(rows_here, planes)

    for at in range(8):
        arrive_a(at)

    def join(rows, first, final):
        rows[pl.ds(cols_x, ROWS), :] = jnp.where(row == 0, first, jnp.where(row == 7, final, 0.0))

    def tails(rows_high, rows_low, pp, mp, pm, mm):
        join(rows_high, mm[0:1, :], pm[0:1, :])
        join(rows_low, mp[7:8, :], pp[7:8, :])
        lane_rows = lax.broadcasted_iota(jnp.int32, (cols_x + ROWS, planes), 1)
        tail_high[strided(ROWS - 1), :] = filter_rows(rows_high[...], lane_rows, cols_x)
        tail_low[strided(0), :] = filter_rows(rows_low[...], lane_rows, cols_x)

    tails(row_high.at[0], row_low, corner_pp, corner_mp, corner_pm, corner_mm.at[0])
    for c in range(3):
        node_row[c, strided(ROWS - 1), :] = row_high[1 + c, pl.ds(0, cols_x), :]
        node_row[c, pl.ds(block + ROWS - 1, 1), :] = corner_mm[1 + c, 0:1, :]

    density = big.at[0]

    for first in range(0, cols_x, size):
        near = pl.ds((first + 1) * ROWS, (size + 1) * ROWS)
        high = pl.ds(first * ROWS, (size + 1) * ROWS)
        shape = (size + 1, ROWS, planes)
        modes = [
            corner_modes(
                big[1 + c, near, :].reshape(shape),
                node_row[c, high, :].reshape(shape),
                row_1,
                lane_1,
            )
            for c in range(3)
        ]
        energy = element_energy(modes)
        inv = tiles(inverse, first)
        kind = tiles(passive, first)
        physical = filter_chunk(density, first, size, tail_low, tail_high, row_s, lane_2) * inv
        physical = jnp.where(kind == 1, 1.0, jnp.where(kind == 2, 0.0, physical))
        raw = (-DERIVATIVE) * physical * physical * energy
        spread[pl.ds((first + 1) * ROWS, rows_here), :] = (raw * inv).reshape(rows_here, planes)

    spread_pack_high[...] = spread[strided(ROWS + ROWS - 1), :]
    spread_pack_low[...] = spread[strided(ROWS), :]
    for at in (3, 2, 1, 0, 7, 4, 5, 6):
        start_b(at)

    def rate_of(sens, held, weight):
        return held * jnp.sqrt(-sens * weight)

    def middle_rows(value, index):
        return jnp.where((index > 0) & (index < ROWS - 1), value, 0.0)

    def plane_group(first, count, place):
        shape = (count, ROWS, planes)
        row_c = lax.broadcasted_iota(jnp.int32, shape, 1)
        lane_c = lax.broadcasted_iota(jnp.int32, (count + 2, ROWS, planes), 2)
        wide = spread[pl.ds(first * ROWS, (count + 2) * ROWS), :].reshape(count + 2, ROWS, planes)
        own, near, far = parts_of_filter(wide, lane_c)
        side = near[1:-1] + far[:-2] + far[2:]
        sens = own[1:-1] + near[:-2] + near[2:]
        sens = sens + (pltpu.roll(side, ROWS - 1, 1) + pltpu.roll(side, 1, 1))
        at = pl.ds(first * ROWS, count * ROWS)
        held = big[0, pl.ds((first + 1) * ROWS, count * ROWS), :].reshape(shape)
        sens = middle_rows(sens, row_c)
        rate = rate_of(sens, held, inverse_volume[at, :].reshape(shape))
        sens_out[at, :] = sens.reshape(count * ROWS, planes)
        scaled[at, :] = rate.reshape(count * ROWS, planes)
        to = pl.ds(place * ROWS, count * ROWS)
        sum_scaled[to, :] = rate.reshape(count * ROWS, planes)
        for source, target in ((lower, sum_lower), (upper, sum_upper)):
            kept = middle_rows(source[at, :].reshape(shape), row_c)
            target[to, :] = kept.reshape(count * ROWS, planes)

    slots = 2**BISECT
    group = 16
    spacing = 2.0 * BRACKET / slots
    scales = jnp.concatenate(
        [jnp.full((1, ROWS, planes), math.exp(-0.5 * spacing * j), jnp.float32) for j in range(group)]
    )

    def add_volumes(first_tile, end_tile, fresh):
        def volumes(i, carry):
            begin = (-BRACKET) + (spacing * group) * i.astype(jnp.float32)
            factors = scales * jnp.exp(jnp.full((ROWS, planes), -0.5 * begin, jnp.float32))[None]
            at = pl.ds(pl.multiple_of(i * (group * ROWS), group * ROWS), group * ROWS)
            if fresh:
                total = jnp.zeros((group, ROWS, planes), jnp.float32)
            else:
                total = partial[at, :].reshape(group, ROWS, planes)
            for x in range(first_tile, end_tile):
                tile = pl.ds(x * ROWS, ROWS)
                moved = jnp.maximum(sum_scaled[tile, :][None] * factors, sum_lower[tile, :][None])
                total = total + jnp.minimum(moved, sum_upper[tile, :][None])
            partial[at, :] = total.reshape(group * ROWS, planes)
            return carry

        lax.fori_loop(0, slots // group, volumes, 0)

    inner = cols_x - 2
    for first in range(1, 1 + inner, size):
        plane_group(first, min(size, 1 + inner - first), first - 1)
    add_volumes(0, inner, True)

    for at in range(8):
        arrive_b(at)
    plane_group(0, 1, inner)
    plane_group(cols_x - 1, 1, inner + 1)
    join(spread_row_high, s_corner_mm[0:1, :], s_corner_pm[0:1, :])
    join(spread_row_low, s_corner_mp[7:8, :], s_corner_pp[7:8, :])
    lane_p = lax.broadcasted_iota(jnp.int32, (cols_x + ROWS, planes), 1)

    def packed_row(r):
        above = spread[pl.ds(last + ROWS + r, 1), :]
        below = spread[pl.ds(r, 1), :]
        tail = jnp.where(row == 0, above, jnp.where(row == ROWS - 1, below, 0.0))
        return jnp.concatenate([spread[strided(ROWS + r), :], tail], axis=0)

    def edge_row(r, beyond, next_row, held, place):
        own, near, _ = parts_of_filter(packed_row(r), lane_p)
        count = own.shape[0]
        sens = (own + pltpu.roll(near, 1, 0) + pltpu.roll(near, count - 1, 0))[:cols_x]
        sens = sens + filter_rows(beyond, lane_p, cols_x)
        sens = sens + filter_rows(packed_row(next_row), lane_p, cols_x)
        rate = rate_of(sens, held, inverse_volume[strided(r), :])
        sens_out[strided(r), :] = sens
        scaled[strided(r), :] = rate
        to = pl.ds(place * ROWS, cols_x)
        sum_scaled[to, :] = rate
        sum_lower[to, :] = lower[strided(r), :]
        sum_upper[to, :] = upper[strided(r), :]

    edge_row(0, spread_row_low[...], 1, pack_low[0], inner + 2)
    edge_row(ROWS - 1, spread_row_high[...], ROWS - 2, pack_high[...], inner + 2 + cols_x // ROWS)
    add_volumes(inner, inner + 2 + 2 * (cols_x // ROWS), False)
    me = ix * count_y + iy
    halves = slots // planes
    for half in range(halves):
        start = half * planes * ROWS
        lines = partial[pl.ds(start, planes, stride=ROWS), :]
        for s in range(1, ROWS):
            lines = lines + partial[pl.ds(start + s, planes, stride=ROWS), :]
        totals[me, half : half + 1, :] = jnp.sum(lines.T, axis=0, keepdims=True)

    def share(step):
        pltpu.make_async_remote_copy(
            src_ref=totals.at[me],
            dst_ref=totals.at[me],
            send_sem=send_c,
            recv_sem=recv_c,
            device_id=peer(step),
            device_id_type=MESH,
        ).start()

    peers(devices, share)
    others = totals.at[pl.ds(0, devices - 1)]
    pltpu.make_async_copy(others, others, recv_c).wait()
    volume = jnp.sum(totals[...], axis=0)
    label = lax.broadcasted_iota(jnp.int32, volume.shape, 0) * planes + lax.broadcasted_iota(
        jnp.int32, volume.shape, 1
    )
    target = VOLUME_SHARE * total_x * total_y * planes
    over = jnp.where((label > 0) & (volume > target), 1.0, 0.0)
    reached = jnp.sum(jnp.sum(over, axis=0, keepdims=True), axis=1, keepdims=True)
    middle = (-BRACKET) + spacing * (jnp.broadcast_to(reached, (ROWS, planes)) + 0.5)
    factor = jnp.exp(-0.5 * middle)[None]
    for first in range(0, cols_x, size):
        at = pl.ds(first * ROWS, rows_here)
        moved = jnp.maximum(tiles(scaled, first) * factor, tiles(lower, first))
        new_out[at, :] = jnp.minimum(moved, tiles(upper, first)).reshape(rows_here, planes)
    for at in range(8):
        sent_a(at)
        sent_b(at)
    pltpu.make_async_copy(others, others, send_c).wait()


def per_device(count_x, count_y, density, displacement, passive):
    cols_x, cols_y, planes = density.shape
    assert cols_y == ROWS and cols_x % ROWS == 0 and planes == 128
    block = cols_x * ROWS
    slots = 2**BISECT

    def buffer(*shape):
        return pltpu.VMEM(shape, jnp.float32)

    field = buffer(block, planes)
    tile = buffer(ROWS, planes)
    wide = buffer(block + 2 * ROWS, planes)
    rows = buffer(cols_x, planes)
    sums = buffer(block + 2 * cols_x, planes)
    ring = buffer(cols_x + ROWS, planes)
    held = functools.partial(pltpu.with_memory_space_constraint, memory_space=pltpu.HBM)
    anywhere = pl.BlockSpec(memory_space=pl.ANY)
    out = jax.ShapeDtypeStruct((2, block, planes), jnp.float32)
    results = pl.pallas_call(
        functools.partial(kernel, count_x, count_y),
        out_shape=out,
        in_specs=[anywhere] * 3,
        out_specs=pl.BlockSpec(memory_space=pltpu.VMEM),
        scratch_shapes=[
            buffer(4, block + 2 * ROWS, planes),
            pltpu.VMEM((block, planes), jnp.int32),
            buffer(4, cols_x, planes),
            rows,
            buffer(4, cols_x + ROWS, planes),
            ring,
            wide,
            rows,
            rows,
            ring,
            ring,
            tile,
            tile,
            tile,
            buffer(4, ROWS, planes),
            tile,
            tile,
            tile,
            tile,
            buffer(3, block + ROWS, planes),
            field,
            field,
            field,
            field,
            field,
            field,
            field,
            sums,
            sums,
            sums,
            buffer(slots * ROWS, planes),
            buffer(count_x * count_y, slots // planes, planes),
            pltpu.SemaphoreType.DMA((3,)),
            pltpu.SemaphoreType.DMA((8,)),
            pltpu.SemaphoreType.DMA((8,)),
            pltpu.SemaphoreType.DMA((8,)),
            pltpu.SemaphoreType.DMA((8,)),
            pltpu.SemaphoreType.DMA,
            pltpu.SemaphoreType.DMA,
        ],
        compiler_params=pltpu.CompilerParams(
            collective_id=0, has_side_effects=True, vmem_limit_bytes=16 * 1024 * 1024
        ),
    )(
        held(density.reshape(block, planes)),
        held(displacement.reshape(3, block, planes)),
        held(passive.reshape(block, planes)),
    )
    return (results[0].reshape(density.shape), results[1].reshape(density.shape))


def solution(mesh):
    return jax.shard_map(
        functools.partial(per_device, mesh.shape["gx"], mesh.shape["gy"]),
        mesh=mesh,
        in_specs=(P("gx", "gy", None), P(None, "gx", "gy", None), P("gx", "gy", None)),
        out_specs=(P("gx", "gy", None), P("gx", "gy", None)),
        check_vma=False,
    )
```

```python
import functools
import math

import jax
import jax.numpy as jnp
from jax import lax
from jax.experimental import pallas as pl
from jax.experimental.pallas import tpu as pltpu
from jax.sharding import PartitionSpec as P

BISECT = 8
BRACKET = 8.0
MOVE_LIMIT = 0.2
VOLUME_SHARE = 0.35
DERIVATIVE = 3.0 * (1.0 - 1e-09)
EDGE_WEIGHT = 1.5 - math.sqrt(2.0)
POISSON = 0.3
LAME_FIRST = POISSON / ((1.0 + POISSON) * (1.0 - 2.0 * POISSON))
SHEAR = 0.5 / (1.0 + POISSON)
ROWS = 8
MESH = pl.DeviceIdType.MESH
WAYS = [(1, 0), (-1, 0), (0, 1), (0, -1), (1, 1), (-1, 1), (1, -1), (-1, -1)]


def z_neighbours(value, lane):
    planes = value.shape[-1]
    axis = value.ndim - 1
    above = jnp.where(lane == planes - 1, 0.0, pltpu.roll(value, planes - 1, axis))
    below = jnp.where(lane == 0, 0.0, pltpu.roll(value, 1, axis))
    return above + below


def parts_of_filter(value, lane):
    beside = z_neighbours(value, lane)
    return (
        1.5 * value + 0.5 * beside,
        0.5 * value + EDGE_WEIGHT * beside,
        EDGE_WEIGHT * value,
    )


def filter_rows(packed, lane, cols_x):
    _, near, far = parts_of_filter(packed, lane)
    count = packed.shape[0]
    return (near + pltpu.roll(far, 1, 0) + pltpu.roll(far, count - 1, 0))[:cols_x]


def packed_filter(beyond, here, beyond_next, lane, cols_x):
    own, near, _ = parts_of_filter(here, lane)
    count = here.shape[0]
    result = (own + pltpu.roll(near, 1, 0) + pltpu.roll(near, count - 1, 0))[:cols_x]
    result = result + filter_rows(beyond, lane, cols_x)
    return result + filter_rows(beyond_next, lane, cols_x)


def plane_filter(wide, lane):
    own, near, far = parts_of_filter(wide, lane)
    side = near[1:-1] + far[:-2] + far[2:]
    result = own[1:-1] + near[:-2] + near[2:]
    return result + (pltpu.roll(side, ROWS - 1, 1) + pltpu.roll(side, 1, 1))


def corner_modes(value, above, lane, packed):
    planes = value.shape[-1]
    total, step = value + above, above - value

    def next_z(field):
        moved = pltpu.roll(field, planes - 1, field.ndim - 1)
        return jnp.where(lane == planes - 1, 0.0, moved)

    def ends(field):
        if packed:
            return field, pltpu.roll(field, field.shape[0] - 1, 0)
        return field[:-1], field[1:]

    total_next, step_next = next_z(total), next_z(step)
    both, both_next = ends(total + total_next)
    along_z, along_z_next = ends(total_next - total)
    along_y, along_y_next = ends(step + step_next)
    along_yz, along_yz_next = ends(step_next - step)
    return (
        both_next - both,
        along_y_next + along_y,
        along_z_next + along_z,
        along_y_next - along_y,
        along_z_next - along_z,
        along_yz_next + along_yz,
        along_yz_next - along_yz,
    )


def element_energy(modes):
    (ax, ay, az, axy, axz, ayz, axyz), (bx, by, bz, bxy, bxz, byz, bxyz), (
        cx,
        cy,
        cz,
        cxy,
        cxz,
        cyz,
        cxyz,
    ) = modes

    def sq(value):
        return value * value

    first = (
        (LAME_FIRST / 16.0) * sq(ax + by + cz)
        + (2.0 * SHEAR / 16.0) * (sq(ax) + sq(by) + sq(cz))
        + (SHEAR / 16.0) * (sq(ay + bx) + sq(az + cx) + sq(bz + cy))
    )
    second = (
        (LAME_FIRST / 48.0) * (sq(axy + cyz) + sq(bxy + cxz) + sq(axz + byz))
        + (3.0 * SHEAR / 48.0) * (sq(axy) + sq(axz) + sq(bxy) + sq(byz) + sq(cxz) + sq(cyz))
        + (SHEAR / 48.0) * (sq(ayz + bxz) + sq(ayz + cxy) + sq(bxz + cxy))
    )
    third = ((LAME_FIRST + 4.0 * SHEAR) / 144.0) * (sq(axyz) + sq(bxyz) + sq(cxyz))
    return first + second + third


def peers(count, body):
    if count <= 64:
        for step in range(1, count):
            body(step)
    else:
        lax.fori_loop(1, count, lambda step, carry: (body(step), carry)[1], 0)


def kernel(
    count_x,
    count_y,
    dens_hbm,
    disp_hbm,
    pas_hbm,
    results,
    big,
    passive,
    pack_low,
    pack_high,
    row_high,
    row_low,
    spread,
    spread_pack_low,
    spread_pack_high,
    spread_row_high,
    spread_row_low,
    corner_pp,
    corner_mp,
    corner_pm,
    corner_mm,
    s_corner_pp,
    s_corner_mp,
    s_corner_pm,
    s_corner_mm,
    inverse,
    inverse_volume,
    scaled,
    lower,
    upper,
    sum_scaled,
    sum_lower,
    sum_upper,
    partial,
    totals,
    local_sems,
    send_a,
    recv_a,
    send_b,
    recv_b,
    send_c,
    recv_c,
):
    new_out, sens_out = results.at[0], results.at[1]
    planes = dens_hbm.shape[-1]
    cols_x = dens_hbm.shape[0] // ROWS
    block = cols_x * ROWS
    last = cols_x * ROWS
    ix, iy = lax.axis_index("gx"), lax.axis_index("gy")
    total_x, total_y = cols_x * count_x, ROWS * count_y

    def inside(x, y):
        return (x >= 0) & (x < count_x) & (y >= 0) & (y < count_y)

    loads = [
        pltpu.make_async_copy(dens_hbm, big.at[0, pl.ds(ROWS, block)], local_sems.at[0]),
        pltpu.make_async_copy(disp_hbm, big.at[pl.ds(1, 3), pl.ds(ROWS, block)], local_sems.at[1]),
        pltpu.make_async_copy(pas_hbm, passive, local_sems.at[2]),
    ]
    for load in loads:
        load.start()

    devices = count_x * count_y

    def peer(step):
        return (lax.rem(ix + step // count_y, count_x), lax.rem(iy + step % count_y, count_y))

    barrier = pltpu.get_barrier_semaphore()
    peers(
        devices,
        lambda step: pl.semaphore_signal(
            barrier, inc=1, device_id=peer(step), device_id_type=MESH
        ),
    )

    def fill(way, refs):
        @pl.when(jnp.logical_not(inside(ix - way[0], iy - way[1])))
        def _():
            for ref in refs:
                ref[...] = jnp.zeros(ref.shape, ref.dtype)

    def exchange(pairs, send, recv):
        def copy(at):
            source, target = pairs[at]
            dx, dy = WAYS[at]
            return pltpu.make_async_remote_copy(
                src_ref=source,
                dst_ref=target,
                send_sem=send.at[at],
                recv_sem=recv.at[at],
                device_id=(ix + dx, iy + dy),
                device_id_type=MESH,
            )

        def start(at):
            dx, dy = WAYS[at]

            @pl.when(inside(ix + dx, iy + dy))
            def _():
                copy(at).start()

        def arrive(at):
            dx, dy = WAYS[at]

            @pl.when(inside(ix - dx, iy - dy))
            def _():
                copy(at).wait_recv()

        def sent(at):
            dx, dy = WAYS[at]

            @pl.when(inside(ix + dx, iy + dy))
            def _():
                copy(at).wait_send()

        return start, arrive, sent

    first_tile, last_tile = pl.ds(ROWS, ROWS), pl.ds(last, ROWS)
    low_tile, high_tile = pl.ds(0, ROWS), pl.ds(last + ROWS, ROWS)
    start_a, arrive_a, sent_a = exchange(
        [
            (big.at[0, last_tile], big.at[0, low_tile]),
            (big.at[:, first_tile], big.at[:, high_tile]),
            (pack_high, row_low.at[pl.ds(0, cols_x)]),
            (pack_low, row_high.at[:, pl.ds(0, cols_x)]),
            (big.at[0, last_tile], corner_pp),
            (big.at[0, first_tile], corner_mp),
            (big.at[0, last_tile], corner_pm),
            (big.at[:, first_tile], corner_mm),
        ],
        send_a,
        recv_a,
    )
    start_b, arrive_b, sent_b = exchange(
        [
            (spread.at[last_tile], spread.at[low_tile]),
            (spread.at[first_tile], spread.at[high_tile]),
            (spread_pack_high, spread_row_low.at[pl.ds(0, cols_x)]),
            (spread_pack_low, spread_row_high.at[pl.ds(0, cols_x)]),
            (spread.at[last_tile], s_corner_pp),
            (spread.at[first_tile], s_corner_mp),
            (spread.at[last_tile], s_corner_pm),
            (spread.at[first_tile], s_corner_mm),
        ],
        send_b,
        recv_b,
    )
    def strided(start):
        return pl.ds(start, cols_x, stride=ROWS)

    loads[0].wait()
    pack_high[...] = big[0, strided(ROWS + ROWS - 1), :]
    pack_low[0] = big[0, strided(ROWS), :]
    loads[1].wait()
    for c in (1, 2, 3):
        pack_low[c] = big[c, strided(ROWS), :]
    pl.semaphore_wait(barrier, devices - 1)
    for at in (3, 1, 2, 7, 0, 4, 5, 6):
        start_a(at)
    fill(WAYS[0], [big.at[0, low_tile], spread.at[low_tile]])
    fill(WAYS[1], [big.at[:, high_tile], spread.at[high_tile]])
    fill(WAYS[2], [row_low.at[pl.ds(0, cols_x)], spread_row_low.at[pl.ds(0, cols_x)]])
    fill(WAYS[3], [row_high.at[:, pl.ds(0, cols_x)], spread_row_high.at[pl.ds(0, cols_x)]])
    fill(WAYS[4], [corner_pp, s_corner_pp])
    fill(WAYS[5], [corner_mp, s_corner_mp])
    fill(WAYS[6], [corner_pm, s_corner_pm])
    fill(WAYS[7], [corner_mm, s_corner_mm])

    lane = lax.broadcasted_iota(jnp.int32, (ROWS, planes), 1)
    row = lax.broadcasted_iota(jnp.int32, (ROWS, planes), 0)

    def counted(at, total):
        one, none = jnp.float32(1.0), jnp.float32(0.0)
        return jnp.where(at > 0, one, none) + jnp.where(at < total - 1, one, none)

    count_z = counted(lane, planes)
    known = {}

    def representative(x):
        return x if x in (-1, 0, cols_x - 1, cols_x) else 1

    def inverse_sums(x, offset):
        x = representative(x)
        if (x, offset) not in known:
            y = iy * ROWS + row + offset
            beside_y = counted(y, total_y)
            global_x = ix * cols_x + x
            beside_x = counted(global_x, total_x)
            sums = (
                1.5
                + 0.5 * (beside_x + beside_y + count_z)
                + EDGE_WEIGHT * (beside_x * beside_y + beside_x * count_z + beside_y * count_z)
            )
            result = 1.0 / sums
            result = jnp.where((y >= 0) & (y < total_y), result, 0.0)
            if x in (-1, cols_x):
                held = (global_x >= 0) & (global_x < total_x)
                result = result * jnp.where(held, jnp.float32(1.0), jnp.float32(0.0))
            known[x, offset] = (result, parts_of_filter(result, lane))
        return known[x, offset]

    weights = {}
    for x in range(cols_x):
        tile = pl.ds(x * ROWS, ROWS)
        inverse[tile, :] = inverse_sums(x, 0)[0]
        key = tuple(representative(x + d) for d in (-1, 0, 1))
        if key not in weights:
            volume = inverse_sums(x, 0)[1][0]
            volume = volume + inverse_sums(x - 1, 0)[1][1] + inverse_sums(x + 1, 0)[1][1]
            for offset in (-1, 1):
                volume = volume + inverse_sums(x, offset)[1][1]
                volume = volume + inverse_sums(x - 1, offset)[1][2]
                volume = volume + inverse_sums(x + 1, offset)[1][2]
            weights[key] = 1.0 / volume
        inverse_volume[tile, :] = weights[key]

    size = 4 if cols_x % 4 == 0 else 1
    rows_here = size * ROWS
    def tiles(ref, first):
        return ref[pl.ds(first * ROWS, rows_here), :].reshape(size, ROWS, planes)

    loads[2].wait()
    for first in range(0, cols_x, size):
        at = pl.ds(first * ROWS, rows_here)
        kind = tiles(passive, first)
        held = big[0, pl.ds((first + 1) * ROWS, rows_here), :].reshape(size, ROWS, planes)
        fixed = jnp.where(kind == 1, 1.0, 0.0)
        low = jnp.where(kind == 0, jnp.maximum(held - MOVE_LIMIT, 0.0), fixed)
        high = jnp.where(kind == 0, jnp.minimum(held + MOVE_LIMIT, 1.0), fixed)
        lower[at, :] = low.reshape(rows_here, planes)
        upper[at, :] = high.reshape(rows_here, planes)

    def spread_of(density_sum, modes, kind, inv):
        physical = density_sum * inv
        physical = jnp.where(kind == 1, 1.0, jnp.where(kind == 2, 0.0, physical))
        raw = (-DERIVATIVE) * physical * physical * element_energy(modes)
        return raw * inv

    def spread_planes(first, count):
        shape = (count, ROWS, planes)
        lane_c = lax.broadcasted_iota(jnp.int32, (count + 2, ROWS, planes), 2)
        wide = big[0, pl.ds(first * ROWS, (count + 2) * ROWS), :]
        density_sum = plane_filter(wide.reshape(count + 2, ROWS, planes), lane_c)
        modes = []
        for c in range(3):
            value = big[1 + c, pl.ds((first + 1) * ROWS, (count + 1) * ROWS), :]
            value = value.reshape(count + 1, ROWS, planes)
            modes.append(corner_modes(value, pltpu.roll(value, ROWS - 1, 1), lane_c[:-1], False))
        at = pl.ds(first * ROWS, count * ROWS)
        result = spread_of(
            density_sum, modes, passive[at, :].reshape(shape), inverse[at, :].reshape(shape)
        )
        to = pl.ds((first + 1) * ROWS, count * ROWS)
        spread[to, :] = result.reshape(count * ROWS, planes)

    inner = cols_x - 2
    for first in range(1, 1 + inner, size):
        spread_planes(first, min(size, 1 + inner - first))

    for at in range(8):
        arrive_a(at)

    def join(rows, first, final):
        rows[pl.ds(cols_x, ROWS), :] = jnp.where(
            row == 0, first, jnp.where(row == ROWS - 1, final, 0.0)
        )

    lane_p = lax.broadcasted_iota(jnp.int32, (cols_x + ROWS, planes), 1)

    def packed_row(field, r):
        above = field[pl.ds(last + ROWS + r, 1), :]
        below = field[pl.ds(r, 1), :]
        tail = jnp.where(row == 0, above, jnp.where(row == ROWS - 1, below, 0.0))
        return jnp.concatenate([field[strided(ROWS + r), :], tail], axis=0)

    def packed_nodes(c, r):
        above = big[c, pl.ds(last + ROWS + r, 1), :]
        tail = jnp.where(row == 0, above, 0.0)
        return jnp.concatenate([big[c, strided(ROWS + r), :], tail], axis=0)

    spread_planes(0, 1)
    spread_planes(cols_x - 1, 1)
    join(row_high.at[0], corner_mm[0, 0:1, :], corner_pm[0:1, :])
    join(row_low, corner_mp[ROWS - 1 : ROWS, :], corner_pp[ROWS - 1 : ROWS, :])
    for c in (1, 2, 3):
        join(row_high.at[c], corner_mm[c, 0:1, :], 0.0)
    density = big.at[0]

    def spread_row(r, beyond, next_row, above):
        density_sum = packed_filter(
            beyond, packed_row(density, r), packed_row(density, next_row), lane_p, cols_x
        )
        modes = []
        for c in (1, 2, 3):
            found = corner_modes(packed_nodes(c, r), above(c), lane_p, True)
            modes.append([mode[:cols_x] for mode in found])
        result = spread_of(density_sum, modes, passive[strided(r), :], inverse[strided(r), :])
        spread[strided(ROWS + r), :] = result
        return result

    spread_pack_low[...] = spread_row(0, row_low[...], 1, lambda c: packed_nodes(c, 1))
    spread_pack_high[...] = spread_row(
        ROWS - 1, row_high[0], ROWS - 2, lambda c: row_high[c]
    )
    for at in (3, 2, 1, 0, 7, 4, 5, 6):
        start_b(at)

    def rate_of(sens, held, weight):
        return held * jnp.sqrt(-sens * weight)

    def middle_rows(value, index):
        return jnp.where((index > 0) & (index < ROWS - 1), value, 0.0)

    def plane_group(first, count, place):
        shape = (count, ROWS, planes)
        row_c = lax.broadcasted_iota(jnp.int32, shape, 1)
        lane_c = lax.broadcasted_iota(jnp.int32, (count + 2, ROWS, planes), 2)
        wide = spread[pl.ds(first * ROWS, (count + 2) * ROWS), :].reshape(count + 2, ROWS, planes)
        sens = plane_filter(wide, lane_c)
        at = pl.ds(first * ROWS, count * ROWS)
        held = big[0, pl.ds((first + 1) * ROWS, count * ROWS), :].reshape(shape)
        sens = middle_rows(sens, row_c)
        rate = rate_of(sens, held, inverse_volume[at, :].reshape(shape))
        sens_out[at, :] = sens.reshape(count * ROWS, planes)
        scaled[at, :] = rate.reshape(count * ROWS, planes)
        to = pl.ds(place * ROWS, count * ROWS)
        sum_scaled[to, :] = rate.reshape(count * ROWS, planes)
        for source, target in ((lower, sum_lower), (upper, sum_upper)):
            kept = middle_rows(source[at, :].reshape(shape), row_c)
            target[to, :] = kept.reshape(count * ROWS, planes)

    slots = 2**BISECT
    group = 16
    spacing = 2.0 * BRACKET / slots
    scales = jnp.concatenate(
        [jnp.full((1, ROWS, planes), math.exp(-0.5 * spacing * j), jnp.float32) for j in range(group)]
    )

    def add_volumes(first_tile, end_tile, fresh):
        def volumes(i, carry):
            begin = (-BRACKET) + (spacing * group) * i.astype(jnp.float32)
            factors = scales * jnp.exp(jnp.full((ROWS, planes), -0.5 * begin, jnp.float32))[None]
            at = pl.ds(pl.multiple_of(i * (group * ROWS), group * ROWS), group * ROWS)
            if fresh:
                total = jnp.zeros((group, ROWS, planes), jnp.float32)
            else:
                total = partial[at, :].reshape(group, ROWS, planes)
            for x in range(first_tile, end_tile):
                tile = pl.ds(x * ROWS, ROWS)
                moved = jnp.maximum(sum_scaled[tile, :][None] * factors, sum_lower[tile, :][None])
                total = total + jnp.minimum(moved, sum_upper[tile, :][None])
            partial[at, :] = total.reshape(group * ROWS, planes)
            return carry

        lax.fori_loop(0, slots // group, volumes, 0)

    for first in range(1, 1 + inner, size):
        plane_group(first, min(size, 1 + inner - first), first - 1)
    add_volumes(0, inner, True)

    for at in range(8):
        arrive_b(at)
    plane_group(0, 1, inner)
    plane_group(cols_x - 1, 1, inner + 1)
    join(spread_row_high, s_corner_mm[0:1, :], s_corner_pm[0:1, :])
    join(spread_row_low, s_corner_mp[7:8, :], s_corner_pp[7:8, :])
    def edge_row(r, beyond, next_row, held, place):
        sens = packed_filter(
            beyond, packed_row(spread, r), packed_row(spread, next_row), lane_p, cols_x
        )
        rate = rate_of(sens, held, inverse_volume[strided(r), :])
        sens_out[strided(r), :] = sens
        scaled[strided(r), :] = rate
        to = pl.ds(place * ROWS, cols_x)
        sum_scaled[to, :] = rate
        sum_lower[to, :] = lower[strided(r), :]
        sum_upper[to, :] = upper[strided(r), :]

    edge_row(0, spread_row_low[...], 1, pack_low[0], inner + 2)
    edge_row(ROWS - 1, spread_row_high[...], ROWS - 2, pack_high[...], inner + 2 + cols_x // ROWS)
    add_volumes(inner, inner + 2 + 2 * (cols_x // ROWS), False)
    me = ix * count_y + iy
    halves = slots // planes
    for half in range(halves):
        start = half * planes * ROWS
        lines = partial[pl.ds(start, planes, stride=ROWS), :]
        for s in range(1, ROWS):
            lines = lines + partial[pl.ds(start + s, planes, stride=ROWS), :]
        totals[me, half : half + 1, :] = jnp.sum(lines.T, axis=0, keepdims=True)

    def share(step):
        pltpu.make_async_remote_copy(
            src_ref=totals.at[me],
            dst_ref=totals.at[me],
            send_sem=send_c,
            recv_sem=recv_c,
            device_id=peer(step),
            device_id_type=MESH,
        ).start()

    peers(devices, share)
    for at in range(8):
        sent_a(at)
        sent_b(at)
    others = totals.at[pl.ds(0, devices - 1)]
    pltpu.make_async_copy(others, others, recv_c).wait()
    volume = jnp.sum(totals[...], axis=0)
    label = lax.broadcasted_iota(jnp.int32, volume.shape, 0) * planes + lax.broadcasted_iota(
        jnp.int32, volume.shape, 1
    )
    target = VOLUME_SHARE * total_x * total_y * planes
    over = jnp.where((label > 0) & (volume > target), 1.0, 0.0)
    reached = jnp.sum(jnp.sum(over, axis=0, keepdims=True), axis=1, keepdims=True)
    middle = (-BRACKET) + spacing * (jnp.broadcast_to(reached, (ROWS, planes)) + 0.5)
    factor = jnp.exp(-0.5 * middle)[None]
    for first in range(0, cols_x, size):
        at = pl.ds(first * ROWS, rows_here)
        moved = jnp.maximum(tiles(scaled, first) * factor, tiles(lower, first))
        new_out[at, :] = jnp.minimum(moved, tiles(upper, first)).reshape(rows_here, planes)
    pltpu.make_async_copy(others, others, send_c).wait()


def per_device(count_x, count_y, density, displacement, passive):
    cols_x, cols_y, planes = density.shape
    assert cols_y == ROWS and cols_x % ROWS == 0 and planes == 128
    block = cols_x * ROWS
    slots = 2**BISECT

    def buffer(*shape):
        return pltpu.VMEM(shape, jnp.float32)

    field = buffer(block, planes)
    tile = buffer(ROWS, planes)
    wide = buffer(block + 2 * ROWS, planes)
    rows = buffer(cols_x, planes)
    sums = buffer(block + 2 * cols_x, planes)
    ring = buffer(cols_x + ROWS, planes)
    held = functools.partial(pltpu.with_memory_space_constraint, memory_space=pltpu.HBM)
    anywhere = pl.BlockSpec(memory_space=pl.ANY)
    out = jax.ShapeDtypeStruct((2, block, planes), jnp.float32)
    results = pl.pallas_call(
        functools.partial(kernel, count_x, count_y),
        out_shape=out,
        in_specs=[anywhere] * 3,
        out_specs=pl.BlockSpec(memory_space=pltpu.VMEM),
        scratch_shapes=[
            buffer(4, block + 2 * ROWS, planes),
            pltpu.VMEM((block, planes), jnp.int32),
            buffer(4, cols_x, planes),
            rows,
            buffer(4, cols_x + ROWS, planes),
            ring,
            wide,
            rows,
            rows,
            ring,
            ring,
            tile,
            tile,
            tile,
            buffer(4, ROWS, planes),
            tile,
            tile,
            tile,
            tile,
            field,
            field,
            field,
            field,
            field,
            sums,
            sums,
            sums,
            buffer(slots * ROWS, planes),
            buffer(count_x * count_y, slots // planes, planes),
            pltpu.SemaphoreType.DMA((3,)),
            pltpu.SemaphoreType.DMA((8,)),
            pltpu.SemaphoreType.DMA((8,)),
            pltpu.SemaphoreType.DMA((8,)),
            pltpu.SemaphoreType.DMA((8,)),
            pltpu.SemaphoreType.DMA,
            pltpu.SemaphoreType.DMA,
        ],
        compiler_params=pltpu.CompilerParams(
            collective_id=0, has_side_effects=True, vmem_limit_bytes=16 * 1024 * 1024
        ),
    )(
        held(density.reshape(block, planes)),
        held(displacement.reshape(3, block, planes)),
        held(passive.reshape(block, planes)),
    )
    return (results[0].reshape(density.shape), results[1].reshape(density.shape))


def solution(mesh):
    return jax.shard_map(
        functools.partial(per_device, mesh.shape["gx"], mesh.shape["gy"]),
        mesh=mesh,
        in_specs=(P("gx", "gy", None), P(None, "gx", "gy", None), P("gx", "gy", None)),
        out_specs=(P("gx", "gy", None), P("gx", "gy", None)),
        check_vma=False,
    )
```

```python
import functools
import math

import jax
import jax.numpy as jnp
from jax import lax
from jax.experimental import pallas as pl
from jax.experimental.pallas import tpu as pltpu
from jax.sharding import PartitionSpec as P

BISECT = 8
BRACKET = 8.0
MOVE_LIMIT = 0.2
VOLUME_SHARE = 0.35
DERIVATIVE = 3.0 * (1.0 - 1e-09)
EDGE_WEIGHT = 1.5 - math.sqrt(2.0)
POISSON = 0.3
LAME_FIRST = POISSON / ((1.0 + POISSON) * (1.0 - 2.0 * POISSON))
SHEAR = 0.5 / (1.0 + POISSON)
ROWS = 8
MESH = pl.DeviceIdType.MESH
WAYS = [(1, 0), (-1, 0), (0, 1), (0, -1), (1, 1), (-1, 1), (1, -1), (-1, -1)]


def z_neighbours(value, lane):
    planes = value.shape[-1]
    axis = value.ndim - 1
    above = jnp.where(lane == planes - 1, 0.0, pltpu.roll(value, planes - 1, axis))
    below = jnp.where(lane == 0, 0.0, pltpu.roll(value, 1, axis))
    return above + below


def parts_of_filter(value, lane):
    beside = z_neighbours(value, lane)
    return (
        1.5 * value + 0.5 * beside,
        0.5 * value + EDGE_WEIGHT * beside,
        EDGE_WEIGHT * value,
    )


def filter_rows(packed, lane, cols_x):
    _, near, far = parts_of_filter(packed, lane)
    count = packed.shape[0]
    return (near + pltpu.roll(far, 1, 0) + pltpu.roll(far, count - 1, 0))[:cols_x]


def packed_filter(beyond, here, beyond_next, lane, cols_x):
    own, near, _ = parts_of_filter(here, lane)
    count = here.shape[0]
    result = (own + pltpu.roll(near, 1, 0) + pltpu.roll(near, count - 1, 0))[:cols_x]
    result = result + filter_rows(beyond, lane, cols_x)
    return result + filter_rows(beyond_next, lane, cols_x)


def plane_filter(wide, lane):
    own, near, far = parts_of_filter(wide, lane)
    side = near[1:-1] + far[:-2] + far[2:]
    result = own[1:-1] + near[:-2] + near[2:]
    return result + (pltpu.roll(side, ROWS - 1, 1) + pltpu.roll(side, 1, 1))


def corner_modes(value, above, lane, packed):
    planes = value.shape[-1]
    total, step = value + above, above - value

    def next_z(field):
        moved = pltpu.roll(field, planes - 1, field.ndim - 1)
        return jnp.where(lane == planes - 1, 0.0, moved)

    def ends(field):
        if packed:
            return field, pltpu.roll(field, field.shape[0] - 1, 0)
        return field[:-1], field[1:]

    total_next, step_next = next_z(total), next_z(step)
    both, both_next = ends(total + total_next)
    along_z, along_z_next = ends(total_next - total)
    along_y, along_y_next = ends(step + step_next)
    along_yz, along_yz_next = ends(step_next - step)
    return (
        both_next - both,
        along_y_next + along_y,
        along_z_next + along_z,
        along_y_next - along_y,
        along_z_next - along_z,
        along_yz_next + along_yz,
        along_yz_next - along_yz,
    )


def element_energy(modes):
    (ax, ay, az, axy, axz, ayz, axyz), (bx, by, bz, bxy, bxz, byz, bxyz), (
        cx,
        cy,
        cz,
        cxy,
        cxz,
        cyz,
        cxyz,
    ) = modes

    def sq(value):
        return value * value

    first = (
        (LAME_FIRST / 16.0) * sq(ax + by + cz)
        + (2.0 * SHEAR / 16.0) * (sq(ax) + sq(by) + sq(cz))
        + (SHEAR / 16.0) * (sq(ay + bx) + sq(az + cx) + sq(bz + cy))
    )
    second = (
        (LAME_FIRST / 48.0) * (sq(axy + cyz) + sq(bxy + cxz) + sq(axz + byz))
        + (3.0 * SHEAR / 48.0) * (sq(axy) + sq(axz) + sq(bxy) + sq(byz) + sq(cxz) + sq(cyz))
        + (SHEAR / 48.0) * (sq(ayz + bxz) + sq(ayz + cxy) + sq(bxz + cxy))
    )
    third = ((LAME_FIRST + 4.0 * SHEAR) / 144.0) * (sq(axyz) + sq(bxyz) + sq(cxyz))
    return first + second + third


def peers(count, body):
    if count <= 64:
        for step in range(1, count):
            body(step)
    else:
        lax.fori_loop(1, count, lambda step, carry: (body(step), carry)[1], 0)


def kernel(
    count_x,
    count_y,
    dens_hbm,
    disp_hbm,
    pas_hbm,
    results,
    big,
    passive,
    pack_low,
    pack_high,
    row_high,
    row_low,
    spread,
    spread_pack_low,
    spread_pack_high,
    spread_row_high,
    spread_row_low,
    corner_pp,
    corner_mp,
    corner_pm,
    corner_mm,
    s_corner_pp,
    s_corner_mp,
    s_corner_pm,
    s_corner_mm,
    inverse,
    inverse_volume,
    scaled,
    lower,
    upper,
    sum_scaled,
    sum_lower,
    sum_upper,
    partial,
    totals,
    local_sems,
    send_a,
    recv_a,
    send_b,
    recv_b,
    send_c,
    recv_c,
):
    new_out, sens_out = results.at[0], results.at[1]
    planes = dens_hbm.shape[-1]
    cols_x = dens_hbm.shape[0] // ROWS
    block = cols_x * ROWS
    last = cols_x * ROWS
    ix, iy = lax.axis_index("gx"), lax.axis_index("gy")
    total_x, total_y = cols_x * count_x, ROWS * count_y

    def inside(x, y):
        return (x >= 0) & (x < count_x) & (y >= 0) & (y < count_y)

    loads = [
        pltpu.make_async_copy(dens_hbm, big.at[0, pl.ds(ROWS, block)], local_sems.at[0]),
        pltpu.make_async_copy(disp_hbm, big.at[pl.ds(1, 3), pl.ds(ROWS, block)], local_sems.at[1]),
        pltpu.make_async_copy(pas_hbm, passive, local_sems.at[2]),
    ]
    for load in loads:
        load.start()

    devices = count_x * count_y

    def peer(step):
        return (lax.rem(ix + step // count_y, count_x), lax.rem(iy + step % count_y, count_y))

    barrier = pltpu.get_barrier_semaphore()
    peers(
        devices,
        lambda step: pl.semaphore_signal(
            barrier, inc=1, device_id=peer(step), device_id_type=MESH
        ),
    )

    def fill(way, refs):
        @pl.when(jnp.logical_not(inside(ix - way[0], iy - way[1])))
        def _():
            for ref in refs:
                ref[...] = jnp.zeros(ref.shape, ref.dtype)

    def exchange(pairs, send, recv):
        def copy(at):
            source, target = pairs[at]
            dx, dy = WAYS[at]
            return pltpu.make_async_remote_copy(
                src_ref=source,
                dst_ref=target,
                send_sem=send.at[at],
                recv_sem=recv.at[at],
                device_id=(ix + dx, iy + dy),
                device_id_type=MESH,
            )

        def start(at):
            dx, dy = WAYS[at]

            @pl.when(inside(ix + dx, iy + dy))
            def _():
                copy(at).start()

        def arrive(at):
            dx, dy = WAYS[at]

            @pl.when(inside(ix - dx, iy - dy))
            def _():
                copy(at).wait_recv()

        def sent(at):
            dx, dy = WAYS[at]

            @pl.when(inside(ix + dx, iy + dy))
            def _():
                copy(at).wait_send()

        return start, arrive, sent

    first_tile, last_tile = pl.ds(ROWS, ROWS), pl.ds(last, ROWS)
    low_tile, high_tile = pl.ds(0, ROWS), pl.ds(last + ROWS, ROWS)
    start_a, arrive_a, sent_a = exchange(
        [
            (big.at[0, last_tile], big.at[0, low_tile]),
            (big.at[:, first_tile], big.at[:, high_tile]),
            (pack_high, row_low.at[pl.ds(0, cols_x)]),
            (pack_low, row_high.at[:, pl.ds(0, cols_x)]),
            (big.at[0, last_tile], corner_pp),
            (big.at[0, first_tile], corner_mp),
            (big.at[0, last_tile], corner_pm),
            (big.at[:, first_tile], corner_mm),
        ],
        send_a,
        recv_a,
    )
    start_b, arrive_b, sent_b = exchange(
        [
            (spread.at[last_tile], spread.at[low_tile]),
            (spread.at[first_tile], spread.at[high_tile]),
            (spread_pack_high, spread_row_low.at[pl.ds(0, cols_x)]),
            (spread_pack_low, spread_row_high.at[pl.ds(0, cols_x)]),
            (spread.at[last_tile], s_corner_pp),
            (spread.at[first_tile], s_corner_mp),
            (spread.at[last_tile], s_corner_pm),
            (spread.at[first_tile], s_corner_mm),
        ],
        send_b,
        recv_b,
    )
    lane = lax.broadcasted_iota(jnp.int32, (ROWS, planes), 1)
    row = lax.broadcasted_iota(jnp.int32, (ROWS, planes), 0)

    def counted(at, total):
        one, none = jnp.float32(1.0), jnp.float32(0.0)
        return jnp.where(at > 0, one, none) + jnp.where(at < total - 1, one, none)

    count_z = counted(lane, planes)
    known = {}

    def representative(x):
        return x if x in (-1, 0, cols_x - 1, cols_x) else 1

    def inverse_sums(x, offset):
        x = representative(x)
        if (x, offset) not in known:
            y = iy * ROWS + row + offset
            beside_y = counted(y, total_y)
            global_x = ix * cols_x + x
            beside_x = counted(global_x, total_x)
            sums = (
                1.5
                + 0.5 * (beside_x + beside_y + count_z)
                + EDGE_WEIGHT * (beside_x * beside_y + beside_x * count_z + beside_y * count_z)
            )
            result = 1.0 / sums
            result = jnp.where((y >= 0) & (y < total_y), result, 0.0)
            if x in (-1, cols_x):
                held = (global_x >= 0) & (global_x < total_x)
                result = result * jnp.where(held, jnp.float32(1.0), jnp.float32(0.0))
            known[x, offset] = (result, parts_of_filter(result, lane))
        return known[x, offset]

    weights = {}
    for x in range(cols_x):
        tile = pl.ds(x * ROWS, ROWS)
        inverse[tile, :] = inverse_sums(x, 0)[0]
        key = tuple(representative(x + d) for d in (-1, 0, 1))
        if key not in weights:
            volume = inverse_sums(x, 0)[1][0]
            volume = volume + inverse_sums(x - 1, 0)[1][1] + inverse_sums(x + 1, 0)[1][1]
            for offset in (-1, 1):
                volume = volume + inverse_sums(x, offset)[1][1]
                volume = volume + inverse_sums(x - 1, offset)[1][2]
                volume = volume + inverse_sums(x + 1, offset)[1][2]
            weights[key] = 1.0 / volume
        inverse_volume[tile, :] = weights[key]

    def strided(start):
        return pl.ds(start, cols_x, stride=ROWS)

    loads[0].wait()
    pack_high[...] = big[0, strided(ROWS + ROWS - 1), :]
    pack_low[0] = big[0, strided(ROWS), :]
    loads[1].wait()
    for c in (1, 2, 3):
        pack_low[c] = big[c, strided(ROWS), :]
    pl.semaphore_wait(barrier, devices - 1)
    for at in (3, 1, 2, 7, 0, 4, 5, 6):
        start_a(at)
    fill(WAYS[0], [big.at[0, low_tile], spread.at[low_tile]])
    fill(WAYS[1], [big.at[:, high_tile], spread.at[high_tile]])
    fill(WAYS[2], [row_low.at[pl.ds(0, cols_x)], spread_row_low.at[pl.ds(0, cols_x)]])
    fill(WAYS[3], [row_high.at[:, pl.ds(0, cols_x)], spread_row_high.at[pl.ds(0, cols_x)]])
    fill(WAYS[4], [corner_pp, s_corner_pp])
    fill(WAYS[5], [corner_mp, s_corner_mp])
    fill(WAYS[6], [corner_pm, s_corner_pm])
    fill(WAYS[7], [corner_mm, s_corner_mm])

    size = 4 if cols_x % 4 == 0 else 1
    rows_here = size * ROWS
    def tiles(ref, first):
        return ref[pl.ds(first * ROWS, rows_here), :].reshape(size, ROWS, planes)

    loads[2].wait()
    for first in range(0, cols_x, size):
        at = pl.ds(first * ROWS, rows_here)
        kind = tiles(passive, first)
        held = big[0, pl.ds((first + 1) * ROWS, rows_here), :].reshape(size, ROWS, planes)
        fixed = jnp.where(kind == 1, 1.0, 0.0)
        low = jnp.where(kind == 0, jnp.maximum(held - MOVE_LIMIT, 0.0), fixed)
        high = jnp.where(kind == 0, jnp.minimum(held + MOVE_LIMIT, 1.0), fixed)
        lower[at, :] = low.reshape(rows_here, planes)
        upper[at, :] = high.reshape(rows_here, planes)

    def spread_of(density_sum, modes, kind, inv):
        physical = density_sum * inv
        physical = jnp.where(kind == 1, 1.0, jnp.where(kind == 2, 0.0, physical))
        raw = (-DERIVATIVE) * physical * physical * element_energy(modes)
        return raw * inv

    def spread_planes(first, count):
        shape = (count, ROWS, planes)
        lane_c = lax.broadcasted_iota(jnp.int32, (count + 2, ROWS, planes), 2)
        wide = big[0, pl.ds(first * ROWS, (count + 2) * ROWS), :]
        density_sum = plane_filter(wide.reshape(count + 2, ROWS, planes), lane_c)
        modes = []
        for c in range(3):
            value = big[1 + c, pl.ds((first + 1) * ROWS, (count + 1) * ROWS), :]
            value = value.reshape(count + 1, ROWS, planes)
            modes.append(corner_modes(value, pltpu.roll(value, ROWS - 1, 1), lane_c[:-1], False))
        at = pl.ds(first * ROWS, count * ROWS)
        result = spread_of(
            density_sum, modes, passive[at, :].reshape(shape), inverse[at, :].reshape(shape)
        )
        to = pl.ds((first + 1) * ROWS, count * ROWS)
        spread[to, :] = result.reshape(count * ROWS, planes)

    inner = cols_x - 2
    for first in range(1, 1 + inner, size):
        spread_planes(first, min(size, 1 + inner - first))

    for at in range(8):
        arrive_a(at)

    def join(rows, first, final):
        rows[pl.ds(cols_x, ROWS), :] = jnp.where(
            row == 0, first, jnp.where(row == ROWS - 1, final, 0.0)
        )

    lane_p = lax.broadcasted_iota(jnp.int32, (cols_x + ROWS, planes), 1)

    def packed_row(field, r):
        above = field[pl.ds(last + ROWS + r, 1), :]
        below = field[pl.ds(r, 1), :]
        tail = jnp.where(row == 0, above, jnp.where(row == ROWS - 1, below, 0.0))
        return jnp.concatenate([field[strided(ROWS + r), :], tail], axis=0)

    def packed_nodes(c, r):
        above = big[c, pl.ds(last + ROWS + r, 1), :]
        tail = jnp.where(row == 0, above, 0.0)
        return jnp.concatenate([big[c, strided(ROWS + r), :], tail], axis=0)

    spread_planes(0, 1)
    spread_planes(cols_x - 1, 1)
    join(row_high.at[0], corner_mm[0, 0:1, :], corner_pm[0:1, :])
    join(row_low, corner_mp[ROWS - 1 : ROWS, :], corner_pp[ROWS - 1 : ROWS, :])
    for c in (1, 2, 3):
        join(row_high.at[c], corner_mm[c, 0:1, :], 0.0)
    density = big.at[0]

    def spread_row(r, beyond, next_row, above):
        density_sum = packed_filter(
            beyond, packed_row(density, r), packed_row(density, next_row), lane_p, cols_x
        )
        modes = []
        for c in (1, 2, 3):
            found = corner_modes(packed_nodes(c, r), above(c), lane_p, True)
            modes.append([mode[:cols_x] for mode in found])
        result = spread_of(density_sum, modes, passive[strided(r), :], inverse[strided(r), :])
        spread[strided(ROWS + r), :] = result
        return result

    spread_pack_low[...] = spread_row(0, row_low[...], 1, lambda c: packed_nodes(c, 1))
    spread_pack_high[...] = spread_row(
        ROWS - 1, row_high[0], ROWS - 2, lambda c: row_high[c]
    )
    for at in (3, 2, 1, 0, 7, 4, 5, 6):
        start_b(at)

    def rate_of(sens, held, weight):
        return held * jnp.sqrt(-sens * weight)

    def middle_rows(value, index):
        return jnp.where((index > 0) & (index < ROWS - 1), value, 0.0)

    def plane_group(first, count, place):
        shape = (count, ROWS, planes)
        row_c = lax.broadcasted_iota(jnp.int32, shape, 1)
        lane_c = lax.broadcasted_iota(jnp.int32, (count + 2, ROWS, planes), 2)
        wide = spread[pl.ds(first * ROWS, (count + 2) * ROWS), :].reshape(count + 2, ROWS, planes)
        sens = plane_filter(wide, lane_c)
        at = pl.ds(first * ROWS, count * ROWS)
        held = big[0, pl.ds((first + 1) * ROWS, count * ROWS), :].reshape(shape)
        sens = middle_rows(sens, row_c)
        rate = rate_of(sens, held, inverse_volume[at, :].reshape(shape))
        sens_out[at, :] = sens.reshape(count * ROWS, planes)
        scaled[at, :] = rate.reshape(count * ROWS, planes)
        to = pl.ds(place * ROWS, count * ROWS)
        sum_scaled[to, :] = rate.reshape(count * ROWS, planes)
        for source, target in ((lower, sum_lower), (upper, sum_upper)):
            kept = middle_rows(source[at, :].reshape(shape), row_c)
            target[to, :] = kept.reshape(count * ROWS, planes)

    slots = 2**BISECT
    group = 16
    spacing = 2.0 * BRACKET / slots
    scales = jnp.concatenate(
        [jnp.full((1, ROWS, planes), math.exp(-0.5 * spacing * j), jnp.float32) for j in range(group)]
    )

    def add_volumes(first_tile, end_tile, fresh):
        def volumes(i, carry):
            begin = (-BRACKET) + (spacing * group) * i.astype(jnp.float32)
            factors = scales * jnp.exp(jnp.full((ROWS, planes), -0.5 * begin, jnp.float32))[None]
            at = pl.ds(pl.multiple_of(i * (group * ROWS), group * ROWS), group * ROWS)
            if fresh:
                total = jnp.zeros((group, ROWS, planes), jnp.float32)
            else:
                total = partial[at, :].reshape(group, ROWS, planes)
            for x in range(first_tile, end_tile):
                tile = pl.ds(x * ROWS, ROWS)
                moved = jnp.maximum(sum_scaled[tile, :][None] * factors, sum_lower[tile, :][None])
                total = total + jnp.minimum(moved, sum_upper[tile, :][None])
            partial[at, :] = total.reshape(group * ROWS, planes)
            return carry

        lax.fori_loop(0, slots // group, volumes, 0)

    for first in range(1, 1 + inner, size):
        plane_group(first, min(size, 1 + inner - first), first - 1)
    add_volumes(0, inner, True)

    for at in range(8):
        arrive_b(at)
    plane_group(0, 1, inner)
    plane_group(cols_x - 1, 1, inner + 1)
    join(spread_row_high, s_corner_mm[0:1, :], s_corner_pm[0:1, :])
    join(spread_row_low, s_corner_mp[7:8, :], s_corner_pp[7:8, :])
    def edge_row(r, beyond, next_row, held, place):
        sens = packed_filter(
            beyond, packed_row(spread, r), packed_row(spread, next_row), lane_p, cols_x
        )
        rate = rate_of(sens, held, inverse_volume[strided(r), :])
        sens_out[strided(r), :] = sens
        scaled[strided(r), :] = rate
        to = pl.ds(place * ROWS, cols_x)
        sum_scaled[to, :] = rate
        sum_lower[to, :] = lower[strided(r), :]
        sum_upper[to, :] = upper[strided(r), :]

    edge_row(0, spread_row_low[...], 1, pack_low[0], inner + 2)
    edge_row(ROWS - 1, spread_row_high[...], ROWS - 2, pack_high[...], inner + 2 + cols_x // ROWS)
    add_volumes(inner, inner + 2 + 2 * (cols_x // ROWS), False)
    me = ix * count_y + iy
    halves = slots // planes
    for half in range(halves):
        start = half * planes * ROWS
        lines = partial[pl.ds(start, planes, stride=ROWS), :]
        for s in range(1, ROWS):
            lines = lines + partial[pl.ds(start + s, planes, stride=ROWS), :]
        totals[me, half : half + 1, :] = jnp.sum(lines.T, axis=0, keepdims=True)

    def share(step):
        pltpu.make_async_remote_copy(
            src_ref=totals.at[me],
            dst_ref=totals.at[me],
            send_sem=send_c,
            recv_sem=recv_c,
            device_id=peer(step),
            device_id_type=MESH,
        ).start()

    peers(devices, share)
    for at in range(8):
        sent_a(at)
        sent_b(at)
    others = totals.at[pl.ds(0, devices - 1)]
    pltpu.make_async_copy(others, others, recv_c).wait()
    volume = jnp.sum(totals[...], axis=0)
    label = lax.broadcasted_iota(jnp.int32, volume.shape, 0) * planes + lax.broadcasted_iota(
        jnp.int32, volume.shape, 1
    )
    target = VOLUME_SHARE * total_x * total_y * planes
    over = jnp.where((label > 0) & (volume > target), 1.0, 0.0)
    reached = jnp.sum(jnp.sum(over, axis=0, keepdims=True), axis=1, keepdims=True)
    middle = (-BRACKET) + spacing * (jnp.broadcast_to(reached, (ROWS, planes)) + 0.5)
    factor = jnp.exp(-0.5 * middle)[None]
    for first in range(0, cols_x, size):
        at = pl.ds(first * ROWS, rows_here)
        moved = jnp.maximum(tiles(scaled, first) * factor, tiles(lower, first))
        new_out[at, :] = jnp.minimum(moved, tiles(upper, first)).reshape(rows_here, planes)
    pltpu.make_async_copy(others, others, send_c).wait()


def per_device(count_x, count_y, density, displacement, passive):
    cols_x, cols_y, planes = density.shape
    assert cols_y == ROWS and cols_x % ROWS == 0 and planes == 128
    block = cols_x * ROWS
    slots = 2**BISECT

    def buffer(*shape):
        return pltpu.VMEM(shape, jnp.float32)

    field = buffer(block, planes)
    tile = buffer(ROWS, planes)
    wide = buffer(block + 2 * ROWS, planes)
    rows = buffer(cols_x, planes)
    sums = buffer(block + 2 * cols_x, planes)
    ring = buffer(cols_x + ROWS, planes)
    held = functools.partial(pltpu.with_memory_space_constraint, memory_space=pltpu.HBM)
    anywhere = pl.BlockSpec(memory_space=pl.ANY)
    out = jax.ShapeDtypeStruct((2, block, planes), jnp.float32)
    results = pl.pallas_call(
        functools.partial(kernel, count_x, count_y),
        out_shape=out,
        in_specs=[anywhere] * 3,
        out_specs=pl.BlockSpec(memory_space=pltpu.VMEM),
        scratch_shapes=[
            buffer(4, block + 2 * ROWS, planes),
            pltpu.VMEM((block, planes), jnp.int32),
            buffer(4, cols_x, planes),
            rows,
            buffer(4, cols_x + ROWS, planes),
            ring,
            wide,
            rows,
            rows,
            ring,
            ring,
            tile,
            tile,
            tile,
            buffer(4, ROWS, planes),
            tile,
            tile,
            tile,
            tile,
            field,
            field,
            field,
            field,
            field,
            sums,
            sums,
            sums,
            buffer(slots * ROWS, planes),
            buffer(count_x * count_y, slots // planes, planes),
            pltpu.SemaphoreType.DMA((3,)),
            pltpu.SemaphoreType.DMA((8,)),
            pltpu.SemaphoreType.DMA((8,)),
            pltpu.SemaphoreType.DMA((8,)),
            pltpu.SemaphoreType.DMA((8,)),
            pltpu.SemaphoreType.DMA,
            pltpu.SemaphoreType.DMA,
        ],
        compiler_params=pltpu.CompilerParams(
            collective_id=0, has_side_effects=True, vmem_limit_bytes=16 * 1024 * 1024
        ),
    )(
        held(density.reshape(block, planes)),
        held(displacement.reshape(3, block, planes)),
        held(passive.reshape(block, planes)),
    )
    return (results[0].reshape(density.shape), results[1].reshape(density.shape))


def solution(mesh):
    return jax.shard_map(
        functools.partial(per_device, mesh.shape["gx"], mesh.shape["gy"]),
        mesh=mesh,
        in_specs=(P("gx", "gy", None), P(None, "gx", "gy", None), P("gx", "gy", None)),
        out_specs=(P("gx", "gy", None), P("gx", "gy", None)),
        check_vma=False,
    )
```

```python
import functools
import math

import jax
import jax.numpy as jnp
from jax import lax
from jax.experimental import pallas as pl
from jax.experimental.pallas import tpu as pltpu
from jax.sharding import PartitionSpec as P

BISECT = 8
BRACKET = 8.0
MOVE_LIMIT = 0.2
VOLUME_SHARE = 0.35
DERIVATIVE = 3.0 * (1.0 - 1e-09)
EDGE_WEIGHT = 1.5 - math.sqrt(2.0)
POISSON = 0.3
LAME_FIRST = POISSON / ((1.0 + POISSON) * (1.0 - 2.0 * POISSON))
SHEAR = 0.5 / (1.0 + POISSON)
ROWS = 8
MESH = pl.DeviceIdType.MESH
WAYS = [(1, 0), (-1, 0), (0, 1), (0, -1), (1, 1), (-1, 1), (1, -1), (-1, -1)]


def z_neighbours(value, lane):
    planes = value.shape[-1]
    axis = value.ndim - 1
    above = jnp.where(lane == planes - 1, 0.0, pltpu.roll(value, planes - 1, axis))
    below = jnp.where(lane == 0, 0.0, pltpu.roll(value, 1, axis))
    return above + below


def parts_of_filter(value, lane):
    beside = z_neighbours(value, lane)
    return (
        1.5 * value + 0.5 * beside,
        0.5 * value + EDGE_WEIGHT * beside,
        EDGE_WEIGHT * value,
    )


def filter_rows(packed, lane, cols_x):
    _, near, far = parts_of_filter(packed, lane)
    count = packed.shape[0]
    return (near + pltpu.roll(far, 1, 0) + pltpu.roll(far, count - 1, 0))[:cols_x]


def packed_filter(beyond, here, beyond_next, lane, cols_x):
    own, near, _ = parts_of_filter(here, lane)
    count = here.shape[0]
    result = (own + pltpu.roll(near, 1, 0) + pltpu.roll(near, count - 1, 0))[:cols_x]
    result = result + filter_rows(beyond, lane, cols_x)
    return result + filter_rows(beyond_next, lane, cols_x)


def plane_filter(wide, lane):
    own, near, far = parts_of_filter(wide, lane)
    side = near[1:-1] + far[:-2] + far[2:]
    result = own[1:-1] + near[:-2] + near[2:]
    return result + (pltpu.roll(side, ROWS - 1, 1) + pltpu.roll(side, 1, 1))


def corner_modes(value, above, lane, packed):
    planes = value.shape[-1]
    total, step = value + above, above - value

    def next_z(field):
        moved = pltpu.roll(field, planes - 1, field.ndim - 1)
        return jnp.where(lane == planes - 1, 0.0, moved)

    def ends(field):
        if packed:
            return field, pltpu.roll(field, field.shape[0] - 1, 0)
        return field[:-1], field[1:]

    total_next, step_next = next_z(total), next_z(step)
    both, both_next = ends(total + total_next)
    along_z, along_z_next = ends(total_next - total)
    along_y, along_y_next = ends(step + step_next)
    along_yz, along_yz_next = ends(step_next - step)
    return (
        both_next - both,
        along_y_next + along_y,
        along_z_next + along_z,
        along_y_next - along_y,
        along_z_next - along_z,
        along_yz_next + along_yz,
        along_yz_next - along_yz,
    )


def element_energy(modes):
    (ax, ay, az, axy, axz, ayz, axyz), (bx, by, bz, bxy, bxz, byz, bxyz), (
        cx,
        cy,
        cz,
        cxy,
        cxz,
        cyz,
        cxyz,
    ) = modes

    def sq(value):
        return value * value

    first = (
        (LAME_FIRST / 16.0) * sq(ax + by + cz)
        + (2.0 * SHEAR / 16.0) * (sq(ax) + sq(by) + sq(cz))
        + (SHEAR / 16.0) * (sq(ay + bx) + sq(az + cx) + sq(bz + cy))
    )
    second = (
        (LAME_FIRST / 48.0) * (sq(axy + cyz) + sq(bxy + cxz) + sq(axz + byz))
        + (3.0 * SHEAR / 48.0) * (sq(axy) + sq(axz) + sq(bxy) + sq(byz) + sq(cxz) + sq(cyz))
        + (SHEAR / 48.0) * (sq(ayz + bxz) + sq(ayz + cxy) + sq(bxz + cxy))
    )
    third = ((LAME_FIRST + 4.0 * SHEAR) / 144.0) * (sq(axyz) + sq(bxyz) + sq(cxyz))
    return first + second + third


def peers(count_x, count_y, own_column_first, body):
    count = count_x * count_y
    if count > 64:
        pair = lambda step: (step // count_y, step % count_y)
        lax.fori_loop(1, count, lambda step, carry: (body(*pair(step)), carry)[1], 0)
        return

    def nearness(step, size):
        return (min(step, size - step), step)

    columns = sorted(range(1, count_x), key=lambda step: nearness(step, count_x))
    columns = [0] + columns if own_column_first else columns + [0]
    rows = sorted(range(count_y), key=lambda step: nearness(step, count_y))
    for step_x in columns:
        for step_y in rows:
            if (step_x, step_y) != (0, 0):
                body(step_x, step_y)


def kernel(
    count_x,
    count_y,
    dens_hbm,
    disp_hbm,
    pas_hbm,
    results,
    big,
    passive,
    pack_low,
    pack_high,
    row_high,
    row_low,
    spread,
    spread_pack_low,
    spread_pack_high,
    spread_row_high,
    spread_row_low,
    corner_pp,
    corner_mp,
    corner_pm,
    corner_mm,
    s_corner_pp,
    s_corner_mp,
    s_corner_pm,
    s_corner_mm,
    inverse,
    inverse_volume,
    scaled,
    lower,
    upper,
    sum_scaled,
    sum_lower,
    sum_upper,
    partial,
    totals,
    local_sems,
    send_a,
    recv_a,
    send_b,
    recv_b,
    send_c,
    recv_c,
):
    new_out, sens_out = results.at[0], results.at[1]
    planes = dens_hbm.shape[-1]
    cols_x = dens_hbm.shape[0] // ROWS
    block = cols_x * ROWS
    last = cols_x * ROWS
    ix, iy = lax.axis_index("gx"), lax.axis_index("gy")
    total_x, total_y = cols_x * count_x, ROWS * count_y

    def inside(x, y):
        return (x >= 0) & (x < count_x) & (y >= 0) & (y < count_y)

    loads = [
        pltpu.make_async_copy(dens_hbm, big.at[0, pl.ds(ROWS, block)], local_sems.at[0]),
        pltpu.make_async_copy(disp_hbm, big.at[pl.ds(1, 3), pl.ds(ROWS, block)], local_sems.at[1]),
        pltpu.make_async_copy(pas_hbm, passive, local_sems.at[2]),
    ]
    for load in loads:
        load.start()

    devices = count_x * count_y

    def peer(step_x, step_y):
        return (lax.rem(ix + step_x, count_x), lax.rem(iy + step_y, count_y))

    barrier = pltpu.get_barrier_semaphore()
    def greet(step_x, step_y):
        pl.semaphore_signal(
            barrier, inc=1, device_id=peer(step_x, step_y), device_id_type=MESH
        )

    peers(count_x, count_y, True, greet)

    def fill(way, refs):
        @pl.when(jnp.logical_not(inside(ix - way[0], iy - way[1])))
        def _():
            for ref in refs:
                ref[...] = jnp.zeros(ref.shape, ref.dtype)

    def exchange(pairs, send, recv):
        def copy(at):
            source, target = pairs[at]
            dx, dy = WAYS[at]
            return pltpu.make_async_remote_copy(
                src_ref=source,
                dst_ref=target,
                send_sem=send.at[at],
                recv_sem=recv.at[at],
                device_id=(ix + dx, iy + dy),
                device_id_type=MESH,
            )

        def start(at):
            dx, dy = WAYS[at]

            @pl.when(inside(ix + dx, iy + dy))
            def _():
                copy(at).start()

        def arrive(at):
            dx, dy = WAYS[at]

            @pl.when(inside(ix - dx, iy - dy))
            def _():
                copy(at).wait_recv()

        def sent(at):
            dx, dy = WAYS[at]

            @pl.when(inside(ix + dx, iy + dy))
            def _():
                copy(at).wait_send()

        return start, arrive, sent

    first_tile, last_tile = pl.ds(ROWS, ROWS), pl.ds(last, ROWS)
    low_tile, high_tile = pl.ds(0, ROWS), pl.ds(last + ROWS, ROWS)
    start_a, arrive_a, sent_a = exchange(
        [
            (big.at[0, last_tile], big.at[0, low_tile]),
            (big.at[:, first_tile], big.at[:, high_tile]),
            (pack_high, row_low.at[pl.ds(0, cols_x)]),
            (pack_low, row_high.at[:, pl.ds(0, cols_x)]),
            (big.at[0, last_tile], corner_pp),
            (big.at[0, first_tile], corner_mp),
            (big.at[0, last_tile], corner_pm),
            (big.at[:, first_tile], corner_mm),
        ],
        send_a,
        recv_a,
    )
    start_b, arrive_b, sent_b = exchange(
        [
            (spread.at[last_tile], spread.at[low_tile]),
            (spread.at[first_tile], spread.at[high_tile]),
            (spread_pack_high, spread_row_low.at[pl.ds(0, cols_x)]),
            (spread_pack_low, spread_row_high.at[pl.ds(0, cols_x)]),
            (spread.at[last_tile], s_corner_pp),
            (spread.at[first_tile], s_corner_mp),
            (spread.at[last_tile], s_corner_pm),
            (spread.at[first_tile], s_corner_mm),
        ],
        send_b,
        recv_b,
    )
    lane = lax.broadcasted_iota(jnp.int32, (ROWS, planes), 1)
    row = lax.broadcasted_iota(jnp.int32, (ROWS, planes), 0)

    def counted(at, total):
        one, none = jnp.float32(1.0), jnp.float32(0.0)
        return jnp.where(at > 0, one, none) + jnp.where(at < total - 1, one, none)

    count_z = counted(lane, planes)
    known = {}

    def representative(x):
        return x if x in (-1, 0, cols_x - 1, cols_x) else 1

    def inverse_sums(x, offset):
        x = representative(x)
        if (x, offset) not in known:
            y = iy * ROWS + row + offset
            beside_y = counted(y, total_y)
            global_x = ix * cols_x + x
            beside_x = counted(global_x, total_x)
            sums = (
                1.5
                + 0.5 * (beside_x + beside_y + count_z)
                + EDGE_WEIGHT * (beside_x * beside_y + beside_x * count_z + beside_y * count_z)
            )
            result = 1.0 / sums
            result = jnp.where((y >= 0) & (y < total_y), result, 0.0)
            if x in (-1, cols_x):
                held = (global_x >= 0) & (global_x < total_x)
                result = result * jnp.where(held, jnp.float32(1.0), jnp.float32(0.0))
            known[x, offset] = (result, parts_of_filter(result, lane))
        return known[x, offset]

    weights = {}
    for x in range(cols_x):
        tile = pl.ds(x * ROWS, ROWS)
        inverse[tile, :] = inverse_sums(x, 0)[0]
        key = tuple(representative(x + d) for d in (-1, 0, 1))
        if key not in weights:
            volume = inverse_sums(x, 0)[1][0]
            volume = volume + inverse_sums(x - 1, 0)[1][1] + inverse_sums(x + 1, 0)[1][1]
            for offset in (-1, 1):
                volume = volume + inverse_sums(x, offset)[1][1]
                volume = volume + inverse_sums(x - 1, offset)[1][2]
                volume = volume + inverse_sums(x + 1, offset)[1][2]
            weights[key] = 1.0 / volume
        inverse_volume[tile, :] = weights[key]

    def strided(start):
        return pl.ds(start, cols_x, stride=ROWS)

    loads[0].wait()
    pack_high[...] = big[0, strided(ROWS + ROWS - 1), :]
    pack_low[0] = big[0, strided(ROWS), :]
    loads[1].wait()
    for c in (1, 2, 3):
        pack_low[c] = big[c, strided(ROWS), :]
    pl.semaphore_wait(barrier, devices - 1)
    for at in (3, 1, 2, 7, 0, 4, 5, 6):
        start_a(at)
    fill(WAYS[0], [big.at[0, low_tile], spread.at[low_tile]])
    fill(WAYS[1], [big.at[:, high_tile], spread.at[high_tile]])
    fill(WAYS[2], [row_low.at[pl.ds(0, cols_x)], spread_row_low.at[pl.ds(0, cols_x)]])
    fill(WAYS[3], [row_high.at[:, pl.ds(0, cols_x)], spread_row_high.at[pl.ds(0, cols_x)]])
    fill(WAYS[4], [corner_pp, s_corner_pp])
    fill(WAYS[5], [corner_mp, s_corner_mp])
    fill(WAYS[6], [corner_pm, s_corner_pm])
    fill(WAYS[7], [corner_mm, s_corner_mm])

    size = 4 if cols_x % 4 == 0 else 1
    rows_here = size * ROWS
    def tiles(ref, first):
        return ref[pl.ds(first * ROWS, rows_here), :].reshape(size, ROWS, planes)

    loads[2].wait()
    for first in range(0, cols_x, size):
        at = pl.ds(first * ROWS, rows_here)
        kind = tiles(passive, first)
        held = big[0, pl.ds((first + 1) * ROWS, rows_here), :].reshape(size, ROWS, planes)
        fixed = jnp.where(kind == 1, 1.0, 0.0)
        low = jnp.where(kind == 0, jnp.maximum(held - MOVE_LIMIT, 0.0), fixed)
        high = jnp.where(kind == 0, jnp.minimum(held + MOVE_LIMIT, 1.0), fixed)
        lower[at, :] = low.reshape(rows_here, planes)
        upper[at, :] = high.reshape(rows_here, planes)

    def spread_of(density_sum, modes, kind, inv):
        physical = density_sum * inv
        physical = jnp.where(kind == 1, 1.0, jnp.where(kind == 2, 0.0, physical))
        raw = (-DERIVATIVE) * physical * physical * element_energy(modes)
        return raw * inv

    def spread_planes(first, count):
        shape = (count, ROWS, planes)
        lane_c = lax.broadcasted_iota(jnp.int32, (count + 2, ROWS, planes), 2)
        wide = big[0, pl.ds(first * ROWS, (count + 2) * ROWS), :]
        density_sum = plane_filter(wide.reshape(count + 2, ROWS, planes), lane_c)
        modes = []
        for c in range(3):
            value = big[1 + c, pl.ds((first + 1) * ROWS, (count + 1) * ROWS), :]
            value = value.reshape(count + 1, ROWS, planes)
            modes.append(corner_modes(value, pltpu.roll(value, ROWS - 1, 1), lane_c[:-1], False))
        at = pl.ds(first * ROWS, count * ROWS)
        result = spread_of(
            density_sum, modes, passive[at, :].reshape(shape), inverse[at, :].reshape(shape)
        )
        to = pl.ds((first + 1) * ROWS, count * ROWS)
        spread[to, :] = result.reshape(count * ROWS, planes)

    inner = cols_x - 2
    for first in range(1, 1 + inner, size):
        spread_planes(first, min(size, 1 + inner - first))

    for at in range(8):
        arrive_a(at)

    def join(rows, first, final):
        rows[pl.ds(cols_x, ROWS), :] = jnp.where(
            row == 0, first, jnp.where(row == ROWS - 1, final, 0.0)
        )

    lane_p = lax.broadcasted_iota(jnp.int32, (cols_x + ROWS, planes), 1)

    def packed_row(field, r):
        above = field[pl.ds(last + ROWS + r, 1), :]
        below = field[pl.ds(r, 1), :]
        tail = jnp.where(row == 0, above, jnp.where(row == ROWS - 1, below, 0.0))
        return jnp.concatenate([field[strided(ROWS + r), :], tail], axis=0)

    def packed_nodes(c, r):
        above = big[c, pl.ds(last + ROWS + r, 1), :]
        tail = jnp.where(row == 0, above, 0.0)
        return jnp.concatenate([big[c, strided(ROWS + r), :], tail], axis=0)

    spread_planes(0, 1)
    spread_planes(cols_x - 1, 1)
    join(row_high.at[0], corner_mm[0, 0:1, :], corner_pm[0:1, :])
    join(row_low, corner_mp[ROWS - 1 : ROWS, :], corner_pp[ROWS - 1 : ROWS, :])
    for c in (1, 2, 3):
        join(row_high.at[c], corner_mm[c, 0:1, :], 0.0)
    density = big.at[0]

    def spread_row(r, beyond, next_row, above):
        density_sum = packed_filter(
            beyond, packed_row(density, r), packed_row(density, next_row), lane_p, cols_x
        )
        modes = []
        for c in (1, 2, 3):
            found = corner_modes(packed_nodes(c, r), above(c), lane_p, True)
            modes.append([mode[:cols_x] for mode in found])
        result = spread_of(density_sum, modes, passive[strided(r), :], inverse[strided(r), :])
        spread[strided(ROWS + r), :] = result
        return result

    spread_pack_low[...] = spread_row(0, row_low[...], 1, lambda c: packed_nodes(c, 1))
    start_b(3)
    spread_pack_high[...] = spread_row(
        ROWS - 1, row_high[0], ROWS - 2, lambda c: row_high[c]
    )
    for at in (2, 1, 0, 7, 4, 5, 6):
        start_b(at)

    def rate_of(sens, held, weight):
        return held * jnp.sqrt(-sens * weight)

    def middle_rows(value, index):
        return jnp.where((index > 0) & (index < ROWS - 1), value, 0.0)

    def plane_group(first, count, place):
        shape = (count, ROWS, planes)
        row_c = lax.broadcasted_iota(jnp.int32, shape, 1)
        lane_c = lax.broadcasted_iota(jnp.int32, (count + 2, ROWS, planes), 2)
        wide = spread[pl.ds(first * ROWS, (count + 2) * ROWS), :].reshape(count + 2, ROWS, planes)
        sens = plane_filter(wide, lane_c)
        at = pl.ds(first * ROWS, count * ROWS)
        held = big[0, pl.ds((first + 1) * ROWS, count * ROWS), :].reshape(shape)
        sens = middle_rows(sens, row_c)
        rate = rate_of(sens, held, inverse_volume[at, :].reshape(shape))
        sens_out[at, :] = sens.reshape(count * ROWS, planes)
        scaled[at, :] = rate.reshape(count * ROWS, planes)
        to = pl.ds(place * ROWS, count * ROWS)
        sum_scaled[to, :] = rate.reshape(count * ROWS, planes)
        for source, target in ((lower, sum_lower), (upper, sum_upper)):
            kept = middle_rows(source[at, :].reshape(shape), row_c)
            target[to, :] = kept.reshape(count * ROWS, planes)

    slots = 2**BISECT
    group = 16
    spacing = 2.0 * BRACKET / slots
    scales = jnp.concatenate(
        [jnp.full((1, ROWS, planes), math.exp(-0.5 * spacing * j), jnp.float32) for j in range(group)]
    )

    def add_volumes(first_tile, end_tile, fresh):
        def volumes(i, carry):
            begin = (-BRACKET) + (spacing * group) * i.astype(jnp.float32)
            factors = scales * jnp.exp(jnp.full((ROWS, planes), -0.5 * begin, jnp.float32))[None]
            at = pl.ds(pl.multiple_of(i * (group * ROWS), group * ROWS), group * ROWS)
            if fresh:
                total = jnp.zeros((group, ROWS, planes), jnp.float32)
            else:
                total = partial[at, :].reshape(group, ROWS, planes)
            for x in range(first_tile, end_tile):
                tile = pl.ds(x * ROWS, ROWS)
                moved = jnp.maximum(sum_scaled[tile, :][None] * factors, sum_lower[tile, :][None])
                total = total + jnp.minimum(moved, sum_upper[tile, :][None])
            partial[at, :] = total.reshape(group * ROWS, planes)
            return carry

        lax.fori_loop(0, slots // group, volumes, 0)

    for first in range(1, 1 + inner, size):
        plane_group(first, min(size, 1 + inner - first), first - 1)
    add_volumes(0, inner, True)

    for at in range(8):
        arrive_b(at)
    plane_group(0, 1, inner)
    plane_group(cols_x - 1, 1, inner + 1)
    join(spread_row_high, s_corner_mm[0:1, :], s_corner_pm[0:1, :])
    join(spread_row_low, s_corner_mp[7:8, :], s_corner_pp[7:8, :])
    def edge_row(r, beyond, next_row, held, place):
        sens = packed_filter(
            beyond, packed_row(spread, r), packed_row(spread, next_row), lane_p, cols_x
        )
        rate = rate_of(sens, held, inverse_volume[strided(r), :])
        sens_out[strided(r), :] = sens
        scaled[strided(r), :] = rate
        to = pl.ds(place * ROWS, cols_x)
        sum_scaled[to, :] = rate
        sum_lower[to, :] = lower[strided(r), :]
        sum_upper[to, :] = upper[strided(r), :]

    edge_row(0, spread_row_low[...], 1, pack_low[0], inner + 2)
    edge_row(ROWS - 1, spread_row_high[...], ROWS - 2, pack_high[...], inner + 2 + cols_x // ROWS)
    add_volumes(inner, inner + 2 + 2 * (cols_x // ROWS), False)
    me = ix * count_y + iy
    halves = slots // planes
    for half in range(halves):
        start = half * planes * ROWS
        lines = partial[pl.ds(start, planes, stride=ROWS), :]
        for s in range(1, ROWS):
            lines = lines + partial[pl.ds(start + s, planes, stride=ROWS), :]
        totals[me, half : half + 1, :] = jnp.sum(lines.T, axis=0, keepdims=True)

    def share(step_x, step_y):
        pltpu.make_async_remote_copy(
            src_ref=totals.at[me],
            dst_ref=totals.at[me],
            send_sem=send_c,
            recv_sem=recv_c,
            device_id=peer(step_x, step_y),
            device_id_type=MESH,
        ).start()

    peers(count_x, count_y, False, share)
    for at in range(8):
        sent_a(at)
        sent_b(at)
    others = totals.at[pl.ds(0, devices - 1)]
    pltpu.make_async_copy(others, others, recv_c).wait()
    volume = jnp.sum(totals[...], axis=0)
    label = lax.broadcasted_iota(jnp.int32, volume.shape, 0) * planes + lax.broadcasted_iota(
        jnp.int32, volume.shape, 1
    )
    target = VOLUME_SHARE * total_x * total_y * planes
    over = jnp.where((label > 0) & (volume > target), 1.0, 0.0)
    reached = jnp.sum(jnp.sum(over, axis=0, keepdims=True), axis=1, keepdims=True)
    middle = (-BRACKET) + spacing * (jnp.broadcast_to(reached, (ROWS, planes)) + 0.5)
    factor = jnp.exp(-0.5 * middle)[None]
    for first in range(0, cols_x, size):
        at = pl.ds(first * ROWS, rows_here)
        moved = jnp.maximum(tiles(scaled, first) * factor, tiles(lower, first))
        new_out[at, :] = jnp.minimum(moved, tiles(upper, first)).reshape(rows_here, planes)
    pltpu.make_async_copy(others, others, send_c).wait()


def per_device(count_x, count_y, density, displacement, passive):
    cols_x, cols_y, planes = density.shape
    assert cols_y == ROWS and cols_x % ROWS == 0 and planes == 128
    block = cols_x * ROWS
    slots = 2**BISECT

    def buffer(*shape):
        return pltpu.VMEM(shape, jnp.float32)

    field = buffer(block, planes)
    tile = buffer(ROWS, planes)
    wide = buffer(block + 2 * ROWS, planes)
    rows = buffer(cols_x, planes)
    sums = buffer(block + 2 * cols_x, planes)
    ring = buffer(cols_x + ROWS, planes)
    held = functools.partial(pltpu.with_memory_space_constraint, memory_space=pltpu.HBM)
    anywhere = pl.BlockSpec(memory_space=pl.ANY)
    out = jax.ShapeDtypeStruct((2, block, planes), jnp.float32)
    results = pl.pallas_call(
        functools.partial(kernel, count_x, count_y),
        out_shape=out,
        in_specs=[anywhere] * 3,
        out_specs=pl.BlockSpec(memory_space=pltpu.VMEM),
        scratch_shapes=[
            buffer(4, block + 2 * ROWS, planes),
            pltpu.VMEM((block, planes), jnp.int32),
            buffer(4, cols_x, planes),
            rows,
            buffer(4, cols_x + ROWS, planes),
            ring,
            wide,
            rows,
            rows,
            ring,
            ring,
            tile,
            tile,
            tile,
            buffer(4, ROWS, planes),
            tile,
            tile,
            tile,
            tile,
            field,
            field,
            field,
            field,
            field,
            sums,
            sums,
            sums,
            buffer(slots * ROWS, planes),
            buffer(count_x * count_y, slots // planes, planes),
            pltpu.SemaphoreType.DMA((3,)),
            pltpu.SemaphoreType.DMA((8,)),
            pltpu.SemaphoreType.DMA((8,)),
            pltpu.SemaphoreType.DMA((8,)),
            pltpu.SemaphoreType.DMA((8,)),
            pltpu.SemaphoreType.DMA,
            pltpu.SemaphoreType.DMA,
        ],
        compiler_params=pltpu.CompilerParams(
            collective_id=0, has_side_effects=True, vmem_limit_bytes=16 * 1024 * 1024
        ),
    )(
        held(density.reshape(block, planes)),
        held(displacement.reshape(3, block, planes)),
        held(passive.reshape(block, planes)),
    )
    return (results[0].reshape(density.shape), results[1].reshape(density.shape))


def solution(mesh):
    return jax.shard_map(
        functools.partial(per_device, mesh.shape["gx"], mesh.shape["gy"]),
        mesh=mesh,
        in_specs=(P("gx", "gy", None), P(None, "gx", "gy", None), P("gx", "gy", None)),
        out_specs=(P("gx", "gy", None), P("gx", "gy", None)),
        check_vma=False,
    )
```
